256 devices in a mesh: seq: 32 (over y, x, core), mp: 8 (over z).
Axes of the slice: x: 4, y: 4, z: 8, core: 2. Of those that a mesh axis runs over, the one named last changes fastest.
Arguments:
- queries: bfloat16 [8192, 5120], P('seq', 'mp'), may hold values from -512 to 512
- keys: bfloat16 [8192, 5120], P('seq', 'mp'), may hold values from -4 to 4
- values: bfloat16 [8192, 5120], P('seq', 'mp'), may hold values from -64 to 64
- decay: float32 [8192, 5120], P('seq', 'mp'), may hold values from 0 to 2.5, as said below
- gain: float32 [5120], P('mp'), may hold values from 0.5 to 1.5
- theta: float32 [16, 5120], P(None, 'mp'), may hold values from -3.140625 to 3.140625
- mode_coeffs: float32 [4, 16, 5120], P(None, None, 'mp'), may hold values from -3 to 3
Outputs:
- attn: bfloat16 [8192, 5120], P('seq', 'mp')
- rec: float32 [8192, 5120], P('seq', 'mp')
The draws below stay inside these ranges and needn't reach their ends.
Inputs may be any that keep to these rules, and one draw needn't show every extreme that they name: `decay`: every entry is positive.
All inputs are finite; a program needn't handle non-finite values.
Results may differ from the reference program's by a relative error of at most 0.0032.
Values may be sent and summed in bfloat16 or wider, within the bound.
No kernel may reach another device: no remote copies, remote signals or barrier semaphores. Data moves between devices by JAX's collectives and lax.ppermute only.
A program may use at most 64 MiB of HBM per device.

```python
import math
import jax
import jax.numpy as jnp
from jax import lax

H = 40
HD = 128
EMBED_DIMENSION = 5120
MODES = 16
WINDOW = 1024
TOK_DEV = 256
SEQUENCE_SPAN = 8192


def query_key_pair(key):
    base = jax.random.fold_in(key, 7301)
    key_q, key_k = jax.random.split(base)
    queries = jnp.clip(1.5 * jax.random.normal(key_q, (SEQUENCE_SPAN, EMBED_DIMENSION), jnp.float32), -6.0, 6.0)
    keys = jnp.clip(jax.random.normal(key_k, (SEQUENCE_SPAN, EMBED_DIMENSION), jnp.float32), -4.0, 4.0)
    return (queries, keys)


def draw_queries(key, part):
    return query_key_pair(key)[0].astype(jnp.bfloat16)


def draw_keys(key, part):
    return query_key_pair(key)[1].astype(jnp.bfloat16)


def draw_values(key, part):
    key_a, key_b, key_c, key_d = jax.random.split(jax.random.fold_in(key, 4409), 4)
    columns = jnp.arange(EMBED_DIMENSION, dtype=jnp.float32)[None, :]
    col_scale = 10.0 ** (0.4 * columns / EMBED_DIMENSION + 0.6 * jax.random.uniform(key_a, (1, EMBED_DIMENSION), jnp.float32) - 0.5)
    row_scale = 10.0 ** (jax.random.uniform(key_b, (SEQUENCE_SPAN, 1), jnp.float32) - 0.5)
    offset = jax.random.uniform(key_c, (1, EMBED_DIMENSION), jnp.float32, -1.0, 1.0)
    noise = jnp.clip(jax.random.normal(key_d, (SEQUENCE_SPAN, EMBED_DIMENSION), jnp.float32), -4.0, 4.0)
    return (col_scale * row_scale * (offset + noise)).astype(jnp.bfloat16)


def draw_decay(key, part):
    entire_attender_matrix = jax.random.split(jax.random.fold_in(key, 9127), 7)
    fast_share = 0.5
    is_fast = jax.random.uniform(entire_attender_matrix[0], (1, EMBED_DIMENSION), jnp.float32) < fast_share
    fast_rate = 1.0 / jax.random.uniform(entire_attender_matrix[1], (1, EMBED_DIMENSION), jnp.float32, 30.0, 50.0)
    slow_total = jax.random.uniform(entire_attender_matrix[2], (1, EMBED_DIMENSION), jnp.float32, 0.05, 0.6)
    base_rate = jnp.where(is_fast, fast_rate, slow_total / SEQUENCE_SPAN)
    segment_count = SEQUENCE_SPAN // TOK_DEV
    segment_factor = jnp.exp(jax.random.uniform(entire_attender_matrix[3], (segment_count,), jnp.float32, math.log(0.5), math.log(2.0)))
    sequence_ordinals = jnp.arange(SEQUENCE_SPAN, dtype=jnp.int32)
    per_token = segment_factor[sequence_ordinals // TOK_DEV][:, None]
    roughness = jax.random.uniform(entire_attender_matrix[4], (SEQUENCE_SPAN, EMBED_DIMENSION), jnp.float32, 0.3, 1.7)
    contiguous_start = jax.random.randint(entire_attender_matrix[5], (3,), 0, SEQUENCE_SPAN)
    contiguous_span = jax.random.uniform(entire_attender_matrix[6], (3, EMBED_DIMENSION), jnp.float32, 0.22, 0.69)
    layer_answer = base_rate * per_token * roughness
    for gather_slot in range(3):
        equality_indicator = (sequence_ordinals == contiguous_start[gather_slot]).astype(jnp.float32)[:, None]
        layer_answer = layer_answer + equality_indicator * contiguous_span[gather_slot][None, :]
    return layer_answer


def level_of(own_key, extent, cuts, smallest, top_value):
    def one(axis_at, blocks):
        heights = jax.random.uniform(jax.random.fold_in(jax.random.fold_in(own_key, 6), axis_at), (blocks,), jnp.float32, smallest / len(cuts), top_value / len(cuts))
        return jnp.repeat(jnp.exp(heights), extent[axis_at] // blocks).reshape((-1,) + (1,) * (len(extent) - axis_at - 1))

    factor_of = one(*cuts[0])
    for cut in cuts[1:]:
        factor_of = factor_of * one(*cut)
    return factor_of


def normal_values(own_key, shape, width, bound, cuts=(), kind=jnp.bfloat16):
    values = width * jax.random.normal(own_key, shape, jnp.float32)
    if cuts:
        values = values * level_of(own_key, shape, cuts, -0.22, 0.18)
    return jnp.clip(values, -bound, bound).astype(kind)


def setup_inputs(seed: int = 0) -> dict:
    streams_of = jax.random.split(jax.random.key(seed), 8)
    return {
        "queries": draw_queries(jax.random.fold_in(streams_of[7], 71), 0),
        "keys": draw_keys(jax.random.fold_in(streams_of[7], 71), 0),
        "values": draw_values(jax.random.fold_in(streams_of[7], 71), 0),
        "decay": draw_decay(jax.random.fold_in(streams_of[7], 71), 0),
        "gain": jnp.clip(1.0 + 0.1 * jax.random.normal(streams_of[4], (EMBED_DIMENSION,), jnp.float32), 0.5, 1.5),
        "theta": jnp.clip(jax.random.uniform(streams_of[5], (MODES, EMBED_DIMENSION), jnp.float32, -3.140625, 3.140625), -3.140625, 3.140625),
        "mode_coeffs": normal_values(streams_of[6], (4, MODES, EMBED_DIMENSION), 0.5, 3.0, ((2, 8),), jnp.float32),
    }


def attention_ref(queries, keys, values):
    q_block = min(512, SEQUENCE_SPAN)
    pad_rows = jnp.zeros((WINDOW, EMBED_DIMENSION), keys.dtype)
    padded_keys = jnp.concatenate([pad_rows, keys], 0)
    padded_values = jnp.concatenate([pad_rows, values], 0)

    def one_block(block_index):
        start = block_index * q_block
        q_part = lax.dynamic_slice_in_dim(queries, start, q_block, 0).reshape(q_block, H, HD)
        k_part = lax.dynamic_slice_in_dim(padded_keys, start, q_block + WINDOW, 0).reshape(q_block + WINDOW, H, HD)
        v_part = lax.dynamic_slice_in_dim(padded_values, start, q_block + WINDOW, 0).reshape(q_block + WINDOW, H, HD)
        scores = jnp.einsum('qhd,khd->hqk', q_part.astype(jnp.float32), k_part.astype(jnp.float32)) / math.sqrt(HD)
        q_pos = start + jnp.arange(q_block, dtype=jnp.int32)
        k_pos = start - WINDOW + jnp.arange(q_block + WINDOW, dtype=jnp.int32)
        allowed = (k_pos[None, :] <= q_pos[:, None]) & (k_pos[None, :] > q_pos[:, None] - WINDOW) & (k_pos[None, :] >= 0)
        scores = jnp.where(allowed[None], scores, -jnp.inf)
        row_max = lax.optimization_barrier(jnp.max(scores, axis=2, keepdims=True))
        weights = jnp.exp(scores - row_max)
        denominator = lax.optimization_barrier(jnp.sum(weights, axis=2))
        weights_b = weights.astype(jnp.bfloat16)
        mixed = jnp.einsum('hqk,khd->qhd', weights_b.astype(jnp.float32), v_part.astype(jnp.float32))
        mixed = mixed / jnp.transpose(denominator)[:, :, None]
        return mixed.reshape(q_block, EMBED_DIMENSION).astype(jnp.bfloat16)
    blocks_out = lax.map(one_block, jnp.arange(SEQUENCE_SPAN // q_block, dtype=jnp.int32))
    return blocks_out.reshape(SEQUENCE_SPAN, EMBED_DIMENSION)

def reference(queries, keys, values, decay, gain, theta, mode_coeffs):
    attn = attention_ref(queries, keys, values)
    attn_f = attn.astype(jnp.float32)
    meansq = lax.optimization_barrier(jnp.mean(attn_f * attn_f, axis=1))
    inflow = attn_f * lax.rsqrt(meansq + 1e-06)[:, None] * gain[None, :]
    inflow = inflow * jnp.sqrt(-jnp.expm1(-2.0 * decay))
    cos_t = jnp.cos(theta)
    sin_t = jnp.sin(theta)
    b_re, b_im, c_re, c_im = (mode_coeffs[0], mode_coeffs[1], mode_coeffs[2], mode_coeffs[3])

    def advance(state, inputs):
        h_re, h_im = state
        rate_row, flow_row = inputs
        fade = jnp.exp(-rate_row)[None, :]
        rot_re = cos_t * h_re - sin_t * h_im
        rot_im = sin_t * h_re + cos_t * h_im
        new_re = fade * rot_re + b_re * flow_row[None, :]
        new_im = fade * rot_im + b_im * flow_row[None, :]
        out_row = lax.optimization_barrier(jnp.sum(c_re * new_re - c_im * new_im, axis=0))
        return ((new_re, new_im), out_row)
    zeros = jnp.zeros((MODES, EMBED_DIMENSION), jnp.float32)
    final_state, rec = lax.scan(advance, (zeros, zeros), (decay, inflow))
    return (attn, rec)
```

```python
import functools
import math

import jax
import jax.numpy as jnp
from jax import lax
from jax.experimental import pallas as pl
from jax.experimental.pallas import tpu as pltpu
from jax.sharding import PartitionSpec as P

HD = 128
EMBED_DIMENSION = 5120
MODES = 16
ROWS = 256
BLK = 16
NBLK = ROWS // BLK
NX = 4
NY = 4
NZ = 8
SEQ = 32
NEG = -1e30
SCALE2 = math.log2(math.e) / math.sqrt(HD)
F32 = jnp.float32


def device_of(y, x, core):
    return (y * NX + x) * 2 + core


def chip_pairs(dy, dx, cores=(0, 1)):
    pairs = []
    for chip in range(NX * NY):
        target = chip + dy * NX + dx
        if 0 <= target < NX * NY:
            pairs += [(chip * 2 + c, target * 2 + c) for c in cores]
    return pairs


def ring_x_pairs(step, cores=(0, 1)):
    return [
        (device_of(y, x, c), device_of(y, (x + step) % NX, c))
        for y in range(NY)
        for x in range(NX)
        for c in cores
    ]


def two_back_second_hop():
    pairs = []
    for chip in range(NX * NY):
        y, x = divmod(chip, NX)
        if chip + 2 < NX * NY:
            pairs.append((device_of(y, (x - 1) % NX, 0), (chip + 2) * 2))
    return pairs


def shift_y_pairs(step):
    return [
        (device_of(y, x, c), device_of(y + step, x, c))
        for y in range(NY - step)
        for x in range(NX)
        for c in (0, 1)
    ]


CORE_SWAP = [(d, d ^ 1) for d in range(SEQ)]
CORE_UP = [(d, d + 1) for d in range(0, SEQ, 2)]
CORE_DOWN = [(d + 1, d) for d in range(0, SEQ, 2)]


def cmul(a, b):
    return (a[0] * b[0] - a[1] * b[1], a[0] * b[1] + a[1] * b[0])


def attention_kernel(
    ok_ref, q_ref, k0, v0, k2, v2, k4, v4, ks, vs, ku, vu, kd, vd, o_ref, ssq_ref, sq_acc
):
    head = pl.program_id(0)
    q = q_ref[...]
    row = lax.broadcasted_iota(jnp.int32, (ROWS, ROWS), 0)
    col = lax.broadcasted_iota(jnp.int32, (ROWS, ROWS), 1)
    core = ok_ref[4]
    kx = jnp.where(core == 0, kd[0], ku[0])
    vx = jnp.where(core == 0, vd[0], vu[0])

    def scores(k):
        return lax.dot_general(q, k, (((1,), (1,)), ((), ())), preferred_element_type=F32)

    low = row - jnp.where(ok_ref[1] == 1, 0, -2 * ROWS)
    parts = [
        jnp.where(col <= row, scores(k0[0]), NEG),
        jnp.where(ok_ref[0] == 1, scores(k2[0]), NEG),
        jnp.where(col > low, scores(k4[0]), NEG),
        jnp.where(ok_ref[2] == 1, scores(ks[0]), NEG),
        jnp.where(ok_ref[3] == 1, scores(kx), NEG),
    ]
    top = functools.reduce(jnp.maximum, parts)
    top = jnp.max(top, axis=1, keepdims=True)
    weights = [jnp.exp2((s - top) * SCALE2) for s in parts]
    total = functools.reduce(jnp.add, weights)
    total = jnp.sum(total, axis=1, keepdims=True)
    mixed = None
    for w, v in zip(weights, (v0[0], v2[0], v4[0], vs[0], vx)):
        term = jnp.dot(w.astype(jnp.bfloat16), v, preferred_element_type=F32)
        mixed = term if mixed is None else mixed + term
    out = (mixed / total).astype(jnp.bfloat16)
    o_ref[...] = out
    wide = out.astype(F32)
    square = wide * wide

    @pl.when(head == 0)
    def _():
        sq_acc[...] = square

    @pl.when(head > 0)
    def _():
        sq_acc[...] += square

    @pl.when(head == pl.num_programs(0) - 1)
    def _():
        ssq_ref[...] = jnp.sum(jnp.transpose(sq_acc[...]), axis=0, keepdims=True)


def attention(ok, queries, own, sh2, sh4, swapped, up, down):
    heads = queries.shape[1] // HD
    col = pl.BlockSpec((ROWS, HD), lambda h: (0, h))
    kspec = pl.BlockSpec((1, ROWS, HD), lambda h: (0, 0, h))
    vspec = pl.BlockSpec((1, ROWS, HD), lambda h: (1, 0, h))
    pairs = [own, sh2, sh4, swapped, up, down]
    operands = [a for pair in pairs for a in (pair, pair)]
    return pl.pallas_call(
        attention_kernel,
        grid=(heads,),
        in_specs=[pl.BlockSpec(memory_space=pltpu.SMEM), col] + [kspec, vspec] * len(pairs),
        out_specs=[col, pl.BlockSpec((1, ROWS), lambda h: (0, 0))],
        out_shape=[
            jax.ShapeDtypeStruct(queries.shape, jnp.bfloat16),
            jax.ShapeDtypeStruct((1, ROWS), F32),
        ],
        scratch_shapes=[pltpu.VMEM((ROWS, HD), F32)],
        compiler_params=pltpu.CompilerParams(vmem_limit_bytes=40 * 2**20),
        cost_estimate=pl.CostEstimate(flops=840_000_000, bytes_accessed=6_000_000, transcendentals=1_640_000),
        name="attention",
    )(ok, queries, *operands)


def tables_kernel(decay_ref, amp_ref, cb_ref, rot_ref, w_ref, fall_ref, fade_ref, kern_ref, total_ref):
    cum = jnp.zeros((NBLK, HD), F32)
    for r in range(BLK):
        tokens = pl.ds(r, NBLK, stride=BLK)
        cum = cum + decay_ref[tokens, :]
        w_ref[r] = jnp.exp(cum) * amp_ref[tokens, :]
        fall_ref[r] = jnp.exp(-cum)
    fade_ref[...] = jnp.exp(-cum)
    total_ref[...] = jnp.sum(cum, axis=0, keepdims=True)
    z = (cb_ref[0], cb_ref[1])
    rot = (rot_ref[0], rot_ref[1])
    for lag in range(BLK):
        kern_ref[pl.ds(lag, 1), :] = jnp.sum(z[0], axis=0, keepdims=True)
        z = cmul(z, rot)


def tables(decay, amp, cb, rot):
    width = decay.shape[1]
    tokens = pl.BlockSpec((ROWS, HD), lambda h: (0, h))
    modes = pl.BlockSpec((2, MODES, HD), lambda h: (0, 0, h))
    cube = pl.BlockSpec((BLK, NBLK, HD), lambda h: (0, 0, h))
    flat = pl.BlockSpec((NBLK, HD), lambda h: (0, h))
    return pl.pallas_call(
        tables_kernel,
        grid=(width // HD,),
        in_specs=[tokens, tokens, modes, modes],
        out_specs=[cube, cube, flat, flat, pl.BlockSpec((1, HD), lambda h: (0, h))],
        out_shape=[
            jax.ShapeDtypeStruct((BLK, NBLK, width), F32),
            jax.ShapeDtypeStruct((BLK, NBLK, width), F32),
            jax.ShapeDtypeStruct((NBLK, width), F32),
            jax.ShapeDtypeStruct((BLK, width), F32),
            jax.ShapeDtypeStruct((1, width), F32),
        ],
        cost_estimate=pl.CostEstimate(flops=4_000_000, bytes_accessed=3_000_000, transcendentals=400_000),
        name="tables",
    )(decay, amp, cb, rot)


def chain_step(state, rot16, fade_row, end):
    turned = cmul(state, rot16)
    return (fade_row * turned[0] + end[0], fade_row * turned[1] + end[1])


def ends_kernel(
    attn_ref, w_ref, ssq_ref, rot_ref, rot16_ref, fade_ref, g_ref, end_re, end_im, sum_ref, flat, scale
):
    heads = attn_ref.shape[1] // HD
    row_scale = lax.rsqrt(ssq_ref[...] * (1.0 / EMBED_DIMENSION) + 1e-06)
    scale[...] = jnp.transpose(jnp.broadcast_to(row_scale, (HD, ROWS)))
    group = 4
    for tile in range(heads):
        lanes = pl.ds(tile * HD, HD)
        flat[tile] = attn_ref[:, lanes].astype(F32)
        for r in range(BLK):
            tokens = pl.ds(r, NBLK, stride=BLK)
            g_ref[r, :, lanes] = flat[tile, tokens, :] * w_ref[r, :, lanes] * scale[tokens, :]
        fade = fade_ref[:, lanes]
        for base in range(0, MODES, group):
            modes = range(base, base + group)
            cos = [rot_ref[0, pl.ds(m, 1), lanes] for m in modes]
            twice = [jnp.broadcast_to(2.0 * c, (NBLK, HD)) for c in cos]
            first = g_ref[0, :, lanes]
            older = [first] * group
            second = g_ref[1, :, lanes]
            newer = [twice[i] * first + second for i in range(group)]
            for r in range(2, BLK):
                term = g_ref[r, :, lanes]
                for i in range(group):
                    older[i], newer[i] = newer[i], twice[i] * newer[i] + (term - older[i])
            for i, m in enumerate(modes):
                sin = rot_ref[1, pl.ds(m, 1), lanes]
                end_re[tile, pl.ds(m * NBLK, NBLK), :] = fade * (newer[i] - cos[i] * older[i])
                end_im[tile, pl.ds(m * NBLK, NBLK), :] = fade * (sin * older[i])
    states = [None] * heads
    for j in range(NBLK):
        at = pl.ds(j, MODES, stride=NBLK)
        for tile in range(heads):
            lanes = pl.ds(tile * HD, HD)
            end = (end_re[tile, at, :], end_im[tile, at, :])
            if j == 0:
                states[tile] = end
            else:
                rot16 = (rot16_ref[0, :, lanes], rot16_ref[1, :, lanes])
                states[tile] = chain_step(states[tile], rot16, fade_ref[pl.ds(j, 1), lanes], end)
    for tile in range(heads):
        lanes = pl.ds(tile * HD, HD)
        sum_ref[0, :, lanes] = states[tile][0]
        sum_ref[1, :, lanes] = states[tile][1]


def block_ends(attn, w, ssq, rot, rot16, fade):
    width = attn.shape[1]
    tiles = width // HD
    return pl.pallas_call(
        ends_kernel,
        out_shape=[
            jax.ShapeDtypeStruct((BLK, NBLK, width), F32),
            jax.ShapeDtypeStruct((tiles, MODES * NBLK, HD), F32),
            jax.ShapeDtypeStruct((tiles, MODES * NBLK, HD), F32),
            jax.ShapeDtypeStruct((2, MODES, width), F32),
        ],
        scratch_shapes=[pltpu.VMEM((tiles, ROWS, HD), F32), pltpu.VMEM((ROWS, HD), F32)],
        compiler_params=pltpu.CompilerParams(vmem_limit_bytes=32 * 2**20),
        cost_estimate=pl.CostEstimate(flops=8_000_000, bytes_accessed=4_000_000, transcendentals=0),
        name="block_ends",
    )(attn, w, ssq, rot, rot16, fade)


def local_kernel(g_ref, kern_ref, out_ref):
    heads = g_ref.shape[2] // HD
    for tile in range(heads):
        lanes = pl.ds(tile * HD, HD)
        g = [g_ref[r, :, lanes] for r in range(BLK)]
        total = [None] * BLK
        for lag in range(BLK):
            k = jnp.broadcast_to(kern_ref[pl.ds(lag, 1), lanes], (NBLK, HD))
            for r in range(lag, BLK):
                term = k * g[r - lag]
                total[r] = term if total[r] is None else total[r] + term
        for r in range(BLK):
            out_ref[r, :, lanes] = total[r]


def local_part(g, kern):
    return pl.pallas_call(
        local_kernel,
        out_shape=jax.ShapeDtypeStruct(g.shape, F32),
        compiler_params=pltpu.CompilerParams(vmem_limit_bytes=32 * 2**20),
        cost_estimate=pl.CostEstimate(flops=3_000_000, bytes_accessed=1_300_000, transcendentals=0),
        name="local_part",
    )(g, kern)


def finish_kernel(
    start_ref, end_re, end_im, local_ref, fall_ref, fade_ref, rot_ref, rot16_ref, cb_ref, rec_ref, st_re, st_im, acc, out
):
    heads = rec_ref.shape[1] // HD
    states = [(start_ref[0, :, pl.ds(t * HD, HD)], start_ref[1, :, pl.ds(t * HD, HD)]) for t in range(heads)]
    for j in range(NBLK):
        at = pl.ds(j, MODES, stride=NBLK)
        for tile in range(heads):
            lanes = pl.ds(tile * HD, HD)
            st_re[tile, at, :] = states[tile][0]
            st_im[tile, at, :] = states[tile][1]
            if j + 1 < NBLK:
                rot16 = (rot16_ref[0, :, lanes], rot16_ref[1, :, lanes])
                end = (end_re[tile, at, :], end_im[tile, at, :])
                states[tile] = chain_step(states[tile], rot16, fade_ref[pl.ds(j, 1), lanes], end)
    group = 8
    for tile in range(heads):
        lanes = pl.ds(tile * HD, HD)
        for base in range(0, MODES, group):
            older, newer, twice = [], [], []
            for m in range(base, base + group):
                at = pl.ds(m * NBLK, NBLK)
                own = pl.ds(m, 1)
                z = cmul((st_re[tile, at, :], st_im[tile, at, :]), (cb_ref[0, own, lanes], cb_ref[1, own, lanes]))
                cos = rot_ref[0, own, lanes]
                older.append(z[0])
                newer.append(cos * z[0] - rot_ref[1, own, lanes] * z[1])
                twice.append(jnp.broadcast_to(2.0 * cos, (NBLK, HD)))
            for r in range(BLK):
                if r > 0:
                    for i in range(group):
                        older[i], newer[i] = newer[i], twice[i] * newer[i] - older[i]
                total = functools.reduce(jnp.add, newer)
                if base == 0:
                    acc[r] = local_ref[r, :, lanes] + total
                else:
                    out[tile, pl.ds(r, NBLK, stride=BLK), :] = (acc[r] + total) * fall_ref[r, :, lanes]
        rec_ref[:, lanes] = out[tile]


def finish(start, end_re, end_im, local, fall, fade, rot, rot16, cb):
    width = fall.shape[2]
    tiles = width // HD
    return pl.pallas_call(
        finish_kernel,
        out_shape=jax.ShapeDtypeStruct((ROWS, width), F32),
        scratch_shapes=[
            pltpu.VMEM((tiles, MODES * NBLK, HD), F32),
            pltpu.VMEM((tiles, MODES * NBLK, HD), F32),
            pltpu.VMEM((BLK, NBLK, HD), F32),
            pltpu.VMEM((tiles, ROWS, HD), F32),
        ],
        compiler_params=pltpu.CompilerParams(vmem_limit_bytes=32 * 2**20),
        cost_estimate=pl.CostEstimate(flops=8_000_000, bytes_accessed=5_000_000, transcendentals=0),
        name="finish",
    )(start, end_re, end_im, local, fall, fade, rot, rot16, cb)


def cexp(theta, steps):
    angle = theta * float(steps)
    return (jnp.cos(angle), jnp.sin(angle))


def scaled(fade, phase):
    return (fade * phase[0], fade * phase[1])


def cadd(*terms):
    return (sum(t[0] for t in terms), sum(t[1] for t in terms))


def where_pair(flag, value):
    return tuple(jnp.where(flag, part, 0.0) for part in value)


def shards(queries, keys, values, decay, gain, theta, mode_coeffs):
    width = queries.shape[1]
    me = lax.axis_index("seq")
    core = me % 2
    chip = me // 2
    x = chip % NX
    y = chip // NX

    own = jnp.stack([keys, values])
    sh2 = lax.ppermute(own, "seq", chip_pairs(0, 1))
    hop = lax.ppermute(own, "seq", ring_x_pairs(-1, (0,)))
    up = lax.ppermute(own, "seq", CORE_UP)
    far0 = lax.ppermute(hop, "seq", two_back_second_hop())
    far1 = lax.ppermute(sh2, "seq", chip_pairs(0, 1, (1,)))
    swapped = lax.ppermute(sh2, "seq", CORE_SWAP)
    down = lax.ppermute(far1, "seq", CORE_DOWN)
    sh4 = jnp.where(core == 0, far0, far1)

    amp = gain[None, :] * jnp.sqrt(-jnp.expm1(-2.0 * decay))
    rot = jnp.stack(cexp(theta, 1))
    rot16 = jnp.stack(cexp(theta, BLK))
    cb = jnp.stack(cmul((mode_coeffs[2], mode_coeffs[3]), (mode_coeffs[0], mode_coeffs[1])))
    w, fall, fade, kern, total = tables(decay, amp, cb, rot)
    totals = lax.all_gather(total[0], "seq")

    ids = jnp.arange(SEQ, dtype=jnp.int32)

    def between(first, last):
        inside = (ids >= first) & (ids < last)
        return jnp.exp(-jnp.sum(jnp.where(inside[:, None], totals, 0.0), axis=0))[None, :]

    t256 = cexp(theta, 256)
    t512 = cexp(theta, 512)
    t1024 = cexp(theta, 1024)
    t1536 = cmul(t512, t1024)
    t2048 = cexp(theta, 2048)
    t4096 = cexp(theta, 4096)
    chip0 = chip * 2
    row0 = y * NX * 2
    one = (jnp.ones_like(theta), jnp.zeros_like(theta))
    chip_turn = [one, t512, t1024, t1536]
    core_to_end = scaled(between(chip0 + 1, chip0 + 2), t256)
    core_skip = scaled(between(chip0, chip0 + 1), t256)
    to_start = []
    to_row_end = []
    for step in range(NX):
        source = jnp.mod(x - step, NX)
        begin = row0 + 2 * source + 2
        to_start.append(
            where_pair(step <= x, scaled(between(begin, chip0), chip_turn[max(step - 1, 0)])) if step else None
        )
        left = NX - 1 - source
        turn = tuple(
            jnp.where(left == 0, one[i], jnp.where(left == 1, t512[i], jnp.where(left == 2, t1024[i], t1536[i])))
            for i in (0, 1)
        )
        to_row_end.append(scaled(between(begin, row0 + 2 * NX), turn))
    row_turn = [None, one, t2048, t4096]
    row_weights = [
        where_pair(step <= y, scaled(between((y - step + 1) * 2 * NX, row0), row_turn[step])) if step > 1 else None
        for step in range(NY)
    ]
    in_row = tuple(
        jnp.where(x == 0, one[i], jnp.where(x == 1, t512[i], jnp.where(x == 2, t1024[i], t1536[i]))) for i in (0, 1)
    )
    row_to_chip = scaled(between(row0, chip0), in_row)

    ok = jnp.stack(
        [
            (me >= 2).astype(jnp.int32),
            (me >= 4).astype(jnp.int32),
            (me >= 2).astype(jnp.int32),
            ((me >= 3) | (core == 1)).astype(jnp.int32),
            core.astype(jnp.int32),
        ]
    )
    attn, ssq = attention(ok, queries, own, sh2, sh4, swapped, up, down)

    ring = lambda step: [(i, (i + step) % NZ) for i in range(NZ)]
    before = lax.ppermute(ssq, "mp", ring(1))
    after = lax.ppermute(ssq, "mp", ring(-1))
    three = before + ssq + after
    two = ssq + after
    ssq_all = three + lax.ppermute(three, "mp", ring(-3)) + lax.ppermute(two, "mp", ring(3))

    g, end_re, end_im, dev_sum = block_ends(attn, w, ssq_all, rot, rot16, fade)
    local = local_part(g, kern)

    other = lax.ppermute(dev_sum, "seq", CORE_SWAP)
    first = tuple(jnp.where(core == 0, dev_sum[i], other[i]) for i in (0, 1))
    second = tuple(jnp.where(core == 0, other[i], dev_sum[i]) for i in (0, 1))
    chip_sum = cadd(cmul(first, core_to_end), second)
    packed = jnp.stack(chip_sum)
    got = [lax.ppermute(packed, "seq", ring_x_pairs(step)) for step in (1, 2, 3)]
    chip_in = cadd(*[cmul((got[s - 1][0], got[s - 1][1]), to_start[s]) for s in (1, 2, 3)])
    row_sum = cadd(
        cmul(chip_sum, to_row_end[0]),
        *[cmul((got[s - 1][0], got[s - 1][1]), to_row_end[s]) for s in (1, 2, 3)],
    )
    packed_row = jnp.stack(row_sum)
    rows = [lax.ppermute(packed_row, "seq", shift_y_pairs(step)) for step in (1, 2, 3)]
    row_in = cadd(
        (rows[0][0], rows[0][1]),
        *[cmul((rows[s - 1][0], rows[s - 1][1]), row_weights[s]) for s in (2, 3)],
    )
    at_chip = cadd(cmul(row_in, row_to_chip), chip_in)
    at_second = cadd(cmul(at_chip, core_skip), first)
    start = jnp.stack([jnp.where(core == 0, at_chip[i], at_second[i]) for i in (0, 1)])

    rec = finish(start, end_re, end_im, local, fall, fade, rot, rot16, cb)
    return (attn, rec)


def solution(mesh):
    placed = (
        P("seq", "mp"),
        P("seq", "mp"),
        P("seq", "mp"),
        P("seq", "mp"),
        P("mp"),
        P(None, "mp"),
        P(None, None, "mp"),
    )
    return jax.shard_map(
        shards,
        mesh=mesh,
        in_specs=placed,
        out_specs=(P("seq", "mp"), P("seq", "mp")),
        check_vma=False,
    )
```

```python
import functools
import math

import jax
import jax.numpy as jnp
from jax import lax
from jax.experimental import pallas as pl
from jax.experimental.pallas import tpu as pltpu
from jax.sharding import PartitionSpec as P

HD = 128
EMBED_DIMENSION = 5120
MODES = 16
HALF = MODES // 2
ROWS = 256
BLK = 16
NBLK = ROWS // BLK
NX = 4
NY = 4
NZ = 8
SEQ = 32
NEG = -1e30
SCALE2 = math.log2(math.e) / math.sqrt(HD)
F32 = jnp.float32


def device_of(y, x, core):
    return (y * NX + x) * 2 + core


def chip_pairs(dy, dx, cores=(0, 1)):
    pairs = []
    for chip in range(NX * NY):
        target = chip + dy * NX + dx
        if 0 <= target < NX * NY:
            pairs += [(chip * 2 + c, target * 2 + c) for c in cores]
    return pairs


def ring_x_pairs(step, cores=(0, 1)):
    return [
        (device_of(y, x, c), device_of(y, (x + step) % NX, c))
        for y in range(NY)
        for x in range(NX)
        for c in cores
    ]


def two_back_second_hop():
    pairs = []
    for chip in range(NX * NY):
        y, x = divmod(chip, NX)
        if chip + 2 < NX * NY:
            pairs.append((device_of(y, (x - 1) % NX, 0), (chip + 2) * 2))
    return pairs


def shift_y_pairs(step):
    return [
        (device_of(y, x, c), device_of(y + step, x, c))
        for y in range(NY - step)
        for x in range(NX)
        for c in (0, 1)
    ]


CORE_SWAP = [(d, d ^ 1) for d in range(SEQ)]
CORE_UP = [(d, d + 1) for d in range(0, SEQ, 2)]
CORE_DOWN = [(d + 1, d) for d in range(0, SEQ, 2)]


def cmul(a, b):
    return (a[0] * b[0] - a[1] * b[1], a[0] * b[1] + a[1] * b[0])


def masks():
    row = lax.broadcasted_iota(jnp.int32, (ROWS, ROWS), 0)
    col = lax.broadcasted_iota(jnp.int32, (ROWS, ROWS), 1)
    return row, col


def scores_of(q, k):
    return lax.dot_general(q, k, (((1,), (1,)), ((), ())), preferred_element_type=F32)


def softmax_parts(parts, vals, top):
    weights = [jnp.exp2((s - top) * SCALE2) for s in parts]
    total = jnp.sum(functools.reduce(jnp.add, weights), axis=1, keepdims=True)
    mixed = [jnp.dot(w.astype(jnp.bfloat16), v, preferred_element_type=F32) for w, v in zip(weights, vals)]
    return total, functools.reduce(jnp.add, mixed)


def near_kernel(pos_ref, q_ref, k0, v0, k2, v2, ks, vs, top_ref, total_ref, mixed_ref):
    q = q_ref[...]
    row, col = masks()
    there = pos_ref[0] == 1
    parts = [
        jnp.where(col <= row, scores_of(q, k0[0]), NEG),
        jnp.where(there, scores_of(q, k2[0]), NEG),
        jnp.where(there, scores_of(q, ks[0]), NEG),
    ]
    top = jnp.max(functools.reduce(jnp.maximum, parts), axis=1, keepdims=True)
    total, mixed = softmax_parts(parts, (v0[0], v2[0], vs[0]), top)
    top_ref[...] = jnp.broadcast_to(top, (ROWS, HD))
    total_ref[...] = jnp.broadcast_to(total, (ROWS, HD))
    mixed_ref[...] = mixed


def far_kernel(
    pos_ref, q_ref, k4, v4, ku, vu, kd, vd, top_ref, total_ref, mixed_ref, o_ref, ssq_ref, sq_acc
):
    head = pl.program_id(0)
    q = q_ref[...]
    row, col = masks()
    first_core = pos_ref[3] == 0
    kx = jnp.where(first_core, kd[0], ku[0])
    vx = jnp.where(first_core, vd[0], vu[0])
    low = row - jnp.where(pos_ref[1] == 1, 0, -2 * ROWS)
    parts = [
        jnp.where(col > low, scores_of(q, k4[0]), NEG),
        jnp.where(pos_ref[2] == 1, scores_of(q, kx), NEG),
    ]
    old = top_ref[...]
    top = jnp.maximum(old[:, :1], jnp.max(jnp.maximum(*parts), axis=1, keepdims=True))
    total, mixed = softmax_parts(parts, (v4[0], vx), top)
    shrink = jnp.exp2((old - top) * SCALE2)
    total = total_ref[...] * shrink + total
    out = ((mixed_ref[...] * shrink + mixed) / total).astype(jnp.bfloat16)
    o_ref[...] = out
    wide = out.astype(F32)
    square = wide * wide

    @pl.when(head == 0)
    def _():
        sq_acc[...] = square

    @pl.when(head > 0)
    def _():
        sq_acc[...] += square

    @pl.when(head == pl.num_programs(0) - 1)
    def _():
        ssq_ref[...] = jnp.sum(jnp.transpose(sq_acc[...]), axis=0, keepdims=True)


def attention_near(pos, queries, own, sh2, swapped):
    width = queries.shape[1]
    col = pl.BlockSpec((ROWS, HD), lambda h: (0, h))
    kspec = pl.BlockSpec((1, ROWS, HD), lambda h: (0, 0, h))
    vspec = pl.BlockSpec((1, ROWS, HD), lambda h: (1, 0, h))
    return pl.pallas_call(
        near_kernel,
        grid=(width // HD,),
        in_specs=[pl.BlockSpec(memory_space=pltpu.SMEM), col] + [kspec, vspec] * 3,
        out_specs=[col, col, col],
        out_shape=[jax.ShapeDtypeStruct(queries.shape, F32)] * 3,
        compiler_params=pltpu.CompilerParams(vmem_limit_bytes=32 * 2**20),
        cost_estimate=pl.CostEstimate(flops=500_000_000, bytes_accessed=5_000_000, transcendentals=1_000_000),
        name="attention_near",
    )(pos, queries, own, own, sh2, sh2, swapped, swapped)


def attention_far(pos, queries, sh4, up, down, near):
    width = queries.shape[1]
    col = pl.BlockSpec((ROWS, HD), lambda h: (0, h))
    kspec = pl.BlockSpec((1, ROWS, HD), lambda h: (0, 0, h))
    vspec = pl.BlockSpec((1, ROWS, HD), lambda h: (1, 0, h))
    return pl.pallas_call(
        far_kernel,
        grid=(width // HD,),
        in_specs=[pl.BlockSpec(memory_space=pltpu.SMEM), col] + [kspec, vspec] * 3 + [col] * 3,
        out_specs=[col, pl.BlockSpec((1, ROWS), lambda h: (0, 0))],
        out_shape=[
            jax.ShapeDtypeStruct(queries.shape, jnp.bfloat16),
            jax.ShapeDtypeStruct((1, ROWS), F32),
        ],
        scratch_shapes=[pltpu.VMEM((ROWS, HD), F32)],
        compiler_params=pltpu.CompilerParams(vmem_limit_bytes=32 * 2**20),
        cost_estimate=pl.CostEstimate(flops=340_000_000, bytes_accessed=5_000_000, transcendentals=650_000),
        name="attention_far",
    )(pos, queries, sh4, sh4, up, up, down, down, *near)


def tables_kernel(decay_ref, amp_ref, cb_ref, rot_ref, w_ref, fall_ref, fade_ref, kern_ref, total_ref):
    cum = jnp.zeros((NBLK, HD), F32)
    for r in range(BLK):
        tokens = pl.ds(r, NBLK, stride=BLK)
        cum = cum + decay_ref[tokens, :]
        w_ref[r] = jnp.exp(cum) * amp_ref[tokens, :]
        fall_ref[r] = jnp.exp(-cum)
    fade_ref[...] = jnp.exp(-cum)
    total_ref[...] = jnp.sum(cum, axis=0, keepdims=True)
    z = (cb_ref[0], cb_ref[1])
    rot = (rot_ref[0], rot_ref[1])
    for lag in range(BLK):
        kern_ref[pl.ds(lag, 1), :] = jnp.sum(z[0], axis=0, keepdims=True)
        z = cmul(z, rot)


def tables(decay, amp, cb, rot):
    width = decay.shape[1]
    tokens = pl.BlockSpec((ROWS, HD), lambda h: (0, h))
    modes = pl.BlockSpec((2, MODES, HD), lambda h: (0, 0, h))
    cube = pl.BlockSpec((BLK, NBLK, HD), lambda h: (0, 0, h))
    flat = pl.BlockSpec((NBLK, HD), lambda h: (0, h))
    return pl.pallas_call(
        tables_kernel,
        grid=(width // HD,),
        in_specs=[tokens, tokens, modes, modes],
        out_specs=[cube, cube, flat, flat, pl.BlockSpec((1, HD), lambda h: (0, h))],
        out_shape=[
            jax.ShapeDtypeStruct((BLK, NBLK, width), F32),
            jax.ShapeDtypeStruct((BLK, NBLK, width), F32),
            jax.ShapeDtypeStruct((NBLK, width), F32),
            jax.ShapeDtypeStruct((BLK, width), F32),
            jax.ShapeDtypeStruct((1, width), F32),
        ],
        cost_estimate=pl.CostEstimate(flops=4_000_000, bytes_accessed=3_000_000, transcendentals=400_000),
        name="tables",
    )(decay, amp, cb, rot)


def chain_step(state, rot16, fade_row, end):
    turned = cmul(state, rot16)
    return (fade_row * turned[0] + end[0], fade_row * turned[1] + end[1])


def ends_kernel(
    attn_ref, w_ref, ssq_ref, rot_ref, rot16_ref, fade_ref, fall_ref, g_ref, end_re, end_im, sum_ref, flat, scale
):
    heads = attn_ref.shape[1] // HD
    row_scale = lax.rsqrt(ssq_ref[...] * (1.0 / EMBED_DIMENSION) + 1e-06)
    scale[...] = jnp.transpose(jnp.broadcast_to(row_scale, (HD, ROWS)))
    group = 4
    for tile in range(heads):
        lanes = pl.ds(tile * HD, HD)
        flat[tile] = attn_ref[:, lanes].astype(F32)
        for r in range(BLK):
            tokens = pl.ds(r, NBLK, stride=BLK)
            g_ref[r, :, lanes] = flat[tile, tokens, :] * w_ref[r, :, lanes] * scale[tokens, :]
        fade = fade_ref[:, lanes]
        for base in range(0, MODES, group):
            modes = range(base, base + group)
            cos = [rot_ref[0, pl.ds(m, 1), lanes] for m in modes]
            twice = [jnp.broadcast_to(2.0 * c, (NBLK, HD)) for c in cos]
            first = g_ref[0, :, lanes]
            older = [first] * group
            second = g_ref[1, :, lanes]
            newer = [twice[i] * first + second for i in range(group)]
            for r in range(2, BLK):
                term = g_ref[r, :, lanes]
                for i in range(group):
                    older[i], newer[i] = newer[i], twice[i] * newer[i] + (term - older[i])
            for i, m in enumerate(modes):
                sin = rot_ref[1, pl.ds(m, 1), lanes]
                end_re[tile, pl.ds(m * NBLK, NBLK), :] = fade * (newer[i] - cos[i] * older[i])
                end_im[tile, pl.ds(m * NBLK, NBLK), :] = fade * (sin * older[i])
    states = [None] * heads
    for j in range(NBLK):
        at = pl.ds(j, MODES, stride=NBLK)
        for tile in range(heads):
            lanes = pl.ds(tile * HD, HD)
            end = (end_re[tile, at, :], end_im[tile, at, :])
            if j == 0:
                states[tile] = end
            else:
                rot16 = (rot16_ref[0, :, lanes], rot16_ref[1, :, lanes])
                states[tile] = chain_step(states[tile], rot16, fade_ref[pl.ds(j, 1), lanes], end)
    for tile in range(heads):
        lanes = pl.ds(tile * HD, HD)
        sum_ref[pl.ds(tile * 2 * MODES, MODES), :] = states[tile][0]
        sum_ref[pl.ds(tile * 2 * MODES + MODES, MODES), :] = states[tile][1]
        sum_ref[pl.ds(heads * 2 * MODES + tile, 1), :] = fall_ref[:, lanes]
    used = heads * (2 * MODES + 1)
    sum_ref[pl.ds(used, sum_ref.shape[0] - used), :] = jnp.zeros((sum_ref.shape[0] - used, HD), F32)


def padded(rows):
    return -(-rows // 8) * 8


def block_ends(attn, w, ssq, rot, rot16, fade, total):
    width = attn.shape[1]
    tiles = width // HD
    return pl.pallas_call(
        ends_kernel,
        out_shape=[
            jax.ShapeDtypeStruct((BLK, NBLK, width), F32),
            jax.ShapeDtypeStruct((tiles, MODES * NBLK, HD), F32),
            jax.ShapeDtypeStruct((tiles, MODES * NBLK, HD), F32),
            jax.ShapeDtypeStruct((padded(tiles * (2 * MODES + 1)), HD), F32),
        ],
        scratch_shapes=[pltpu.VMEM((tiles, ROWS, HD), F32), pltpu.VMEM((ROWS, HD), F32)],
        compiler_params=pltpu.CompilerParams(vmem_limit_bytes=32 * 2**20),
        cost_estimate=pl.CostEstimate(flops=8_000_000, bytes_accessed=4_000_000, transcendentals=0),
        name="block_ends",
    )(attn, w, ssq, rot, rot16, fade, total)


def local_kernel(g_ref, kern_ref, out_ref):
    heads = g_ref.shape[2] // HD
    for tile in range(heads):
        lanes = pl.ds(tile * HD, HD)
        g = [g_ref[r, :, lanes] for r in range(BLK)]
        total = [None] * BLK
        for lag in range(BLK):
            k = jnp.broadcast_to(kern_ref[pl.ds(lag, 1), lanes], (NBLK, HD))
            for r in range(lag, BLK):
                term = k * g[r - lag]
                total[r] = term if total[r] is None else total[r] + term
        for r in range(BLK):
            out_ref[r, :, lanes] = total[r]


def local_part(g, kern):
    return pl.pallas_call(
        local_kernel,
        out_shape=jax.ShapeDtypeStruct(g.shape, F32),
        compiler_params=pltpu.CompilerParams(vmem_limit_bytes=32 * 2**20),
        cost_estimate=pl.CostEstimate(flops=3_000_000, bytes_accessed=1_300_000, transcendentals=0),
        name="local_part",
    )(g, kern)


def chip_kernel(pos_ref, own_ref, other_ref, turn_ref, out_ref):
    tiles = turn_ref.shape[2] // HD
    core = pos_ref[3]
    first_core = core == 0
    half = pl.multiple_of(core * HALF, HALF)
    for tile in range(tiles):
        lanes = pl.ds(tile * HD, HD)
        rows = [pl.ds(pl.multiple_of(tile * 2 * MODES + i * MODES + half, HALF), HALF) for i in (0, 1)]
        own = [own_ref[at, :] for at in rows]
        other = [other_ref[at, :] for at in rows]
        at = pl.ds(tiles * 2 * MODES + tile, 1)
        own_decay, other_decay = own_ref[at, :], other_ref[at, :]
        fade = jnp.exp(-jnp.where(first_core, other_decay, own_decay))
        turn = [fade * turn_ref[i, pl.ds(half, HALF), lanes] for i in (0, 1)]
        first = [jnp.where(first_core, own[i], other[i]) for i in (0, 1)]
        second = [jnp.where(first_core, other[i], own[i]) for i in (0, 1)]
        moved = cmul(first, turn)
        out_ref[pl.ds(tile * MODES, HALF), :] = moved[0] + second[0]
        out_ref[pl.ds(tile * MODES + HALF, HALF), :] = moved[1] + second[1]
        out_ref[pl.ds(tiles * MODES + tile, 1), :] = own_decay + other_decay
    used = tiles * (MODES + 1)
    out_ref[pl.ds(used, out_ref.shape[0] - used), :] = jnp.zeros((out_ref.shape[0] - used, HD), F32)


def chip_sum(pos, own, other, turn):
    tiles = turn.shape[2] // HD
    return pl.pallas_call(
        chip_kernel,
        in_specs=[pl.BlockSpec(memory_space=pltpu.SMEM)] + [pl.BlockSpec(memory_space=pltpu.VMEM)] * 3,
        out_shape=jax.ShapeDtypeStruct((padded(tiles * (MODES + 1)), HD), F32),
        cost_estimate=pl.CostEstimate(flops=100_000, bytes_accessed=300_000, transcendentals=640),
        name="chip_sum",
    )(pos, own, other, turn)


def half_of(ref, tile):
    return (ref[pl.ds(tile * MODES, HALF), :], ref[pl.ds(tile * MODES + HALF, HALF), :])


def row_kernel(pos_ref, c0, c1, c2, c3, turn_ref, row_ref, in_ref, before_ref):
    tiles = in_ref.shape[0] // MODES
    chips = (c0, c1, c2, c3)
    x = pos_ref[4]
    place = [jnp.where(x >= s, x - s, x - s + NX) for s in range(NX)]
    for tile in range(tiles):
        lanes = pl.ds(tile * HD, HD)
        at = pl.ds(tiles * MODES + tile, 1)
        decay = [c[at, :] for c in chips]
        value = [half_of(c, tile) for c in chips]
        row = [jnp.zeros((HALF, HD), F32)] * 2
        into = [jnp.zeros((HALF, HD), F32)] * 2
        for s in range(NX):
            after = jnp.zeros((1, HD), F32)
            for k in range(NX):
                if k != s:
                    after = after + jnp.where(place[k] > place[s], decay[k], 0.0)
            fade = jnp.exp(-after)
            left = NX - 1 - place[s]
            part = cmul(value[s], [fade * turn_ref[left, i, :, lanes] for i in (0, 1)])
            row = [row[i] + part[i] for i in (0, 1)]
            if s:
                turn = [turn_ref[s - 1, i, :, lanes] for i in (0, 1)]
                if s > 1:
                    fade = jnp.exp(-functools.reduce(jnp.add, decay[1:s]))
                    turn = [fade * t for t in turn]
                part = cmul(value[s], turn)
                into = [into[i] + jnp.where(x >= s, part[i], 0.0) for i in (0, 1)]
        row_ref[pl.ds(tile * MODES, HALF), :] = row[0]
        row_ref[pl.ds(tile * MODES + HALF, HALF), :] = row[1]
        row_ref[at, :] = functools.reduce(jnp.add, decay)
        in_ref[pl.ds(tile * MODES, HALF), :] = into[0]
        in_ref[pl.ds(tile * MODES + HALF, HALF), :] = into[1]
        before = jnp.zeros((1, HD), F32)
        for s in range(1, NX):
            before = before + jnp.where(x >= s, decay[s], 0.0)
        before_ref[:, lanes] = before
    used = tiles * (MODES + 1)
    row_ref[pl.ds(used, row_ref.shape[0] - used), :] = jnp.zeros((row_ref.shape[0] - used, HD), F32)


def row_sum(pos, chips, turns):
    width = turns.shape[3]
    tiles = width // HD
    return pl.pallas_call(
        row_kernel,
        in_specs=[pl.BlockSpec(memory_space=pltpu.SMEM)] + [pl.BlockSpec(memory_space=pltpu.VMEM)] * 5,
        out_shape=[
            jax.ShapeDtypeStruct((padded(tiles * (MODES + 1)), HD), F32),
            jax.ShapeDtypeStruct((tiles * MODES, HD), F32),
            jax.ShapeDtypeStruct((1, width), F32),
        ],
        cost_estimate=pl.CostEstimate(flops=300_000, bytes_accessed=400_000, transcendentals=5000),
        name="row_sum",
    )(pos, *chips, turns)


def entry_kernel(pos_ref, r1, r2, r3, in_ref, before_ref, turn_ref, out_ref):
    tiles = in_ref.shape[0] // MODES
    x = pos_ref[4]
    for tile in range(tiles):
        lanes = pl.ds(tile * HD, HD)
        at = pl.ds(tiles * MODES + tile, 1)
        fade = jnp.exp(-r1[at, :])
        row = half_of(r1, tile)
        part = cmul(half_of(r2, tile), [fade * turn_ref[NX, i, :, lanes] for i in (0, 1)])
        row = [row[i] + part[i] for i in (0, 1)]
        fade = jnp.exp(-(r1[at, :] + r2[at, :]))
        part = cmul(half_of(r3, tile), [fade * turn_ref[NX + 1, i, :, lanes] for i in (0, 1)])
        row = [row[i] + part[i] for i in (0, 1)]
        fade = jnp.exp(-before_ref[:, lanes])
        part = cmul(row, [fade * turn_ref[x, i, :, lanes] for i in (0, 1)])
        into = half_of(in_ref, tile)
        out_ref[pl.ds(tile * MODES, HALF), :] = part[0] + into[0]
        out_ref[pl.ds(tile * MODES + HALF, HALF), :] = part[1] + into[1]


def chip_entry(pos, rows, into, before, turns):
    return pl.pallas_call(
        entry_kernel,
        in_specs=[pl.BlockSpec(memory_space=pltpu.SMEM)] + [pl.BlockSpec(memory_space=pltpu.VMEM)] * 6,
        out_shape=jax.ShapeDtypeStruct(into.shape, F32),
        cost_estimate=pl.CostEstimate(flops=300_000, bytes_accessed=400_000, transcendentals=5000),
        name="chip_entry",
    )(pos, *rows, into, before, turns)


def finish_kernel(
    pos_ref, mine_ref, theirs_ref, other_ref, turn_ref, end_re, end_im, local_ref, fall_ref, fade_ref, rot_ref,
    rot16_ref, cb_ref, rec_ref, st_re, st_im, acc, out
):
    heads = rec_ref.shape[1] // HD
    first_core = pos_ref[3] == 0
    states = []
    for tile in range(heads):
        lanes = pl.ds(tile * HD, HD)
        mine, theirs = half_of(mine_ref, tile), half_of(theirs_ref, tile)
        at_chip = [
            jnp.concatenate(
                [jnp.where(first_core, mine[i], theirs[i]), jnp.where(first_core, theirs[i], mine[i])], axis=0
            )
            for i in (0, 1)
        ]
        fade = jnp.exp(-other_ref[pl.ds(heads * 2 * MODES + tile, 1), :])
        moved = cmul(at_chip, [fade * turn_ref[i, :, lanes] for i in (0, 1)])
        other = [other_ref[pl.ds(tile * 2 * MODES + i * MODES, MODES), :] for i in (0, 1)]
        states.append(tuple(jnp.where(first_core, at_chip[i], moved[i] + other[i]) for i in (0, 1)))
    for j in range(NBLK):
        at = pl.ds(j, MODES, stride=NBLK)
        for tile in range(heads):
            lanes = pl.ds(tile * HD, HD)
            st_re[tile, at, :] = states[tile][0]
            st_im[tile, at, :] = states[tile][1]
            if j + 1 < NBLK:
                rot16 = (rot16_ref[0, :, lanes], rot16_ref[1, :, lanes])
                end = (end_re[tile, at, :], end_im[tile, at, :])
                states[tile] = chain_step(states[tile], rot16, fade_ref[pl.ds(j, 1), lanes], end)
    group = 8
    for tile in range(heads):
        lanes = pl.ds(tile * HD, HD)
        for base in range(0, MODES, group):
            older, newer, twice = [], [], []
            for m in range(base, base + group):
                at = pl.ds(m * NBLK, NBLK)
                own = pl.ds(m, 1)
                z = cmul((st_re[tile, at, :], st_im[tile, at, :]), (cb_ref[0, own, lanes], cb_ref[1, own, lanes]))
                cos = rot_ref[0, own, lanes]
                older.append(z[0])
                newer.append(cos * z[0] - rot_ref[1, own, lanes] * z[1])
                twice.append(jnp.broadcast_to(2.0 * cos, (NBLK, HD)))
            for r in range(BLK):
                if r > 0:
                    for i in range(group):
                        older[i], newer[i] = newer[i], twice[i] * newer[i] - older[i]
                total = functools.reduce(jnp.add, newer)
                if base == 0:
                    acc[r] = local_ref[r, :, lanes] + total
                else:
                    out[tile, pl.ds(r, NBLK, stride=BLK), :] = (acc[r] + total) * fall_ref[r, :, lanes]
        rec_ref[:, lanes] = out[tile]


def finish(pos, mine, theirs, other, turn, end_re, end_im, local, fall, fade, rot, rot16, cb):
    width = fall.shape[2]
    tiles = width // HD
    return pl.pallas_call(
        finish_kernel,
        in_specs=[pl.BlockSpec(memory_space=pltpu.SMEM)] + [pl.BlockSpec(memory_space=pltpu.VMEM)] * 12,
        out_shape=jax.ShapeDtypeStruct((ROWS, width), F32),
        scratch_shapes=[
            pltpu.VMEM((tiles, MODES * NBLK, HD), F32),
            pltpu.VMEM((tiles, MODES * NBLK, HD), F32),
            pltpu.VMEM((BLK, NBLK, HD), F32),
            pltpu.VMEM((tiles, ROWS, HD), F32),
        ],
        compiler_params=pltpu.CompilerParams(vmem_limit_bytes=32 * 2**20),
        cost_estimate=pl.CostEstimate(flops=8_000_000, bytes_accessed=5_000_000, transcendentals=0),
        name="finish",
    )(pos, mine, theirs, other, turn, end_re, end_im, local, fall, fade, rot, rot16, cb)


def cexp(theta, steps):
    angle = theta * float(steps)
    return (jnp.cos(angle), jnp.sin(angle))


def shards(queries, keys, values, decay, gain, theta, mode_coeffs):
    width = queries.shape[1]
    me = lax.axis_index("seq")
    core = me % 2
    chip = me // 2
    x = chip % NX

    own = jnp.stack([keys, values])
    sh2 = lax.ppermute(own, "seq", chip_pairs(0, 1))
    hop = lax.ppermute(own, "seq", ring_x_pairs(-1, (0,)))
    up = lax.ppermute(own, "seq", CORE_UP)
    far0 = lax.ppermute(hop, "seq", two_back_second_hop())
    far1 = lax.ppermute(sh2, "seq", chip_pairs(0, 1, (1,)))
    swapped = lax.ppermute(sh2, "seq", CORE_SWAP)
    down = lax.ppermute(far1, "seq", CORE_DOWN)
    sh4 = jnp.where(core == 0, far0, far1)

    amp = gain[None, :] * jnp.sqrt(-jnp.expm1(-2.0 * decay))
    rot = jnp.stack(cexp(theta, 1))
    rot16 = jnp.stack(cexp(theta, BLK))
    cb = jnp.stack(cmul((mode_coeffs[2], mode_coeffs[3]), (mode_coeffs[0], mode_coeffs[1])))
    w, fall, fade, kern, total = tables(decay, amp, cb, rot)
    turn256 = jnp.stack(cexp(theta, ROWS))
    half = lax.dynamic_slice_in_dim(theta, core * HALF, HALF, 0)
    t512, t1024 = cexp(half, 2 * ROWS), cexp(half, 4 * ROWS)
    one = (jnp.ones_like(half), jnp.zeros_like(half))
    turns = [one, t512, t1024, cmul(t512, t1024), cexp(half, 8 * ROWS), cexp(half, 16 * ROWS)]
    turns = jnp.stack([jnp.stack(t) for t in turns])

    pos = jnp.stack(
        [
            (me >= 2).astype(jnp.int32),
            (me >= 4).astype(jnp.int32),
            ((me >= 3) | (core == 1)).astype(jnp.int32),
            core.astype(jnp.int32),
            x.astype(jnp.int32),
        ]
    )
    near = attention_near(pos, queries, own, sh2, swapped)
    attn, ssq = attention_far(pos, queries, sh4, up, down, near)

    ring = lambda step: [(i, (i + step) % NZ) for i in range(NZ)]
    before = lax.ppermute(ssq, "mp", ring(1))
    after = lax.ppermute(ssq, "mp", ring(-1))
    three = before + ssq + after
    two = ssq + after
    ssq_all = three + lax.ppermute(three, "mp", ring(-3)) + lax.ppermute(two, "mp", ring(3))

    g, end_re, end_im, dev_sum = block_ends(attn, w, ssq_all, rot, rot16, fade, total)
    local = local_part(g, kern)

    other = lax.ppermute(dev_sum, "seq", CORE_SWAP)
    packed = chip_sum(pos, dev_sum, other, turn256)
    chips = [packed] + [lax.ppermute(packed, "seq", ring_x_pairs(step)) for step in (1, 2, 3)]
    row, into, before_row = row_sum(pos, chips, turns)
    rows = [lax.ppermute(row, "seq", shift_y_pairs(step)) for step in (1, 2, 3)]
    mine = chip_entry(pos, rows, into, before_row, turns)
    theirs = lax.ppermute(mine, "seq", CORE_SWAP)

    rec = finish(pos, mine, theirs, other, turn256, end_re, end_im, local, fall, fade, rot, rot16, cb)
    return (attn, rec)


def solution(mesh):
    placed = (
        P("seq", "mp"),
        P("seq", "mp"),
        P("seq", "mp"),
        P("seq", "mp"),
        P("mp"),
        P(None, "mp"),
        P(None, None, "mp"),
    )
    return jax.shard_map(
        shards,
        mesh=mesh,
        in_specs=placed,
        out_specs=(P("seq", "mp"), P("seq", "mp")),
        check_vma=False,
    )
```

```python
import functools
import math

import jax
import jax.numpy as jnp
from jax import lax
from jax.experimental import pallas as pl
from jax.experimental.pallas import tpu as pltpu
from jax.sharding import PartitionSpec as P

HD = 128
EMBED_DIMENSION = 5120
MODES = 16
HALF = MODES // 2
ROWS = 256
BLK = 16
NBLK = ROWS // BLK
NX = 4
NY = 4
NZ = 8
SEQ = 32
NEG = -1e30
SCALE2 = math.log2(math.e) / math.sqrt(HD)
F32 = jnp.float32
TURNS = (1, BLK, ROWS, 2 * ROWS, 4 * ROWS, 8 * ROWS, 16 * ROWS)


def device_of(y, x, core):
    return (y * NX + x) * 2 + core


def chip_pairs(dy, dx, cores=(0, 1)):
    pairs = []
    for chip in range(NX * NY):
        target = chip + dy * NX + dx
        if 0 <= target < NX * NY:
            pairs += [(chip * 2 + c, target * 2 + c) for c in cores]
    return pairs


def ring_x_pairs(step, cores=(0, 1)):
    return [
        (device_of(y, x, c), device_of(y, (x + step) % NX, c))
        for y in range(NY)
        for x in range(NX)
        for c in cores
    ]


def two_back_second_hop():
    pairs = []
    for chip in range(NX * NY):
        y, x = divmod(chip, NX)
        if chip + 2 < NX * NY:
            pairs.append((device_of(y, (x - 1) % NX, 0), (chip + 2) * 2))
    return pairs


def shift_y_pairs(step):
    return [
        (device_of(y, x, c), device_of(y + step, x, c))
        for y in range(NY - step)
        for x in range(NX)
        for c in (0, 1)
    ]


CORE_SWAP = [(d, d ^ 1) for d in range(SEQ)]
CORE_UP = [(d, d + 1) for d in range(0, SEQ, 2)]
CORE_DOWN = [(d + 1, d) for d in range(0, SEQ, 2)]


def cmul(a, b):
    return (a[0] * b[0] - a[1] * b[1], a[0] * b[1] + a[1] * b[0])


def masks():
    row = lax.broadcasted_iota(jnp.int32, (ROWS, ROWS), 0)
    col = lax.broadcasted_iota(jnp.int32, (ROWS, ROWS), 1)
    return row, col


def scores_of(q, k):
    return lax.dot_general(q, k, (((1,), (1,)), ((), ())), preferred_element_type=F32)


def softmax_parts(parts, vals, top):
    weights = [jnp.exp2((s - top) * SCALE2) for s in parts]
    total = jnp.sum(functools.reduce(jnp.add, weights), axis=1, keepdims=True)
    mixed = [jnp.dot(w.astype(jnp.bfloat16), v, preferred_element_type=F32) for w, v in zip(weights, vals)]
    return total, functools.reduce(jnp.add, mixed)


def near_kernel(pos_ref, q_ref, k0, v0, k2, v2, ks, vs, top_ref, total_ref, mixed_ref):
    q = q_ref[...]
    row, col = masks()
    there = pos_ref[0] == 1
    parts = [
        jnp.where(col <= row, scores_of(q, k0[0]), NEG),
        jnp.where(there, scores_of(q, k2[0]), NEG),
        jnp.where(there, scores_of(q, ks[0]), NEG),
    ]
    top = jnp.max(functools.reduce(jnp.maximum, parts), axis=1, keepdims=True)
    total, mixed = softmax_parts(parts, (v0[0], v2[0], vs[0]), top)
    top_ref[...] = jnp.broadcast_to(top, (ROWS, HD))
    total_ref[...] = jnp.broadcast_to(total, (ROWS, HD))
    mixed_ref[...] = mixed


def far_kernel(
    pos_ref, q_ref, k4, v4, ku, vu, kd, vd, top_ref, total_ref, mixed_ref, o_ref, ssq_ref, sq_acc
):
    head = pl.program_id(0)
    q = q_ref[...]
    row, col = masks()
    first_core = pos_ref[3] == 0
    kx = jnp.where(first_core, kd[0], ku[0])
    vx = jnp.where(first_core, vd[0], vu[0])
    low = row - jnp.where(pos_ref[1] == 1, 0, -2 * ROWS)
    parts = [
        jnp.where(col > low, scores_of(q, k4[0]), NEG),
        jnp.where(pos_ref[2] == 1, scores_of(q, kx), NEG),
    ]
    old = top_ref[...]
    top = jnp.maximum(old[:, :1], jnp.max(jnp.maximum(*parts), axis=1, keepdims=True))
    total, mixed = softmax_parts(parts, (v4[0], vx), top)
    shrink = jnp.exp2((old - top) * SCALE2)
    total = total_ref[...] * shrink + total
    out = ((mixed_ref[...] * shrink + mixed) / total).astype(jnp.bfloat16)
    o_ref[...] = out
    wide = out.astype(F32)
    square = wide * wide

    @pl.when(head == 0)
    def _():
        sq_acc[...] = square

    @pl.when(head > 0)
    def _():
        sq_acc[...] += square

    @pl.when(head == pl.num_programs(0) - 1)
    def _():
        ssq_ref[...] = jnp.sum(jnp.transpose(sq_acc[...]), axis=0, keepdims=True)


def attention_near(pos, queries, own, sh2, swapped):
    width = queries.shape[1]
    col = pl.BlockSpec((ROWS, HD), lambda h: (0, h))
    kspec = pl.BlockSpec((1, ROWS, HD), lambda h: (0, 0, h))
    vspec = pl.BlockSpec((1, ROWS, HD), lambda h: (1, 0, h))
    return pl.pallas_call(
        near_kernel,
        grid=(width // HD,),
        in_specs=[pl.BlockSpec(memory_space=pltpu.SMEM), col] + [kspec, vspec] * 3,
        out_specs=[col, col, col],
        out_shape=[jax.ShapeDtypeStruct(queries.shape, F32)] * 3,
        compiler_params=pltpu.CompilerParams(vmem_limit_bytes=20 * 2**20),
        cost_estimate=pl.CostEstimate(flops=500_000_000, bytes_accessed=5_000_000, transcendentals=1_000_000),
        name="attention_near",
    )(pos, queries, own, own, sh2, sh2, swapped, swapped)


def attention_far(pos, queries, sh4, up, down, near):
    width = queries.shape[1]
    col = pl.BlockSpec((ROWS, HD), lambda h: (0, h))
    kspec = pl.BlockSpec((1, ROWS, HD), lambda h: (0, 0, h))
    vspec = pl.BlockSpec((1, ROWS, HD), lambda h: (1, 0, h))
    return pl.pallas_call(
        far_kernel,
        grid=(width // HD,),
        in_specs=[pl.BlockSpec(memory_space=pltpu.SMEM), col] + [kspec, vspec] * 3 + [col] * 3,
        out_specs=[col, pl.BlockSpec((1, ROWS), lambda h: (0, 0))],
        out_shape=[
            jax.ShapeDtypeStruct(queries.shape, jnp.bfloat16),
            jax.ShapeDtypeStruct((1, ROWS), F32),
        ],
        scratch_shapes=[pltpu.VMEM((ROWS, HD), F32)],
        compiler_params=pltpu.CompilerParams(vmem_limit_bytes=20 * 2**20),
        cost_estimate=pl.CostEstimate(flops=340_000_000, bytes_accessed=5_000_000, transcendentals=650_000),
        name="attention_far",
    )(pos, queries, sh4, sh4, up, up, down, down, *near)


def one_less_exp(v):
    series = 1.0 / 720.0
    for order in (120.0, 24.0, 6.0, 2.0, 1.0):
        series = 1.0 / order - v * series
    return jnp.where(v < 0.25, v * series, 1.0 - jnp.exp(-v))


def tables_kernel(
    decay_ref, gain_ref, coef_ref, cos_ref, sin_ref, w_ref, fall_ref, fade_ref, kern_ref, total_ref, cb_ref
):
    gain = gain_ref[...]
    cum = jnp.zeros((NBLK, HD), F32)
    for r in range(BLK):
        step = decay_ref[pl.ds(r, NBLK, stride=BLK), :]
        cum = cum + step
        w_ref[r] = jnp.exp(cum) * (gain * jnp.sqrt(one_less_exp(2.0 * step)))
        fall_ref[r] = jnp.exp(-cum)
    fade_ref[...] = jnp.exp(-cum)
    total_ref[...] = jnp.sum(cum, axis=0, keepdims=True)
    z = cmul((coef_ref[2], coef_ref[3]), (coef_ref[0], coef_ref[1]))
    cb_ref[0], cb_ref[1] = z
    rot = (cos_ref[0], sin_ref[0])
    for lag in range(BLK):
        kern_ref[pl.ds(lag, 1), :] = jnp.sum(z[0], axis=0, keepdims=True)
        z = cmul(z, rot)


def tables(decay, gain, mode_coeffs, cos, sin):
    width = decay.shape[1]
    tokens = pl.BlockSpec((ROWS, HD), lambda h: (0, h))
    cube = pl.BlockSpec((BLK, NBLK, HD), lambda h: (0, 0, h))
    flat = pl.BlockSpec((NBLK, HD), lambda h: (0, h))
    line = pl.BlockSpec((1, HD), lambda h: (0, h))
    return pl.pallas_call(
        tables_kernel,
        grid=(width // HD,),
        in_specs=[
            tokens,
            line,
            pl.BlockSpec((4, MODES, HD), lambda h: (0, 0, h)),
            pl.BlockSpec((1, MODES, HD), lambda h: (0, 0, h)),
            pl.BlockSpec((1, MODES, HD), lambda h: (0, 0, h)),
        ],
        out_specs=[cube, cube, flat, flat, line, pl.BlockSpec((2, MODES, HD), lambda h: (0, 0, h))],
        out_shape=[
            jax.ShapeDtypeStruct((BLK, NBLK, width), F32),
            jax.ShapeDtypeStruct((BLK, NBLK, width), F32),
            jax.ShapeDtypeStruct((NBLK, width), F32),
            jax.ShapeDtypeStruct((BLK, width), F32),
            jax.ShapeDtypeStruct((1, width), F32),
            jax.ShapeDtypeStruct((2, MODES, width), F32),
        ],
        compiler_params=pltpu.CompilerParams(vmem_limit_bytes=16 * 2**20),
        cost_estimate=pl.CostEstimate(flops=4_000_000, bytes_accessed=3_000_000, transcendentals=400_000),
        name="tables",
    )(decay, gain, mode_coeffs, cos, sin)


def chain_step(state, rot16, fade_row, end):
    turned = cmul(state, rot16)
    return (fade_row * turned[0] + end[0], fade_row * turned[1] + end[1])


def ends_kernel(
    attn_ref, w_ref, ssq_ref, cos_ref, sin_ref, fade_ref, total_ref, g_ref, end_re, end_im, sum_ref, flat, scale
):
    heads = attn_ref.shape[1] // HD
    row_scale = lax.rsqrt(ssq_ref[...] * (1.0 / EMBED_DIMENSION) + 1e-06)
    scale[...] = jnp.transpose(jnp.broadcast_to(row_scale, (HD, ROWS)))
    group = 4
    for tile in range(heads):
        lanes = pl.ds(tile * HD, HD)
        flat[tile] = attn_ref[:, lanes].astype(F32)
        for r in range(BLK):
            tokens = pl.ds(r, NBLK, stride=BLK)
            g_ref[r, :, lanes] = flat[tile, tokens, :] * w_ref[r, :, lanes] * scale[tokens, :]
        fade = fade_ref[:, lanes]
        for base in range(0, MODES, group):
            modes = range(base, base + group)
            cos = [cos_ref[0, pl.ds(m, 1), lanes] for m in modes]
            twice = [jnp.broadcast_to(2.0 * c, (NBLK, HD)) for c in cos]
            first = g_ref[0, :, lanes]
            older = [first] * group
            second = g_ref[1, :, lanes]
            newer = [twice[i] * first + second for i in range(group)]
            for r in range(2, BLK):
                term = g_ref[r, :, lanes]
                for i in range(group):
                    older[i], newer[i] = newer[i], twice[i] * newer[i] + (term - older[i])
            for i, m in enumerate(modes):
                sin = sin_ref[0, pl.ds(m, 1), lanes]
                end_re[tile, pl.ds(m * NBLK, NBLK), :] = fade * (newer[i] - cos[i] * older[i])
                end_im[tile, pl.ds(m * NBLK, NBLK), :] = fade * (sin * older[i])
    states = [None] * heads
    for j in range(NBLK):
        at = pl.ds(j, MODES, stride=NBLK)
        for tile in range(heads):
            lanes = pl.ds(tile * HD, HD)
            end = (end_re[tile, at, :], end_im[tile, at, :])
            if j == 0:
                states[tile] = end
            else:
                rot16 = (cos_ref[1, :, lanes], sin_ref[1, :, lanes])
                states[tile] = chain_step(states[tile], rot16, fade_ref[pl.ds(j, 1), lanes], end)
    for tile in range(heads):
        lanes = pl.ds(tile * HD, HD)
        sum_ref[pl.ds(tile * 2 * MODES, MODES), :] = states[tile][0]
        sum_ref[pl.ds(tile * 2 * MODES + MODES, MODES), :] = states[tile][1]
        sum_ref[pl.ds(heads * 2 * MODES + tile, 1), :] = total_ref[:, lanes]
    used = heads * (2 * MODES + 1)
    sum_ref[pl.ds(used, sum_ref.shape[0] - used), :] = jnp.zeros((sum_ref.shape[0] - used, HD), F32)


def padded(rows):
    return -(-rows // 8) * 8


def block_ends(attn, w, ssq, cos, sin, fade, total):
    width = attn.shape[1]
    tiles = width // HD
    return pl.pallas_call(
        ends_kernel,
        out_shape=[
            jax.ShapeDtypeStruct((BLK, NBLK, width), F32),
            jax.ShapeDtypeStruct((tiles, MODES * NBLK, HD), F32),
            jax.ShapeDtypeStruct((tiles, MODES * NBLK, HD), F32),
            jax.ShapeDtypeStruct((padded(tiles * (2 * MODES + 1)), HD), F32),
        ],
        scratch_shapes=[pltpu.VMEM((tiles, ROWS, HD), F32), pltpu.VMEM((ROWS, HD), F32)],
        compiler_params=pltpu.CompilerParams(vmem_limit_bytes=20 * 2**20),
        cost_estimate=pl.CostEstimate(flops=8_000_000, bytes_accessed=4_000_000, transcendentals=0),
        name="block_ends",
    )(attn, w, ssq, cos, sin, fade, total)


def local_kernel(g_ref, kern_ref, out_ref):
    heads = g_ref.shape[2] // HD
    for tile in range(heads):
        lanes = pl.ds(tile * HD, HD)
        g = [g_ref[r, :, lanes] for r in range(BLK)]
        total = [None] * BLK
        for lag in range(BLK):
            k = jnp.broadcast_to(kern_ref[pl.ds(lag, 1), lanes], (NBLK, HD))
            for r in range(lag, BLK):
                term = k * g[r - lag]
                total[r] = term if total[r] is None else total[r] + term
        for r in range(BLK):
            out_ref[r, :, lanes] = total[r]


def local_part(g, kern):
    return pl.pallas_call(
        local_kernel,
        out_shape=jax.ShapeDtypeStruct(g.shape, F32),
        compiler_params=pltpu.CompilerParams(vmem_limit_bytes=20 * 2**20),
        cost_estimate=pl.CostEstimate(flops=3_000_000, bytes_accessed=1_300_000, transcendentals=0),
        name="local_part",
    )(g, kern)


def chip_kernel(pos_ref, own_ref, other_ref, cos_ref, sin_ref, out_ref):
    tiles = cos_ref.shape[2] // HD
    core = pos_ref[3]
    first_core = core == 0
    half = pl.multiple_of(core * HALF, HALF)
    for tile in range(tiles):
        lanes = pl.ds(tile * HD, HD)
        rows = [pl.ds(pl.multiple_of(tile * 2 * MODES + i * MODES + half, HALF), HALF) for i in (0, 1)]
        own = [own_ref[at, :] for at in rows]
        other = [other_ref[at, :] for at in rows]
        at = pl.ds(tiles * 2 * MODES + tile, 1)
        own_decay, other_decay = own_ref[at, :], other_ref[at, :]
        fade = jnp.exp(-jnp.where(first_core, other_decay, own_decay))
        turn = [fade * ref[2, pl.ds(half, HALF), lanes] for ref in (cos_ref, sin_ref)]
        first = [jnp.where(first_core, own[i], other[i]) for i in (0, 1)]
        second = [jnp.where(first_core, other[i], own[i]) for i in (0, 1)]
        moved = cmul(first, turn)
        out_ref[pl.ds(tile * MODES, HALF), :] = moved[0] + second[0]
        out_ref[pl.ds(tile * MODES + HALF, HALF), :] = moved[1] + second[1]
        out_ref[pl.ds(tiles * MODES + tile, 1), :] = own_decay + other_decay
    used = tiles * (MODES + 1)
    out_ref[pl.ds(used, out_ref.shape[0] - used), :] = jnp.zeros((out_ref.shape[0] - used, HD), F32)


def chip_sum(pos, own, other, cos, sin):
    tiles = cos.shape[2] // HD
    return pl.pallas_call(
        chip_kernel,
        in_specs=[pl.BlockSpec(memory_space=pltpu.SMEM)] + [pl.BlockSpec()] * 4,
        out_shape=jax.ShapeDtypeStruct((padded(tiles * (MODES + 1)), HD), F32),
        compiler_params=pltpu.CompilerParams(vmem_limit_bytes=4 * 2**20),
        cost_estimate=pl.CostEstimate(flops=100_000, bytes_accessed=300_000, transcendentals=640),
        name="chip_sum",
    )(pos, own, other, cos, sin)


def half_of(ref, tile):
    return (ref[pl.ds(tile * MODES, HALF), :], ref[pl.ds(tile * MODES + HALF, HALF), :])


def chip_turns(cos_ref, sin_ref, half, lanes, turn_ref):
    turn_ref[0, 0] = jnp.ones((HALF, HD), F32)
    turn_ref[0, 1] = jnp.zeros((HALF, HD), F32)
    one = (cos_ref[3, half, lanes], sin_ref[3, half, lanes])
    two = (cos_ref[4, half, lanes], sin_ref[4, half, lanes])
    for at, value in ((1, one), (2, two), (3, cmul(one, two))):
        turn_ref[at, 0], turn_ref[at, 1] = value


def row_kernel(pos_ref, c0, c1, c2, c3, cos_ref, sin_ref, row_ref, in_ref, before_ref, turn_ref):
    tiles = in_ref.shape[0] // MODES
    chips = (c0, c1, c2, c3)
    x = pos_ref[4]
    place = [jnp.where(x >= s, x - s, x - s + NX) for s in range(NX)]
    half = pl.ds(pl.multiple_of(pos_ref[3] * HALF, HALF), HALF)
    for tile in range(tiles):
        lanes = pl.ds(tile * HD, HD)
        chip_turns(cos_ref, sin_ref, half, lanes, turn_ref)
        at = pl.ds(tiles * MODES + tile, 1)
        decay = [c[at, :] for c in chips]
        value = [half_of(c, tile) for c in chips]
        row = [jnp.zeros((HALF, HD), F32)] * 2
        into = [jnp.zeros((HALF, HD), F32)] * 2
        for s in range(NX):
            after = jnp.zeros((1, HD), F32)
            for k in range(NX):
                if k != s:
                    after = after + jnp.where(place[k] > place[s], decay[k], 0.0)
            fade = jnp.exp(-after)
            left = NX - 1 - place[s]
            part = cmul(value[s], [fade * turn_ref[left, i] for i in (0, 1)])
            row = [row[i] + part[i] for i in (0, 1)]
            if s:
                turn = [turn_ref[s - 1, i] for i in (0, 1)]
                if s > 1:
                    fade = jnp.exp(-functools.reduce(jnp.add, decay[1:s]))
                    turn = [fade * t for t in turn]
                part = cmul(value[s], turn)
                into = [into[i] + jnp.where(x >= s, part[i], 0.0) for i in (0, 1)]
        row_ref[pl.ds(tile * MODES, HALF), :] = row[0]
        row_ref[pl.ds(tile * MODES + HALF, HALF), :] = row[1]
        row_ref[at, :] = functools.reduce(jnp.add, decay)
        in_ref[pl.ds(tile * MODES, HALF), :] = into[0]
        in_ref[pl.ds(tile * MODES + HALF, HALF), :] = into[1]
        before = jnp.zeros((1, HD), F32)
        for s in range(1, NX):
            before = before + jnp.where(x >= s, decay[s], 0.0)
        before_ref[:, lanes] = before
    used = tiles * (MODES + 1)
    row_ref[pl.ds(used, row_ref.shape[0] - used), :] = jnp.zeros((row_ref.shape[0] - used, HD), F32)


def row_sum(pos, chips, cos, sin):
    width = cos.shape[2]
    tiles = width // HD
    return pl.pallas_call(
        row_kernel,
        in_specs=[pl.BlockSpec(memory_space=pltpu.SMEM)] + [pl.BlockSpec()] * 6,
        out_shape=[
            jax.ShapeDtypeStruct((padded(tiles * (MODES + 1)), HD), F32),
            jax.ShapeDtypeStruct((tiles * MODES, HD), F32),
            jax.ShapeDtypeStruct((1, width), F32),
        ],
        scratch_shapes=[pltpu.VMEM((NX, 2, HALF, HD), F32)],
        compiler_params=pltpu.CompilerParams(vmem_limit_bytes=4 * 2**20),
        cost_estimate=pl.CostEstimate(flops=300_000, bytes_accessed=400_000, transcendentals=5000),
        name="row_sum",
    )(pos, *chips, cos, sin)


def entry_kernel(pos_ref, r1, r2, r3, in_ref, before_ref, cos_ref, sin_ref, out_ref, turn_ref):
    tiles = in_ref.shape[0] // MODES
    x = pos_ref[4]
    half = pl.ds(pl.multiple_of(pos_ref[3] * HALF, HALF), HALF)
    for tile in range(tiles):
        lanes = pl.ds(tile * HD, HD)
        chip_turns(cos_ref, sin_ref, half, lanes, turn_ref)
        at = pl.ds(tiles * MODES + tile, 1)
        fade = jnp.exp(-r1[at, :])
        row = half_of(r1, tile)
        part = cmul(half_of(r2, tile), [fade * ref[5, half, lanes] for ref in (cos_ref, sin_ref)])
        row = [row[i] + part[i] for i in (0, 1)]
        fade = jnp.exp(-(r1[at, :] + r2[at, :]))
        part = cmul(half_of(r3, tile), [fade * ref[6, half, lanes] for ref in (cos_ref, sin_ref)])
        row = [row[i] + part[i] for i in (0, 1)]
        fade = jnp.exp(-before_ref[:, lanes])
        part = cmul(row, [fade * turn_ref[x, i] for i in (0, 1)])
        into = half_of(in_ref, tile)
        out_ref[pl.ds(tile * MODES, HALF), :] = part[0] + into[0]
        out_ref[pl.ds(tile * MODES + HALF, HALF), :] = part[1] + into[1]


def chip_entry(pos, rows, into, before, cos, sin):
    return pl.pallas_call(
        entry_kernel,
        in_specs=[pl.BlockSpec(memory_space=pltpu.SMEM)] + [pl.BlockSpec()] * 7,
        out_shape=jax.ShapeDtypeStruct(into.shape, F32),
        scratch_shapes=[pltpu.VMEM((NX, 2, HALF, HD), F32)],
        compiler_params=pltpu.CompilerParams(vmem_limit_bytes=4 * 2**20),
        cost_estimate=pl.CostEstimate(flops=300_000, bytes_accessed=400_000, transcendentals=5000),
        name="chip_entry",
    )(pos, *rows, into, before, cos, sin)


def finish_kernel(
    pos_ref, mine_ref, theirs_ref, other_ref, end_re, end_im, local_ref, fall_ref, fade_ref, cos_ref, sin_ref,
    cb_ref, rec_ref, st_re, st_im, acc, out
):
    heads = rec_ref.shape[1] // HD
    first_core = pos_ref[3] == 0
    states = []
    for tile in range(heads):
        lanes = pl.ds(tile * HD, HD)
        mine, theirs = half_of(mine_ref, tile), half_of(theirs_ref, tile)
        at_chip = [
            jnp.concatenate(
                [jnp.where(first_core, mine[i], theirs[i]), jnp.where(first_core, theirs[i], mine[i])], axis=0
            )
            for i in (0, 1)
        ]
        fade = jnp.exp(-other_ref[pl.ds(heads * 2 * MODES + tile, 1), :])
        moved = cmul(at_chip, [fade * ref[2, :, lanes] for ref in (cos_ref, sin_ref)])
        other = [other_ref[pl.ds(tile * 2 * MODES + i * MODES, MODES), :] for i in (0, 1)]
        states.append(tuple(jnp.where(first_core, at_chip[i], moved[i] + other[i]) for i in (0, 1)))
    for j in range(NBLK):
        at = pl.ds(j, MODES, stride=NBLK)
        for tile in range(heads):
            lanes = pl.ds(tile * HD, HD)
            st_re[tile, at, :] = states[tile][0]
            st_im[tile, at, :] = states[tile][1]
            if j + 1 < NBLK:
                rot16 = (cos_ref[1, :, lanes], sin_ref[1, :, lanes])
                end = (end_re[tile, at, :], end_im[tile, at, :])
                states[tile] = chain_step(states[tile], rot16, fade_ref[pl.ds(j, 1), lanes], end)
    group = 8
    for tile in range(heads):
        lanes = pl.ds(tile * HD, HD)
        for base in range(0, MODES, group):
            older, newer, twice = [], [], []
            for m in range(base, base + group):
                at = pl.ds(m * NBLK, NBLK)
                own = pl.ds(m, 1)
                z = cmul((st_re[tile, at, :], st_im[tile, at, :]), (cb_ref[0, own, lanes], cb_ref[1, own, lanes]))
                cos = cos_ref[0, own, lanes]
                older.append(z[0])
                newer.append(cos * z[0] - sin_ref[0, own, lanes] * z[1])
                twice.append(jnp.broadcast_to(2.0 * cos, (NBLK, HD)))
            for r in range(BLK):
                if r > 0:
                    for i in range(group):
                        older[i], newer[i] = newer[i], twice[i] * newer[i] - older[i]
                total = functools.reduce(jnp.add, newer)
                if base == 0:
                    acc[r] = local_ref[r, :, lanes] + total
                else:
                    out[tile, pl.ds(r, NBLK, stride=BLK), :] = (acc[r] + total) * fall_ref[r, :, lanes]
        rec_ref[:, lanes] = out[tile]


def finish(pos, mine, theirs, other, end_re, end_im, local, fall, fade, cos, sin, cb):
    width = fall.shape[2]
    tiles = width // HD
    return pl.pallas_call(
        finish_kernel,
        in_specs=[pl.BlockSpec(memory_space=pltpu.SMEM)] + [pl.BlockSpec()] * 11,
        out_shape=jax.ShapeDtypeStruct((ROWS, width), F32),
        scratch_shapes=[
            pltpu.VMEM((tiles, MODES * NBLK, HD), F32),
            pltpu.VMEM((tiles, MODES * NBLK, HD), F32),
            pltpu.VMEM((BLK, NBLK, HD), F32),
            pltpu.VMEM((tiles, ROWS, HD), F32),
        ],
        compiler_params=pltpu.CompilerParams(vmem_limit_bytes=20 * 2**20),
        cost_estimate=pl.CostEstimate(flops=8_000_000, bytes_accessed=5_000_000, transcendentals=0),
        name="finish",
    )(pos, mine, theirs, other, end_re, end_im, local, fall, fade, cos, sin, cb)


def shards(queries, keys, values, decay, gain, theta, mode_coeffs):
    width = queries.shape[1]
    me = lax.axis_index("seq")
    core = me % 2
    chip = me // 2
    x = chip % NX

    own = jnp.stack([keys, values])
    sh2 = lax.ppermute(own, "seq", chip_pairs(0, 1))
    hop = lax.ppermute(own, "seq", ring_x_pairs(-1, (0,)))
    up = lax.ppermute(own, "seq", CORE_UP)
    angles = jnp.asarray(TURNS, F32)[:, None, None] * theta[None]
    cos, sin = jnp.cos(angles), jnp.sin(angles)
    made = tables(decay, gain[None, :], mode_coeffs, cos, sin)
    sh2, made, cos, sin = lax.optimization_barrier((sh2, made, cos, sin))
    w, fall, fade, kern, total, cb = made
    far1 = lax.ppermute(sh2, "seq", chip_pairs(0, 1, (1,)))
    swapped = lax.ppermute(sh2, "seq", CORE_SWAP)
    far0 = lax.ppermute(hop, "seq", two_back_second_hop())
    pos = jnp.stack(
        [
            (me >= 2).astype(jnp.int32),
            (me >= 4).astype(jnp.int32),
            ((me >= 3) | (core == 1)).astype(jnp.int32),
            core.astype(jnp.int32),
            x.astype(jnp.int32),
        ]
    )
    near = attention_near(pos, queries, own, sh2, swapped)
    far1, near = lax.optimization_barrier((far1, near))
    down = lax.ppermute(far1, "seq", CORE_DOWN)
    sh4 = jnp.where(core == 0, far0, far1)
    attn, ssq = attention_far(pos, queries, sh4, up, down, near)

    ring = lambda step: [(i, (i + step) % NZ) for i in range(NZ)]
    before = lax.ppermute(ssq, "mp", ring(1))
    after = lax.ppermute(ssq, "mp", ring(-1))
    three = before + ssq + after
    two = ssq + after
    ssq_all = three + lax.ppermute(three, "mp", ring(-3)) + lax.ppermute(two, "mp", ring(3))

    g, end_re, end_im, dev_sum = block_ends(attn, w, ssq_all, cos, sin, fade, total)
    local = local_part(g, kern)

    other = lax.ppermute(dev_sum, "seq", CORE_SWAP)
    packed = chip_sum(pos, dev_sum, other, cos, sin)
    chips = [packed] + [lax.ppermute(packed, "seq", ring_x_pairs(step)) for step in (1, 2, 3)]
    row, into, before_row = row_sum(pos, chips, cos, sin)
    rows = [lax.ppermute(row, "seq", shift_y_pairs(step)) for step in (1, 2, 3)]
    mine = chip_entry(pos, rows, into, before_row, cos, sin)
    theirs = lax.ppermute(mine, "seq", CORE_SWAP)

    rec = finish(pos, mine, theirs, other, end_re, end_im, local, fall, fade, cos, sin, cb)
    return (attn, rec)


def solution(mesh):
    placed = (
        P("seq", "mp"),
        P("seq", "mp"),
        P("seq", "mp"),
        P("seq", "mp"),
        P("mp"),
        P(None, "mp"),
        P(None, None, "mp"),
    )
    return jax.shard_map(
        shards,
        mesh=mesh,
        in_specs=placed,
        out_specs=(P("seq", "mp"), P("seq", "mp")),
        check_vma=False,
    )
```

```python
import functools
import math

import jax
import jax.numpy as jnp
from jax import lax
from jax.experimental import pallas as pl
from jax.experimental.pallas import tpu as pltpu
from jax.sharding import PartitionSpec as P

HD = 128
EMBED_DIMENSION = 5120
MODES = 16
HALF = MODES // 2
ROWS = 256
BLK = 16
NBLK = ROWS // BLK
NX = 4
NY = 4
NZ = 8
SEQ = 32
NEG = -1e30
SCALE2 = math.log2(math.e) / math.sqrt(HD)
F32 = jnp.float32
TURNS = (1, BLK, ROWS, 2 * ROWS, 4 * ROWS, 8 * ROWS)


def device_of(y, x, core):
    return (y * NX + x) * 2 + core


def chip_pairs(dy, dx, cores=(0, 1)):
    pairs = []
    for chip in range(NX * NY):
        target = chip + dy * NX + dx
        if 0 <= target < NX * NY:
            pairs += [(chip * 2 + c, target * 2 + c) for c in cores]
    return pairs


def ring_x_pairs(step, cores=(0, 1)):
    return [
        (device_of(y, x, c), device_of(y, (x + step) % NX, c))
        for y in range(NY)
        for x in range(NX)
        for c in cores
    ]


def two_back_second_hop():
    pairs = []
    for chip in range(NX * NY):
        y, x = divmod(chip, NX)
        if chip + 2 < NX * NY:
            pairs.append((device_of(y, (x - 1) % NX, 0), (chip + 2) * 2))
    return pairs


CORE_SWAP = [(d, d ^ 1) for d in range(SEQ)]
CORE_UP = [(d, d + 1) for d in range(0, SEQ, 2)]
CORE_DOWN = [(d + 1, d) for d in range(0, SEQ, 2)]


def cmul(a, b):
    return (a[0] * b[0] - a[1] * b[1], a[0] * b[1] + a[1] * b[0])


def masks():
    row = lax.broadcasted_iota(jnp.int32, (ROWS, ROWS), 0)
    col = lax.broadcasted_iota(jnp.int32, (ROWS, ROWS), 1)
    return row, col


def scores_of(q, k):
    return lax.dot_general(q, k, (((1,), (1,)), ((), ())), preferred_element_type=F32)


def softmax_parts(parts, vals, top):
    weights = [jnp.exp2((s - top) * SCALE2) for s in parts]
    total = jnp.sum(functools.reduce(jnp.add, weights), axis=1, keepdims=True)
    mixed = [jnp.dot(w.astype(jnp.bfloat16), v, preferred_element_type=F32) for w, v in zip(weights, vals)]
    return total, functools.reduce(jnp.add, mixed)


def own_kernel(q_ref, own_ref, up_ref, top_ref, total_ref, mixed_ref):
    row, col = masks()
    for head in range(q_ref.shape[1] // HD):
        lanes = pl.ds(head * HD, HD)
        part = jnp.where(col <= row, scores_of(q_ref[:, lanes], own_ref[0, :, lanes]), NEG)
        top = jnp.max(part, axis=1, keepdims=True)
        total, mixed = softmax_parts([part], [own_ref[1, :, lanes]], top)
        top_ref[:, lanes] = jnp.broadcast_to(top, (ROWS, HD))
        total_ref[:, lanes] = jnp.broadcast_to(total, (ROWS, HD))
        mixed_ref[:, lanes] = mixed


def next_kernel(
    pos_ref, q_ref, two_ref, swap_ref, top_in, total_in, mixed_in, top_ref, total_ref, mixed_ref, mark_ref
):
    there = pos_ref[0] == 1
    for head in range(q_ref.shape[1] // HD):
        lanes = pl.ds(head * HD, HD)
        q = q_ref[:, lanes]
        parts = [jnp.where(there, scores_of(q, ref[0, :, lanes]), NEG) for ref in (two_ref, swap_ref)]
        old = top_in[:, lanes]
        top = jnp.maximum(old[:, :1], jnp.max(jnp.maximum(*parts), axis=1, keepdims=True))
        total, mixed = softmax_parts(parts, [ref[1, :, lanes] for ref in (two_ref, swap_ref)], top)
        shrink = jnp.exp2((old - top) * SCALE2)
        top_ref[:, lanes] = jnp.broadcast_to(top, (ROWS, HD))
        total_ref[:, lanes] = total_in[:, lanes] * shrink + total
        mixed_ref[:, lanes] = mixed_in[:, lanes] * shrink + mixed
    mark_ref[...] = jnp.zeros(mark_ref.shape, F32)


def pick_kernel(pos_ref, hop_ref, two_ref, out_ref):
    @pl.when(pos_ref[3] == 0)
    def _():
        out_ref[...] = hop_ref[...]

    @pl.when(pos_ref[3] != 0)
    def _():
        out_ref[...] = two_ref[...]


def far_kernel(
    pos_ref, q_ref, far_ref, up_ref, down_ref, top_ref, total_ref, mixed_ref, mark_ref, o_ref, wide_ref, ssq_ref
):
    row, col = masks()
    first_core = pos_ref[3] == 0
    there = pos_ref[2] == 1
    low = row - jnp.where(pos_ref[1] == 1, 0, -2 * ROWS)
    square = None
    for head in range(q_ref.shape[1] // HD):
        lanes = pl.ds(head * HD, HD)
        q = q_ref[:, lanes]
        last = [far_ref[i, :, lanes] for i in (0, 1)]
        side = [jnp.where(first_core, down_ref[i, :, lanes], up_ref[i, :, lanes]) for i in (0, 1)]
        parts = [
            jnp.where(col > low, scores_of(q, last[0]), NEG),
            jnp.where(there, scores_of(q, side[0]), NEG),
        ]
        old = top_ref[:, lanes]
        top = jnp.maximum(old[:, :1], jnp.max(jnp.maximum(*parts), axis=1, keepdims=True))
        total, mixed = softmax_parts(parts, (last[1], side[1]), top)
        shrink = jnp.exp2((old - top) * SCALE2)
        total = total_ref[:, lanes] * shrink + total
        out = ((mixed_ref[:, lanes] * shrink + mixed) / total).astype(jnp.bfloat16)
        o_ref[:, lanes] = out
        wide = out.astype(F32)
        wide_ref[head] = wide
        square = wide * wide if square is None else square + wide * wide
    ssq_ref[...] = jnp.sum(jnp.transpose(square), axis=0, keepdims=True)


def attention_own(queries, own, up):
    wide = jax.ShapeDtypeStruct(queries.shape, F32)
    return pl.pallas_call(
        own_kernel,
        in_specs=[pl.BlockSpec()] * 2 + [pl.BlockSpec(memory_space=pl.ANY)],
        out_shape=[wide, wide, wide],
        compiler_params=pltpu.CompilerParams(vmem_limit_bytes=24 * 2**20),
        cost_estimate=pl.CostEstimate(flops=170_000_000, bytes_accessed=3_000_000, transcendentals=330_000),
        name="attention_own",
    )(queries, own, up)


def attention_next(pos, queries, sh2, swapped, top, total, mixed):
    wide = jax.ShapeDtypeStruct(queries.shape, F32)
    return pl.pallas_call(
        next_kernel,
        in_specs=[pl.BlockSpec(memory_space=pltpu.SMEM)] + [pl.BlockSpec()] * 6,
        out_shape=[wide, wide, wide, jax.ShapeDtypeStruct((8, HD), F32)],
        compiler_params=pltpu.CompilerParams(vmem_limit_bytes=24 * 2**20),
        cost_estimate=pl.CostEstimate(flops=340_000_000, bytes_accessed=5_000_000, transcendentals=650_000),
        name="attention_next",
    )(pos, queries, sh2, swapped, top, total, mixed)


def pick(pos, hop, sh2):
    return pl.pallas_call(
        pick_kernel,
        in_specs=[pl.BlockSpec(memory_space=pltpu.SMEM)] + [pl.BlockSpec()] * 2,
        out_shape=jax.ShapeDtypeStruct(hop.shape, hop.dtype),
        compiler_params=pltpu.CompilerParams(vmem_limit_bytes=4 * 2**20),
        cost_estimate=pl.CostEstimate(flops=0, bytes_accessed=1_300_000, transcendentals=0),
        name="pick",
    )(pos, hop, sh2)


def attention_far(pos, queries, far, up, down, top, total, mixed, mark):
    return pl.pallas_call(
        far_kernel,
        in_specs=[pl.BlockSpec(memory_space=pltpu.SMEM)] + [pl.BlockSpec()] * 8,
        out_shape=[
            jax.ShapeDtypeStruct(queries.shape, jnp.bfloat16),
            jax.ShapeDtypeStruct((queries.shape[1] // HD, ROWS, HD), F32),
            jax.ShapeDtypeStruct((1, ROWS), F32),
        ],
        compiler_params=pltpu.CompilerParams(vmem_limit_bytes=24 * 2**20),
        cost_estimate=pl.CostEstimate(flops=340_000_000, bytes_accessed=5_000_000, transcendentals=650_000),
        name="attention_far",
    )(pos, queries, far, up, down, top, total, mixed, mark)


def one_less_exp(v):
    series = 1.0 / 720.0
    for order in (120.0, 24.0, 6.0, 2.0, 1.0):
        series = 1.0 / order - v * series
    return jnp.where(v < 0.25, v * series, 1.0 - jnp.exp(-v))


def tables_kernel(
    decay_ref, gain_ref, coef_ref, cos_ref, sin_ref, w_ref, fall_ref, fade_ref, kern_ref, total_ref, cb_ref, pass_re,
    pass_im
):
    gain = gain_ref[...]
    cum = jnp.zeros((NBLK, HD), F32)
    for r in range(BLK):
        step = decay_ref[pl.ds(r, NBLK, stride=BLK), :]
        cum = cum + step
        w_ref[r] = jnp.exp(cum) * (gain * jnp.sqrt(one_less_exp(2.0 * step)))
        fall_ref[r] = jnp.exp(-cum)
    fade_ref[...] = jnp.exp(-cum)
    total_ref[...] = jnp.sum(cum, axis=0, keepdims=True)
    z = cmul((coef_ref[2], coef_ref[3]), (coef_ref[0], coef_ref[1]))
    cb_ref[0], cb_ref[1] = z
    rot = (cos_ref[0], sin_ref[0])
    for lag in range(BLK):
        kern_ref[pl.ds(lag, 1), :] = jnp.sum(z[0], axis=0, keepdims=True)
        z = cmul(z, rot)
    moved = (jnp.ones((MODES, HD), F32), jnp.zeros((MODES, HD), F32))
    rot16 = (cos_ref[1], sin_ref[1])
    for j in range(NBLK):
        at = pl.ds(j, MODES, stride=NBLK)
        pass_re[0, at, :] = moved[0]
        pass_im[0, at, :] = moved[1]
        fade = fade_ref[pl.ds(j, 1), :]
        moved = tuple(fade * part for part in cmul(moved, rot16))


def tables(decay, gain, mode_coeffs, cos, sin):
    width = decay.shape[1]
    tokens = pl.BlockSpec((ROWS, HD), lambda h: (0, h))
    cube = pl.BlockSpec((BLK, NBLK, HD), lambda h: (0, 0, h))
    flat = pl.BlockSpec((NBLK, HD), lambda h: (0, h))
    line = pl.BlockSpec((1, HD), lambda h: (0, h))
    deep = pl.BlockSpec((1, MODES * NBLK, HD), lambda h: (h, 0, 0))
    return pl.pallas_call(
        tables_kernel,
        grid=(width // HD,),
        in_specs=[
            tokens,
            line,
            pl.BlockSpec((4, MODES, HD), lambda h: (0, 0, h)),
            pl.BlockSpec((2, MODES, HD), lambda h: (0, 0, h)),
            pl.BlockSpec((2, MODES, HD), lambda h: (0, 0, h)),
        ],
        out_specs=[cube, cube, flat, flat, line, pl.BlockSpec((2, MODES, HD), lambda h: (0, 0, h)), deep, deep],
        out_shape=[
            jax.ShapeDtypeStruct((BLK, NBLK, width), F32),
            jax.ShapeDtypeStruct((BLK, NBLK, width), F32),
            jax.ShapeDtypeStruct((NBLK, width), F32),
            jax.ShapeDtypeStruct((BLK, width), F32),
            jax.ShapeDtypeStruct((1, width), F32),
            jax.ShapeDtypeStruct((2, MODES, width), F32),
            jax.ShapeDtypeStruct((width // HD, MODES * NBLK, HD), F32),
            jax.ShapeDtypeStruct((width // HD, MODES * NBLK, HD), F32),
        ],
        compiler_params=pltpu.CompilerParams(vmem_limit_bytes=16 * 2**20),
        cost_estimate=pl.CostEstimate(flops=4000000, bytes_accessed=4000000, transcendentals=0),
        name="tables",
    )(decay, gain, mode_coeffs, cos, sin)


def chain_step(state, rot16, fade_row, end):
    turned = cmul(state, rot16)
    return (fade_row * turned[0] + end[0], fade_row * turned[1] + end[1])


def ends_kernel(
    wide_ref, w_ref, ssq_ref, cos_ref, sin_ref, fade_ref, total_ref, cb_ref, g_ref, st_re, st_im, sum_ref, scale, end_re,
    end_im
):
    heads = wide_ref.shape[0]
    row_scale = lax.rsqrt(jnp.sum(ssq_ref[...], axis=0, keepdims=True) * (1.0 / EMBED_DIMENSION) + 1e-06)
    scale[...] = jnp.transpose(jnp.broadcast_to(row_scale, (HD, ROWS)))
    group = 4
    for tile in range(heads):
        lanes = pl.ds(tile * HD, HD)
        for r in range(BLK):
            tokens = pl.ds(r, NBLK, stride=BLK)
            g_ref[r, :, lanes] = wide_ref[tile, tokens, :] * w_ref[r, :, lanes] * scale[tokens, :]
        fade = fade_ref[:, lanes]
        for base in range(0, MODES, group):
            modes = range(base, base + group)
            cos = [cos_ref[0, pl.ds(m, 1), lanes] for m in modes]
            twice = [jnp.broadcast_to(2.0 * c, (NBLK, HD)) for c in cos]
            first = g_ref[0, :, lanes]
            older = [first] * group
            second = g_ref[1, :, lanes]
            newer = [twice[i] * first + second for i in range(group)]
            for r in range(2, BLK):
                term = g_ref[r, :, lanes]
                for i in range(group):
                    older[i], newer[i] = newer[i], twice[i] * newer[i] + (term - older[i])
            for i, m in enumerate(modes):
                sin = sin_ref[0, pl.ds(m, 1), lanes]
                end_re[tile, pl.ds(m * NBLK, NBLK), :] = fade * (newer[i] - cos[i] * older[i])
                end_im[tile, pl.ds(m * NBLK, NBLK), :] = fade * (sin * older[i])
    states = [None] * heads
    for j in range(NBLK):
        at = pl.ds(j, MODES, stride=NBLK)
        for tile in range(heads):
            lanes = pl.ds(tile * HD, HD)
            end = (end_re[tile, at, :], end_im[tile, at, :])
            if j == 0:
                st_re[tile, at, :] = jnp.zeros((MODES, HD), F32)
                st_im[tile, at, :] = jnp.zeros((MODES, HD), F32)
                states[tile] = end
            else:
                given = cmul(states[tile], (cb_ref[0, :, lanes], cb_ref[1, :, lanes]))
                st_re[tile, at, :] = given[0]
                st_im[tile, at, :] = given[1]
                rot16 = (cos_ref[1, :, lanes], sin_ref[1, :, lanes])
                states[tile] = chain_step(states[tile], rot16, fade_ref[pl.ds(j, 1), lanes], end)
    for tile in range(heads):
        lanes = pl.ds(tile * HD, HD)
        sum_ref[pl.ds(tile * 2 * MODES, MODES), :] = states[tile][0]
        sum_ref[pl.ds(tile * 2 * MODES + MODES, MODES), :] = states[tile][1]
        sum_ref[pl.ds(heads * 2 * MODES + tile, 1), :] = total_ref[:, lanes]
    used = heads * (2 * MODES + 1)
    sum_ref[pl.ds(used, sum_ref.shape[0] - used), :] = jnp.zeros((sum_ref.shape[0] - used, HD), F32)


def padded(rows):
    return -(-rows // 8) * 8


def block_ends(wide, w, ssq, cos, sin, fade, total, cb):
    width = w.shape[2]
    tiles = width // HD
    return pl.pallas_call(
        ends_kernel,
        out_shape=[
            jax.ShapeDtypeStruct((BLK, NBLK, width), F32),
            jax.ShapeDtypeStruct((tiles, MODES * NBLK, HD), F32),
            jax.ShapeDtypeStruct((tiles, MODES * NBLK, HD), F32),
            jax.ShapeDtypeStruct((padded(tiles * (2 * MODES + 1)), HD), F32),
        ],
        scratch_shapes=[pltpu.VMEM((ROWS, HD), F32)]
        + [pltpu.VMEM((tiles, MODES * NBLK, HD), F32)] * 2,
        compiler_params=pltpu.CompilerParams(vmem_limit_bytes=20 * 2**20),
        cost_estimate=pl.CostEstimate(flops=8_000_000, bytes_accessed=4_000_000, transcendentals=0),
        name="block_ends",
    )(wide, w, ssq, cos, sin, fade, total, cb)


def local_kernel(g_ref, kern_ref, out_ref):
    heads = g_ref.shape[2] // HD
    for tile in range(heads):
        lanes = pl.ds(tile * HD, HD)
        g = [g_ref[r, :, lanes] for r in range(BLK)]
        total = [None] * BLK
        for lag in range(BLK):
            k = jnp.broadcast_to(kern_ref[pl.ds(lag, 1), lanes], (NBLK, HD))
            for r in range(lag, BLK):
                term = k * g[r - lag]
                total[r] = term if total[r] is None else total[r] + term
        for r in range(BLK):
            out_ref[r, :, lanes] = total[r]


def local_part(g, kern):
    return pl.pallas_call(
        local_kernel,
        out_shape=jax.ShapeDtypeStruct(g.shape, F32),
        compiler_params=pltpu.CompilerParams(vmem_limit_bytes=20 * 2**20),
        cost_estimate=pl.CostEstimate(flops=3_000_000, bytes_accessed=1_300_000, transcendentals=0),
        name="local_part",
    )(g, kern)


def chip_kernel(pos_ref, own_ref, other_ref, cos_ref, sin_ref, out_ref):
    tiles = cos_ref.shape[2] // HD
    core = pos_ref[3]
    first_core = core == 0
    half = pl.multiple_of(core * HALF, HALF)
    for tile in range(tiles):
        lanes = pl.ds(tile * HD, HD)
        rows = [pl.ds(pl.multiple_of(tile * 2 * MODES + i * MODES + half, HALF), HALF) for i in (0, 1)]
        own = [own_ref[at, :] for at in rows]
        other = [other_ref[at, :] for at in rows]
        at = pl.ds(tiles * 2 * MODES + tile, 1)
        own_decay, other_decay = own_ref[at, :], other_ref[at, :]
        fade = jnp.exp(-jnp.where(first_core, other_decay, own_decay))
        turn = [fade * ref[2, pl.ds(half, HALF), lanes] for ref in (cos_ref, sin_ref)]
        first = [jnp.where(first_core, own[i], other[i]) for i in (0, 1)]
        second = [jnp.where(first_core, other[i], own[i]) for i in (0, 1)]
        moved = cmul(first, turn)
        out_ref[pl.ds(tile * MODES, HALF), :] = moved[0] + second[0]
        out_ref[pl.ds(tile * MODES + HALF, HALF), :] = moved[1] + second[1]
        out_ref[pl.ds(tiles * MODES + tile, 1), :] = own_decay + other_decay
    used = tiles * (MODES + 1)
    out_ref[pl.ds(used, out_ref.shape[0] - used), :] = jnp.zeros((out_ref.shape[0] - used, HD), F32)


def chip_sum(pos, own, other, cos, sin):
    tiles = cos.shape[2] // HD
    return pl.pallas_call(
        chip_kernel,
        in_specs=[pl.BlockSpec(memory_space=pltpu.SMEM)] + [pl.BlockSpec()] * 4,
        out_shape=jax.ShapeDtypeStruct((padded(tiles * (MODES + 1)), HD), F32),
        compiler_params=pltpu.CompilerParams(vmem_limit_bytes=4 * 2**20),
        cost_estimate=pl.CostEstimate(flops=100_000, bytes_accessed=300_000, transcendentals=640),
        name="chip_sum",
    )(pos, own, other, cos, sin)


def half_of(ref, tile):
    return (ref[pl.ds(tile * MODES, HALF), :], ref[pl.ds(tile * MODES + HALF, HALF), :])


def block_kernel(bit, place, pos_ref, own_ref, other_ref, cos_ref, sin_ref, out_ref):
    tiles = cos_ref.shape[2] // HD
    first_half = (pos_ref[4] // bit) % 2 == 0
    half = pl.ds(pl.multiple_of(pos_ref[3] * HALF, HALF), HALF)
    for tile in range(tiles):
        lanes = pl.ds(tile * HD, HD)
        at = pl.ds(tiles * MODES + tile, 1)
        own, other = half_of(own_ref, tile), half_of(other_ref, tile)
        fade = jnp.exp(-jnp.where(first_half, other_ref[at, :], own_ref[at, :]))
        first = [jnp.where(first_half, own[i], other[i]) for i in (0, 1)]
        second = [jnp.where(first_half, other[i], own[i]) for i in (0, 1)]
        moved = cmul(first, [fade * ref[place, half, lanes] for ref in (cos_ref, sin_ref)])
        out_ref[pl.ds(tile * MODES, HALF), :] = moved[0] + second[0]
        out_ref[pl.ds(tile * MODES + HALF, HALF), :] = moved[1] + second[1]
        out_ref[at, :] = own_ref[at, :] + other_ref[at, :]
    used = tiles * (MODES + 1)
    out_ref[pl.ds(used, out_ref.shape[0] - used), :] = jnp.zeros((out_ref.shape[0] - used, HD), F32)


def block_sum(level, pos, own, other, cos, sin):
    return pl.pallas_call(
        functools.partial(block_kernel, 1 << level, 3 + level),
        in_specs=[pl.BlockSpec(memory_space=pltpu.SMEM)] + [pl.BlockSpec()] * 4,
        out_shape=jax.ShapeDtypeStruct(own.shape, F32),
        compiler_params=pltpu.CompilerParams(vmem_limit_bytes=4 * 2**20),
        cost_estimate=pl.CostEstimate(flops=100_000, bytes_accessed=300_000, transcendentals=640),
        name="block_sum",
    )(pos, own, other, cos, sin)


def entry_kernel(pos_ref, b0, b1, b2, cos_ref, sin_ref, in_ref, turn_ref):
    tiles = in_ref.shape[0] // MODES
    chip = pos_ref[4]
    half = pl.ds(pl.multiple_of(pos_ref[3] * HALF, HALF), HALF)
    upper = [(chip // (1 << level)) % 2 == 1 for level in range(3)]
    for tile in range(tiles):
        lanes = pl.ds(tile * HD, HD)
        at = pl.ds(tiles * MODES + tile, 1)
        into = (jnp.zeros((HALF, HD), F32), jnp.zeros((HALF, HD), F32))
        turn = (jnp.ones((HALF, HD), F32), jnp.zeros((HALF, HD), F32))
        for level, block in enumerate((b0, b1, b2)):
            part = cmul(half_of(block, tile), turn)
            into = [into[i] + jnp.where(upper[level], part[i], 0.0) for i in (0, 1)]
            fade = jnp.exp(-block[at, :])
            longer = cmul(turn, [fade * ref[3 + level, half, lanes] for ref in (cos_ref, sin_ref)])
            turn = [jnp.where(upper[level], longer[i], turn[i]) for i in (0, 1)]
        for ref, value in ((in_ref, into), (turn_ref, turn)):
            ref[pl.ds(tile * MODES, HALF), :] = value[0]
            ref[pl.ds(tile * MODES + HALF, HALF), :] = value[1]


def half_entry(pos, blocks, cos, sin):
    rows = cos.shape[2] // HD * MODES
    return pl.pallas_call(
        entry_kernel,
        in_specs=[pl.BlockSpec(memory_space=pltpu.SMEM)] + [pl.BlockSpec()] * 5,
        out_shape=[jax.ShapeDtypeStruct((rows, HD), F32)] * 2,
        compiler_params=pltpu.CompilerParams(vmem_limit_bytes=4 * 2**20),
        cost_estimate=pl.CostEstimate(flops=300_000, bytes_accessed=400_000, transcendentals=2000),
        name="half_entry",
    )(pos, *blocks, cos, sin)


def chip_entry_kernel(top_ref, in_ref, turn_ref, out_ref):
    for tile in range(in_ref.shape[0] // MODES):
        part = cmul(half_of(top_ref, tile), half_of(turn_ref, tile))
        into = half_of(in_ref, tile)
        out_ref[pl.ds(tile * MODES, HALF), :] = part[0] + into[0]
        out_ref[pl.ds(tile * MODES + HALF, HALF), :] = part[1] + into[1]


def chip_entry(top, into, turn):
    return pl.pallas_call(
        chip_entry_kernel,
        in_specs=[pl.BlockSpec()] * 3,
        out_shape=jax.ShapeDtypeStruct(into.shape, F32),
        compiler_params=pltpu.CompilerParams(vmem_limit_bytes=4 * 2**20),
        cost_estimate=pl.CostEstimate(flops=100_000, bytes_accessed=200_000, transcendentals=0),
        name="chip_entry",
    )(top, into, turn)


def finish_kernel(
    pos_ref, mine_ref, theirs_ref, other_ref, st_re, st_im, pass_re, pass_im, local_ref, fall_ref, cos_ref, sin_ref,
    cb_ref, rec_ref, start, acc, out
):
    heads = rec_ref.shape[1] // HD
    first_core = pos_ref[3] == 0
    for tile in range(heads):
        lanes = pl.ds(tile * HD, HD)
        mine, theirs = half_of(mine_ref, tile), half_of(theirs_ref, tile)
        at_chip = [
            jnp.concatenate(
                [jnp.where(first_core, mine[i], theirs[i]), jnp.where(first_core, theirs[i], mine[i])], axis=0
            )
            for i in (0, 1)
        ]
        fade = jnp.exp(-other_ref[pl.ds(heads * 2 * MODES + tile, 1), :])
        moved = cmul(at_chip, [fade * ref[2, :, lanes] for ref in (cos_ref, sin_ref)])
        other = [other_ref[pl.ds(tile * 2 * MODES + i * MODES, MODES), :] for i in (0, 1)]
        state = [jnp.where(first_core, at_chip[i], moved[i] + other[i]) for i in (0, 1)]
        start[tile, 0], start[tile, 1] = cmul(state, (cb_ref[0, :, lanes], cb_ref[1, :, lanes]))
    group = 8
    for tile in range(heads):
        lanes = pl.ds(tile * HD, HD)
        for base in range(0, MODES, group):
            older, newer, twice = [], [], []
            for m in range(base, base + group):
                at = pl.ds(m * NBLK, NBLK)
                own = pl.ds(m, 1)
                moved = cmul((pass_re[tile, at, :], pass_im[tile, at, :]), (start[tile, 0, own, :], start[tile, 1, own, :]))
                z = (st_re[tile, at, :] + moved[0], st_im[tile, at, :] + moved[1])
                cos = cos_ref[0, own, lanes]
                older.append(z[0])
                newer.append(cos * z[0] - sin_ref[0, own, lanes] * z[1])
                twice.append(jnp.broadcast_to(2.0 * cos, (NBLK, HD)))
            for r in range(BLK):
                if r > 0:
                    for i in range(group):
                        older[i], newer[i] = newer[i], twice[i] * newer[i] - older[i]
                total = functools.reduce(jnp.add, newer)
                if base == 0:
                    acc[r] = local_ref[r, :, lanes] + total
                else:
                    out[tile, pl.ds(r, NBLK, stride=BLK), :] = (acc[r] + total) * fall_ref[r, :, lanes]
        rec_ref[:, lanes] = out[tile]


def finish(pos, mine, theirs, other, states, passing, local, fall, cos, sin, cb):
    width = fall.shape[2]
    tiles = width // HD
    return pl.pallas_call(
        finish_kernel,
        in_specs=[pl.BlockSpec(memory_space=pltpu.SMEM)] + [pl.BlockSpec()] * 12,
        out_shape=jax.ShapeDtypeStruct((ROWS, width), F32),
        scratch_shapes=[
            pltpu.VMEM((tiles, 2, MODES, HD), F32),
            pltpu.VMEM((BLK, NBLK, HD), F32),
            pltpu.VMEM((tiles, ROWS, HD), F32),
        ],
        compiler_params=pltpu.CompilerParams(vmem_limit_bytes=20 * 2**20),
        cost_estimate=pl.CostEstimate(flops=8_000_000, bytes_accessed=5_000_000, transcendentals=0),
        name="finish",
    )(pos, mine, theirs, other, *states, *passing, local, fall, cos, sin, cb)


def shards(queries, keys, values, decay, gain, theta, mode_coeffs):
    width = queries.shape[1]
    me = lax.axis_index("seq")
    core = me % 2
    chip = me // 2

    own = jnp.stack([keys, values])
    sh2 = lax.ppermute(own, "seq", chip_pairs(0, 1))
    hop = lax.ppermute(own, "seq", ring_x_pairs(-1, (0,)))
    up = lax.ppermute(own, "seq", CORE_UP)
    angles = jnp.asarray(TURNS, F32)[:, None, None] * theta[None]
    cos, sin = jnp.cos(angles), jnp.sin(angles)
    made = tables(decay, gain[None, :], mode_coeffs, cos, sin)
    w, fall, fade, kern, total, cb, *passing = made
    pos = jnp.stack(
        [
            (me >= 2).astype(jnp.int32),
            (me >= 4).astype(jnp.int32),
            ((me >= 3) | (core == 1)).astype(jnp.int32),
            core.astype(jnp.int32),
            chip.astype(jnp.int32),
        ]
    )
    begun = attention_own(queries, own, up)
    sh2, total = lax.optimization_barrier((sh2, total))
    far = lax.ppermute(pick(pos, hop, sh2), "seq", two_back_second_hop() + chip_pairs(0, 1, (1,)))
    swapped = lax.ppermute(sh2, "seq", CORE_SWAP)
    *near, mark = attention_next(pos, queries, sh2, swapped, *begun)
    far, mark = lax.optimization_barrier((far, mark))
    down = lax.ppermute(far, "seq", CORE_DOWN)
    attn, wide, ssq = attention_far(pos, queries, far, up, down, *near, mark)

    ssq_all = lax.all_to_all(jnp.broadcast_to(ssq, (NZ, ROWS)), "mp", 0, 0)

    g, *states, dev_sum = block_ends(wide, w, ssq_all, cos, sin, fade, total, cb)
    local = local_part(g, kern)

    other = lax.ppermute(dev_sum, "seq", CORE_SWAP)
    block = chip_sum(pos, dev_sum, other, cos, sin)
    blocks = []
    for level in range(3):
        blocks.append(lax.ppermute(block, "seq", [(d, d ^ (2 << level)) for d in range(SEQ)]))
        block = block_sum(level, pos, block, blocks[-1], cos, sin)
    top = lax.ppermute(block, "seq", [(d, d + SEQ // 2) for d in range(SEQ // 2)])
    into, turn = half_entry(pos, blocks, cos, sin)
    mine = chip_entry(top, into, turn)
    theirs = lax.ppermute(mine, "seq", CORE_SWAP)

    rec = finish(pos, mine, theirs, other, states, passing, local, fall, cos, sin, cb)
    return (attn, rec)


def solution(mesh):
    placed = (
        P("seq", "mp"),
        P("seq", "mp"),
        P("seq", "mp"),
        P("seq", "mp"),
        P("mp"),
        P(None, "mp"),
        P(None, None, "mp"),
    )
    return jax.shard_map(
        shards,
        mesh=mesh,
        in_specs=placed,
        out_specs=(P("seq", "mp"), P("seq", "mp")),
        check_vma=False,
    )
```

```python
import functools
import math

import jax
import jax.numpy as jnp
from jax import lax
from jax.experimental import pallas as pl
from jax.experimental.pallas import tpu as pltpu
from jax.sharding import PartitionSpec as P

HD = 128
EMBED_DIMENSION = 5120
MODES = 16
HALF = MODES // 2
ROWS = 256
BLK = 16
NBLK = ROWS // BLK
NX = 4
NY = 4
NZ = 8
SEQ = 32
NEG = -1e30
SCALE2 = math.log2(math.e) / math.sqrt(HD)
F32 = jnp.float32
TURNS = (1, BLK, ROWS, 2 * ROWS, 2 * NX * ROWS)


def device_of(y, x, core):
    return (y * NX + x) * 2 + core


def chip_pairs(dy, dx, cores=(0, 1)):
    pairs = []
    for chip in range(NX * NY):
        target = chip + dy * NX + dx
        if 0 <= target < NX * NY:
            pairs += [(chip * 2 + c, target * 2 + c) for c in cores]
    return pairs


def two_back(hop):
    pairs = []
    for chip in range(NX * NY - 2):
        y, x = divmod(chip, NX)
        middle = device_of(y + (x == 2), (x - 1) % NX, 0)
        pairs.append((chip * 2, middle) if hop == 0 else (middle, (chip + 2) * 2))
    return pairs


X_GROUPS = [[device_of(y, x, c) for x in range(NX)] for y in range(NY) for c in (0, 1)]
Y_GROUPS = [[device_of(y, x, c) for y in range(NY)] for x in range(NX) for c in (0, 1)]
CORE_SWAP = [(d, d ^ 1) for d in range(SEQ)]
CORE_UP = [(d, d + 1) for d in range(0, SEQ, 2)]
CORE_DOWN = [(d + 1, d) for d in range(0, SEQ, 2)]


def cmul(a, b):
    return (a[0] * b[0] - a[1] * b[1], a[0] * b[1] + a[1] * b[0])


def masks():
    row = lax.broadcasted_iota(jnp.int32, (ROWS, ROWS), 0)
    col = lax.broadcasted_iota(jnp.int32, (ROWS, ROWS), 1)
    return row, col


def scores_of(q, k):
    return lax.dot_general(q, k, (((1,), (1,)), ((), ())), preferred_element_type=F32)


def softmax_parts(parts, vals, top):
    weights = [jnp.exp2((s - top) * SCALE2) for s in parts]
    total = jnp.sum(functools.reduce(jnp.add, weights), axis=1, keepdims=True)
    mixed = [jnp.dot(w.astype(jnp.bfloat16), v, preferred_element_type=F32) for w, v in zip(weights, vals)]
    return total, functools.reduce(jnp.add, mixed)


def own_kernel(q_ref, own_ref, up_ref, top_ref, total_ref, mixed_ref):
    row, col = masks()
    for head in range(q_ref.shape[1] // HD):
        lanes = pl.ds(head * HD, HD)
        part = jnp.where(col <= row, scores_of(q_ref[:, lanes], own_ref[0, :, lanes]), NEG)
        top = jnp.max(part, axis=1, keepdims=True)
        total, mixed = softmax_parts([part], [own_ref[1, :, lanes]], top)
        top_ref[:, lanes] = jnp.broadcast_to(top, (ROWS, HD))
        total_ref[:, lanes] = jnp.broadcast_to(total, (ROWS, HD))
        mixed_ref[:, lanes] = mixed


def next_kernel(
    pos_ref, q_ref, two_ref, swap_ref, top_in, total_in, mixed_in, top_ref, total_ref, mixed_ref, mark_ref
):
    there = pos_ref[0] == 1
    for head in range(q_ref.shape[1] // HD):
        lanes = pl.ds(head * HD, HD)
        q = q_ref[:, lanes]
        parts = [jnp.where(there, scores_of(q, ref[0, :, lanes]), NEG) for ref in (two_ref, swap_ref)]
        old = top_in[:, lanes]
        top = jnp.maximum(old[:, :1], jnp.max(jnp.maximum(*parts), axis=1, keepdims=True))
        total, mixed = softmax_parts(parts, [ref[1, :, lanes] for ref in (two_ref, swap_ref)], top)
        shrink = jnp.exp2((old - top) * SCALE2)
        top_ref[:, lanes] = jnp.broadcast_to(top, (ROWS, HD))
        total_ref[:, lanes] = total_in[:, lanes] * shrink + total
        mixed_ref[:, lanes] = mixed_in[:, lanes] * shrink + mixed
    mark_ref[...] = jnp.zeros(mark_ref.shape, F32)


def pick_kernel(pos_ref, hop_ref, two_ref, out_ref, sem):
    @pl.when(pos_ref[3] == 0)
    def _():
        copy = pltpu.make_async_copy(hop_ref, out_ref, sem)
        copy.start()
        copy.wait()

    @pl.when(pos_ref[3] != 0)
    def _():
        copy = pltpu.make_async_copy(two_ref, out_ref, sem)
        copy.start()
        copy.wait()


def far_kernel(
    pos_ref, q_ref, far_ref, up_ref, down_ref, top_ref, total_ref, mixed_ref, mark_ref, o_ref, wide_ref, ssq_ref
):
    row, col = masks()
    first_core = pos_ref[3] == 0
    there = pos_ref[2] == 1
    low = row - jnp.where(pos_ref[1] == 1, 0, -2 * ROWS)
    square = None
    for head in range(q_ref.shape[1] // HD):
        lanes = pl.ds(head * HD, HD)
        q = q_ref[:, lanes]
        last = [far_ref[i, :, lanes] for i in (0, 1)]
        side = [jnp.where(first_core, down_ref[i, :, lanes], up_ref[i, :, lanes]) for i in (0, 1)]
        parts = [
            jnp.where(col > low, scores_of(q, last[0]), NEG),
            jnp.where(there, scores_of(q, side[0]), NEG),
        ]
        old = top_ref[:, lanes]
        top = jnp.maximum(old[:, :1], jnp.max(jnp.maximum(*parts), axis=1, keepdims=True))
        total, mixed = softmax_parts(parts, (last[1], side[1]), top)
        shrink = jnp.exp2((old - top) * SCALE2)
        total = total_ref[:, lanes] * shrink + total
        out = ((mixed_ref[:, lanes] * shrink + mixed) / total).astype(jnp.bfloat16)
        o_ref[:, lanes] = out
        wide = out.astype(F32)
        wide_ref[head] = wide
        square = wide * wide if square is None else square + wide * wide
    ssq_ref[...] = jnp.sum(jnp.transpose(square), axis=0, keepdims=True)


def attention_own(queries, own, up):
    wide = jax.ShapeDtypeStruct(queries.shape, F32)
    return pl.pallas_call(
        own_kernel,
        in_specs=[pl.BlockSpec()] * 2 + [pl.BlockSpec(memory_space=pl.ANY)],
        out_shape=[wide, wide, wide],
        compiler_params=pltpu.CompilerParams(vmem_limit_bytes=24 * 2**20),
        cost_estimate=pl.CostEstimate(flops=170_000_000, bytes_accessed=3_000_000, transcendentals=330_000),
        name="attention_own",
    )(queries, own, up)


def attention_next(pos, queries, sh2, swapped, top, total, mixed):
    wide = jax.ShapeDtypeStruct(queries.shape, F32)
    return pl.pallas_call(
        next_kernel,
        in_specs=[pl.BlockSpec(memory_space=pltpu.SMEM)] + [pl.BlockSpec()] * 6,
        out_shape=[wide, wide, wide, jax.ShapeDtypeStruct((8, HD), F32)],
        compiler_params=pltpu.CompilerParams(vmem_limit_bytes=24 * 2**20),
        cost_estimate=pl.CostEstimate(flops=340_000_000, bytes_accessed=5_000_000, transcendentals=650_000),
        name="attention_next",
    )(pos, queries, sh2, swapped, top, total, mixed)


def pick(pos, hop, sh2):
    return pl.pallas_call(
        pick_kernel,
        in_specs=[pl.BlockSpec(memory_space=pltpu.SMEM)] + [pl.BlockSpec(memory_space=pl.ANY)] * 2,
        out_specs=pl.BlockSpec(memory_space=pl.ANY),
        out_shape=jax.ShapeDtypeStruct(hop.shape, hop.dtype),
        scratch_shapes=[pltpu.SemaphoreType.DMA],
        compiler_params=pltpu.CompilerParams(vmem_limit_bytes=2 * 2**20),
        cost_estimate=pl.CostEstimate(flops=0, bytes_accessed=1_300_000, transcendentals=0),
        name="pick",
    )(pos, hop, sh2)


def attention_far(pos, queries, far, up, down, top, total, mixed, mark):
    return pl.pallas_call(
        far_kernel,
        in_specs=[pl.BlockSpec(memory_space=pltpu.SMEM)] + [pl.BlockSpec()] * 8,
        out_shape=[
            jax.ShapeDtypeStruct(queries.shape, jnp.bfloat16),
            jax.ShapeDtypeStruct((queries.shape[1] // HD, ROWS, HD), F32),
            jax.ShapeDtypeStruct((1, ROWS), F32),
        ],
        compiler_params=pltpu.CompilerParams(vmem_limit_bytes=24 * 2**20),
        cost_estimate=pl.CostEstimate(flops=340_000_000, bytes_accessed=5_000_000, transcendentals=650_000),
        name="attention_far",
    )(pos, queries, far, up, down, top, total, mixed, mark)


def one_less_exp(v):
    series = 1.0 / 720.0
    for order in (120.0, 24.0, 6.0, 2.0, 1.0):
        series = 1.0 / order - v * series
    return jnp.where(v < 0.25, v * series, 1.0 - jnp.exp(-v))


def tables_kernel(
    decay_ref, gain_ref, coef_ref, cos_ref, sin_ref, w_ref, fall_ref, fade_ref, kern_ref, total_ref, cb_ref, pass_re,
    pass_im
):
    gain = gain_ref[...]
    cum = jnp.zeros((NBLK, HD), F32)
    for r in range(BLK):
        step = decay_ref[pl.ds(r, NBLK, stride=BLK), :]
        cum = cum + step
        w_ref[r] = jnp.exp(cum) * (gain * jnp.sqrt(one_less_exp(2.0 * step)))
        fall_ref[r] = jnp.exp(-cum)
    fade_ref[...] = jnp.exp(-cum)
    total_ref[...] = jnp.sum(cum, axis=0, keepdims=True)
    z = cmul((coef_ref[2], coef_ref[3]), (coef_ref[0], coef_ref[1]))
    cb_ref[0], cb_ref[1] = z
    rot = (cos_ref[0], sin_ref[0])
    for lag in range(BLK):
        kern_ref[pl.ds(lag, 1), :] = jnp.sum(z[0], axis=0, keepdims=True)
        z = cmul(z, rot)
    moved = (jnp.ones((MODES, HD), F32), jnp.zeros((MODES, HD), F32))
    rot16 = (cos_ref[1], sin_ref[1])
    for j in range(NBLK):
        at = pl.ds(j, MODES, stride=NBLK)
        pass_re[0, at, :] = moved[0]
        pass_im[0, at, :] = moved[1]
        fade = fade_ref[pl.ds(j, 1), :]
        moved = tuple(fade * part for part in cmul(moved, rot16))


def tables(decay, gain, mode_coeffs, cos, sin):
    width = decay.shape[1]
    tokens = pl.BlockSpec((ROWS, HD), lambda h: (0, h))
    cube = pl.BlockSpec((BLK, NBLK, HD), lambda h: (0, 0, h))
    flat = pl.BlockSpec((NBLK, HD), lambda h: (0, h))
    line = pl.BlockSpec((1, HD), lambda h: (0, h))
    deep = pl.BlockSpec((1, MODES * NBLK, HD), lambda h: (h, 0, 0))
    return pl.pallas_call(
        tables_kernel,
        grid=(width // HD,),
        in_specs=[
            tokens,
            line,
            pl.BlockSpec((4, MODES, HD), lambda h: (0, 0, h)),
            pl.BlockSpec((2, MODES, HD), lambda h: (0, 0, h)),
            pl.BlockSpec((2, MODES, HD), lambda h: (0, 0, h)),
        ],
        out_specs=[cube, cube, flat, flat, line, pl.BlockSpec((2, MODES, HD), lambda h: (0, 0, h)), deep, deep],
        out_shape=[
            jax.ShapeDtypeStruct((BLK, NBLK, width), F32),
            jax.ShapeDtypeStruct((BLK, NBLK, width), F32),
            jax.ShapeDtypeStruct((NBLK, width), F32),
            jax.ShapeDtypeStruct((BLK, width), F32),
            jax.ShapeDtypeStruct((1, width), F32),
            jax.ShapeDtypeStruct((2, MODES, width), F32),
            jax.ShapeDtypeStruct((width // HD, MODES * NBLK, HD), F32),
            jax.ShapeDtypeStruct((width // HD, MODES * NBLK, HD), F32),
        ],
        compiler_params=pltpu.CompilerParams(vmem_limit_bytes=16 * 2**20),
        cost_estimate=pl.CostEstimate(flops=4000000, bytes_accessed=4000000, transcendentals=0),
        name="tables",
    )(decay, gain, mode_coeffs, cos, sin)


def chain_step(state, rot16, fade_row, end):
    turned = cmul(state, rot16)
    return (fade_row * turned[0] + end[0], fade_row * turned[1] + end[1])


def ends_kernel(
    wide_ref, w_ref, ssq_ref, cos_ref, sin_ref, fade_ref, total_ref, cb_ref, g_ref, st_re, st_im, sum_ref, scale, end_re,
    end_im
):
    heads = wide_ref.shape[0]
    row_scale = lax.rsqrt(jnp.sum(ssq_ref[...], axis=0, keepdims=True) * (1.0 / EMBED_DIMENSION) + 1e-06)
    scale[...] = jnp.transpose(jnp.broadcast_to(row_scale, (HD, ROWS)))
    group = 4
    for tile in range(heads):
        lanes = pl.ds(tile * HD, HD)
        for r in range(BLK):
            tokens = pl.ds(r, NBLK, stride=BLK)
            g_ref[r, :, lanes] = wide_ref[tile, tokens, :] * w_ref[r, :, lanes] * scale[tokens, :]
        fade = fade_ref[:, lanes]
        for base in range(0, MODES, group):
            modes = range(base, base + group)
            cos = [cos_ref[0, pl.ds(m, 1), lanes] for m in modes]
            twice = [jnp.broadcast_to(2.0 * c, (NBLK, HD)) for c in cos]
            first = g_ref[0, :, lanes]
            older = [first] * group
            second = g_ref[1, :, lanes]
            newer = [twice[i] * first + second for i in range(group)]
            for r in range(2, BLK):
                term = g_ref[r, :, lanes]
                for i in range(group):
                    older[i], newer[i] = newer[i], twice[i] * newer[i] + (term - older[i])
            for i, m in enumerate(modes):
                sin = sin_ref[0, pl.ds(m, 1), lanes]
                end_re[tile, pl.ds(m * NBLK, NBLK), :] = fade * (newer[i] - cos[i] * older[i])
                end_im[tile, pl.ds(m * NBLK, NBLK), :] = fade * (sin * older[i])
    states = [None] * heads
    for j in range(NBLK):
        at = pl.ds(j, MODES, stride=NBLK)
        for tile in range(heads):
            lanes = pl.ds(tile * HD, HD)
            end = (end_re[tile, at, :], end_im[tile, at, :])
            if j == 0:
                st_re[tile, at, :] = jnp.zeros((MODES, HD), F32)
                st_im[tile, at, :] = jnp.zeros((MODES, HD), F32)
                states[tile] = end
            else:
                given = cmul(states[tile], (cb_ref[0, :, lanes], cb_ref[1, :, lanes]))
                st_re[tile, at, :] = given[0]
                st_im[tile, at, :] = given[1]
                rot16 = (cos_ref[1, :, lanes], sin_ref[1, :, lanes])
                states[tile] = chain_step(states[tile], rot16, fade_ref[pl.ds(j, 1), lanes], end)
    for tile in range(heads):
        lanes = pl.ds(tile * HD, HD)
        sum_ref[pl.ds(tile * 2 * MODES, MODES), :] = states[tile][0]
        sum_ref[pl.ds(tile * 2 * MODES + MODES, MODES), :] = states[tile][1]
        sum_ref[pl.ds(heads * 2 * MODES + tile, 1), :] = total_ref[:, lanes]
    used = heads * (2 * MODES + 1)
    sum_ref[pl.ds(used, sum_ref.shape[0] - used), :] = jnp.zeros((sum_ref.shape[0] - used, HD), F32)


def padded(rows):
    return -(-rows // 8) * 8


def block_ends(wide, w, ssq, cos, sin, fade, total, cb):
    width = w.shape[2]
    tiles = width // HD
    return pl.pallas_call(
        ends_kernel,
        out_shape=[
            jax.ShapeDtypeStruct((BLK, NBLK, width), F32),
            jax.ShapeDtypeStruct((tiles, MODES * NBLK, HD), F32),
            jax.ShapeDtypeStruct((tiles, MODES * NBLK, HD), F32),
            jax.ShapeDtypeStruct((padded(tiles * (2 * MODES + 1)), HD), F32),
        ],
        scratch_shapes=[pltpu.VMEM((ROWS, HD), F32)]
        + [pltpu.VMEM((tiles, MODES * NBLK, HD), F32)] * 2,
        compiler_params=pltpu.CompilerParams(vmem_limit_bytes=20 * 2**20),
        cost_estimate=pl.CostEstimate(flops=8_000_000, bytes_accessed=4_000_000, transcendentals=0),
        name="block_ends",
    )(wide, w, ssq, cos, sin, fade, total, cb)


def local_kernel(g_ref, kern_ref, out_ref):
    heads = g_ref.shape[2] // HD
    for tile in range(heads):
        lanes = pl.ds(tile * HD, HD)
        g = [g_ref[r, :, lanes] for r in range(BLK)]
        total = [None] * BLK
        for lag in range(BLK):
            k = jnp.broadcast_to(kern_ref[pl.ds(lag, 1), lanes], (NBLK, HD))
            for r in range(lag, BLK):
                term = k * g[r - lag]
                total[r] = term if total[r] is None else total[r] + term
        for r in range(BLK):
            out_ref[r, :, lanes] = total[r]


def local_part(g, kern):
    return pl.pallas_call(
        local_kernel,
        out_shape=jax.ShapeDtypeStruct(g.shape, F32),
        compiler_params=pltpu.CompilerParams(vmem_limit_bytes=20 * 2**20),
        cost_estimate=pl.CostEstimate(flops=3_000_000, bytes_accessed=1_300_000, transcendentals=0),
        name="local_part",
    )(g, kern)


def half_of(ref, tile, base=0):
    return (ref[pl.ds(base + tile * MODES, HALF), :], ref[pl.ds(base + tile * MODES + HALF, HALF), :])


def write_copies(ref, size, tiles, tile, value, decay):
    for copy in range(ref.shape[0] // size):
        base = copy * size
        ref[pl.ds(base + tile * MODES, HALF), :] = value[0]
        ref[pl.ds(base + tile * MODES + HALF, HALF), :] = value[1]
        ref[pl.ds(base + tiles * MODES + tile, 1), :] = decay


def clear_rest(ref, size, used):
    for copy in range(ref.shape[0] // size):
        ref[pl.ds(copy * size + used, size - used), :] = jnp.zeros((size - used, HD), F32)


def chip_kernel(pos_ref, own_ref, other_ref, cos_ref, sin_ref, out_ref):
    tiles = cos_ref.shape[2] // HD
    size = out_ref.shape[0] // NX
    core = pos_ref[3]
    first_core = core == 0
    half = pl.multiple_of(core * HALF, HALF)
    for tile in range(tiles):
        lanes = pl.ds(tile * HD, HD)
        rows = [pl.ds(pl.multiple_of(tile * 2 * MODES + i * MODES + half, HALF), HALF) for i in (0, 1)]
        own = [own_ref[at, :] for at in rows]
        other = [other_ref[at, :] for at in rows]
        at = pl.ds(tiles * 2 * MODES + tile, 1)
        own_decay, other_decay = own_ref[at, :], other_ref[at, :]
        fade = jnp.exp(-jnp.where(first_core, other_decay, own_decay))
        turn = [fade * ref[2, pl.ds(half, HALF), lanes] for ref in (cos_ref, sin_ref)]
        first = [jnp.where(first_core, own[i], other[i]) for i in (0, 1)]
        second = [jnp.where(first_core, other[i], own[i]) for i in (0, 1)]
        moved = cmul(first, turn)
        write_copies(
            out_ref, size, tiles, tile, [moved[i] + second[i] for i in (0, 1)], own_decay + other_decay
        )
    clear_rest(out_ref, size, tiles * (MODES + 1))


def chip_sum(pos, own, other, cos, sin):
    tiles = cos.shape[2] // HD
    return pl.pallas_call(
        chip_kernel,
        in_specs=[pl.BlockSpec(memory_space=pltpu.SMEM)] + [pl.BlockSpec()] * 4,
        out_shape=jax.ShapeDtypeStruct((NX * padded(tiles * (MODES + 1)), HD), F32),
        compiler_params=pltpu.CompilerParams(vmem_limit_bytes=4 * 2**20),
        cost_estimate=pl.CostEstimate(flops=100_000, bytes_accessed=300_000, transcendentals=640),
        name="chip_sum",
    )(pos, own, other, cos, sin)


def running(ref, size, tiles, tile, count, mine, step, state, turn):
    at = tiles * MODES + tile
    into = turned = None
    decay = jnp.zeros((1, HD), F32)
    zero = jnp.zeros((HALF, HD), F32)
    for k in range(count):
        if k:
            here = mine == k
            into = [jnp.where(here, state[i], into[i]) for i in (0, 1)]
            turned = [jnp.where(here, turn[i], turned[i]) for i in (0, 1)]
        else:
            into, turned = [zero, zero], list(turn)
        step_decay = ref[pl.ds(k * size + at, 1), :]
        fade = jnp.exp(-step_decay)
        moving = [fade * part for part in step]
        value = half_of(ref, tile, k * size)
        if k:
            moved = cmul(state, moving)
            state = [moved[i] + value[i] for i in (0, 1)]
        else:
            state = list(value)
        turn = cmul(turn, moving)
        decay = decay + step_decay
    return into, turned, state, decay


def row_kernel(pos_ref, chips_ref, cos_ref, sin_ref, row_ref, in_ref, turn_ref):
    tiles = in_ref.shape[0] // MODES
    size = chips_ref.shape[0] // NX
    half = pl.ds(pl.multiple_of(pos_ref[3] * HALF, HALF), HALF)
    one = (jnp.ones((HALF, HD), F32), jnp.zeros((HALF, HD), F32))
    for tile in range(tiles):
        lanes = pl.ds(tile * HD, HD)
        step = (cos_ref[3, half, lanes], sin_ref[3, half, lanes])
        into, turned, state, decay = running(chips_ref, size, tiles, tile, NX, pos_ref[4], step, None, one)
        write_copies(row_ref, size, tiles, tile, state, decay)
        for ref, value in ((in_ref, into), (turn_ref, turned)):
            ref[pl.ds(tile * MODES, HALF), :] = value[0]
            ref[pl.ds(tile * MODES + HALF, HALF), :] = value[1]
    clear_rest(row_ref, size, tiles * (MODES + 1))


def row_sum(pos, chips, cos, sin):
    tiles = cos.shape[2] // HD
    return pl.pallas_call(
        row_kernel,
        in_specs=[pl.BlockSpec(memory_space=pltpu.SMEM)] + [pl.BlockSpec()] * 3,
        out_shape=[
            jax.ShapeDtypeStruct((NY * padded(tiles * (MODES + 1)), HD), F32),
            jax.ShapeDtypeStruct((tiles * MODES, HD), F32),
            jax.ShapeDtypeStruct((tiles * MODES, HD), F32),
        ],
        compiler_params=pltpu.CompilerParams(vmem_limit_bytes=4 * 2**20),
        cost_estimate=pl.CostEstimate(flops=300_000, bytes_accessed=400_000, transcendentals=5000),
        name="row_sum",
    )(pos, chips, cos, sin)


def entry_kernel(pos_ref, rows_ref, in_ref, turn_ref, cos_ref, sin_ref, out_ref):
    tiles = in_ref.shape[0] // MODES
    size = rows_ref.shape[0] // NY
    half = pl.ds(pl.multiple_of(pos_ref[3] * HALF, HALF), HALF)
    one = (jnp.ones((HALF, HD), F32), jnp.zeros((HALF, HD), F32))
    for tile in range(tiles):
        lanes = pl.ds(tile * HD, HD)
        step = (cos_ref[4, half, lanes], sin_ref[4, half, lanes])
        row, _, _, _ = running(rows_ref, size, tiles, tile, NY, pos_ref[5], step, None, one)
        moved = cmul(row, half_of(turn_ref, tile))
        into = half_of(in_ref, tile)
        out_ref[pl.ds(tile * MODES, HALF), :] = moved[0] + into[0]
        out_ref[pl.ds(tile * MODES + HALF, HALF), :] = moved[1] + into[1]


def chip_entry(pos, rows, into, turn, cos, sin):
    return pl.pallas_call(
        entry_kernel,
        in_specs=[pl.BlockSpec(memory_space=pltpu.SMEM)] + [pl.BlockSpec()] * 5,
        out_shape=jax.ShapeDtypeStruct(into.shape, F32),
        compiler_params=pltpu.CompilerParams(vmem_limit_bytes=4 * 2**20),
        cost_estimate=pl.CostEstimate(flops=300_000, bytes_accessed=400_000, transcendentals=5000),
        name="chip_entry",
    )(pos, rows, into, turn, cos, sin)


def gathered(copies, count, groups):
    parts = copies.reshape(count, copies.shape[0] // count, copies.shape[1])
    return lax.all_to_all(parts, "seq", 0, 0, axis_index_groups=groups).reshape(copies.shape)


def finish_kernel(
    pos_ref, mine_ref, theirs_ref, other_ref, st_re, st_im, pass_re, pass_im, local_ref, fall_ref, cos_ref, sin_ref,
    cb_ref, rec_ref, start, acc, out
):
    heads = rec_ref.shape[1] // HD
    first_core = pos_ref[3] == 0
    for tile in range(heads):
        lanes = pl.ds(tile * HD, HD)
        mine, theirs = half_of(mine_ref, tile), half_of(theirs_ref, tile)
        at_chip = [
            jnp.concatenate(
                [jnp.where(first_core, mine[i], theirs[i]), jnp.where(first_core, theirs[i], mine[i])], axis=0
            )
            for i in (0, 1)
        ]
        fade = jnp.exp(-other_ref[pl.ds(heads * 2 * MODES + tile, 1), :])
        moved = cmul(at_chip, [fade * ref[2, :, lanes] for ref in (cos_ref, sin_ref)])
        other = [other_ref[pl.ds(tile * 2 * MODES + i * MODES, MODES), :] for i in (0, 1)]
        state = [jnp.where(first_core, at_chip[i], moved[i] + other[i]) for i in (0, 1)]
        start[tile, 0], start[tile, 1] = cmul(state, (cb_ref[0, :, lanes], cb_ref[1, :, lanes]))
    group = 8
    for tile in range(heads):
        lanes = pl.ds(tile * HD, HD)
        for base in range(0, MODES, group):
            older, newer, twice = [], [], []
            for m in range(base, base + group):
                at = pl.ds(m * NBLK, NBLK)
                own = pl.ds(m, 1)
                moved = cmul((pass_re[tile, at, :], pass_im[tile, at, :]), (start[tile, 0, own, :], start[tile, 1, own, :]))
                z = (st_re[tile, at, :] + moved[0], st_im[tile, at, :] + moved[1])
                cos = cos_ref[0, own, lanes]
                older.append(z[0])
                newer.append(cos * z[0] - sin_ref[0, own, lanes] * z[1])
                twice.append(jnp.broadcast_to(2.0 * cos, (NBLK, HD)))
            for r in range(BLK):
                if r > 0:
                    for i in range(group):
                        older[i], newer[i] = newer[i], twice[i] * newer[i] - older[i]
                total = functools.reduce(jnp.add, newer)
                if base == 0:
                    acc[r] = local_ref[r, :, lanes] + total
                else:
                    out[tile, pl.ds(r, NBLK, stride=BLK), :] = (acc[r] + total) * fall_ref[r, :, lanes]
        rec_ref[:, lanes] = out[tile]


def finish(pos, mine, theirs, other, states, passing, local, fall, cos, sin, cb):
    width = fall.shape[2]
    tiles = width // HD
    return pl.pallas_call(
        finish_kernel,
        in_specs=[pl.BlockSpec(memory_space=pltpu.SMEM)] + [pl.BlockSpec()] * 12,
        out_shape=jax.ShapeDtypeStruct((ROWS, width), F32),
        scratch_shapes=[
            pltpu.VMEM((tiles, 2, MODES, HD), F32),
            pltpu.VMEM((BLK, NBLK, HD), F32),
            pltpu.VMEM((tiles, ROWS, HD), F32),
        ],
        compiler_params=pltpu.CompilerParams(vmem_limit_bytes=20 * 2**20),
        cost_estimate=pl.CostEstimate(flops=8_000_000, bytes_accessed=5_000_000, transcendentals=0),
        name="finish",
    )(pos, mine, theirs, other, *states, *passing, local, fall, cos, sin, cb)


def shards(queries, keys, values, decay, gain, theta, mode_coeffs):
    width = queries.shape[1]
    me = lax.axis_index("seq")
    core = me % 2
    chip = me // 2

    own = jnp.stack([keys, values])
    sh2 = lax.ppermute(own, "seq", chip_pairs(0, 1))
    hop = lax.ppermute(own, "seq", two_back(0))
    up = lax.ppermute(own, "seq", CORE_UP)
    angles = jnp.asarray(TURNS, F32)[:, None, None] * theta[None]
    cos, sin = jnp.cos(angles), jnp.sin(angles)
    made = tables(decay, gain[None, :], mode_coeffs, cos, sin)
    w, fall, fade, kern, total, cb, *passing = made
    pos = jnp.stack(
        [
            (me >= 2).astype(jnp.int32),
            (me >= 4).astype(jnp.int32),
            ((me >= 3) | (core == 1)).astype(jnp.int32),
            core.astype(jnp.int32),
            (chip % NX).astype(jnp.int32),
            (chip // NX).astype(jnp.int32),
        ]
    )
    begun = attention_own(queries, own, up)
    sh2, total = lax.optimization_barrier((sh2, total))
    far = lax.ppermute(pick(pos, hop, sh2), "seq", two_back(1) + chip_pairs(0, 1, (1,)))
    swapped = lax.ppermute(sh2, "seq", CORE_SWAP)
    *near, mark = attention_next(pos, queries, sh2, swapped, *begun)
    far, mark = lax.optimization_barrier((far, mark))
    down = lax.ppermute(far, "seq", CORE_DOWN)
    attn, wide, ssq = attention_far(pos, queries, far, up, down, *near, mark)

    ssq_all = lax.all_to_all(jnp.broadcast_to(ssq, (NZ, ROWS)), "mp", 0, 0)

    g, *states, dev_sum = block_ends(wide, w, ssq_all, cos, sin, fade, total, cb)
    local = local_part(g, kern)

    other = lax.ppermute(dev_sum, "seq", CORE_SWAP)
    chips = gathered(chip_sum(pos, dev_sum, other, cos, sin), NX, X_GROUPS)
    row, into, turn = row_sum(pos, chips, cos, sin)
    rows = gathered(row, NY, Y_GROUPS)
    mine = chip_entry(pos, rows, into, turn, cos, sin)
    theirs = lax.ppermute(mine, "seq", CORE_SWAP)

    rec = finish(pos, mine, theirs, other, states, passing, local, fall, cos, sin, cb)
    return (attn, rec)


def solution(mesh):
    placed = (
        P("seq", "mp"),
        P("seq", "mp"),
        P("seq", "mp"),
        P("seq", "mp"),
        P("mp"),
        P(None, "mp"),
        P(None, None, "mp"),
    )
    return jax.shard_map(
        shards,
        mesh=mesh,
        in_specs=placed,
        out_specs=(P("seq", "mp"), P("seq", "mp")),
        check_vma=False,
    )
```

```python
import functools
import math

import jax
import jax.numpy as jnp
from jax import lax
from jax.experimental import pallas as pl
from jax.experimental.pallas import tpu as pltpu
from jax.sharding import PartitionSpec as P

HD = 128
EMBED_DIMENSION = 5120
MODES = 16
HALF = MODES // 2
ROWS = 256
BLK = 16
NBLK = ROWS // BLK
NX = 4
NY = 4
NZ = 8
SEQ = 32
NEG = -1e30
SCALE2 = math.log2(math.e) / math.sqrt(HD)
F32 = jnp.float32
TURNS = (1, BLK, ROWS, 2 * ROWS, 2 * NX * ROWS)


def device_of(y, x, core):
    return (y * NX + x) * 2 + core


def chip_pairs(dy, dx, cores=(0, 1)):
    pairs = []
    for chip in range(NX * NY):
        target = chip + dy * NX + dx
        if 0 <= target < NX * NY:
            pairs += [(chip * 2 + c, target * 2 + c) for c in cores]
    return pairs


def two_back(hop):
    pairs = []
    for chip in range(NX * NY - 2):
        y, x = divmod(chip, NX)
        middle = device_of(y + (x == 2), (x - 1) % NX, 0)
        pairs.append((chip * 2, middle) if hop == 0 else (middle, (chip + 2) * 2))
    return pairs


X_GROUPS = [[device_of(y, x, c) for x in range(NX)] for y in range(NY) for c in (0, 1)]
Y_GROUPS = [[device_of(y, x, c) for y in range(NY)] for x in range(NX) for c in (0, 1)]
CORE_SWAP = [(d, d ^ 1) for d in range(SEQ)]
CORE_UP = [(d, d + 1) for d in range(0, SEQ, 2)]
CORE_DOWN = [(d + 1, d) for d in range(0, SEQ, 2)]


def cmul(a, b):
    return (a[0] * b[0] - a[1] * b[1], a[0] * b[1] + a[1] * b[0])


def masks():
    row = lax.broadcasted_iota(jnp.int32, (ROWS, ROWS), 0)
    col = lax.broadcasted_iota(jnp.int32, (ROWS, ROWS), 1)
    return row, col


def scores_of(q, k):
    return lax.dot_general(q, k, (((1,), (1,)), ((), ())), preferred_element_type=F32)


def softmax_parts(parts, vals, top):
    weights = [jnp.exp2((s - top) * SCALE2) for s in parts]
    total = jnp.sum(functools.reduce(jnp.add, weights), axis=1, keepdims=True)
    mixed = [jnp.dot(w.astype(jnp.bfloat16), v, preferred_element_type=F32) for w, v in zip(weights, vals)]
    return total, functools.reduce(jnp.add, mixed)


def merged(parts, vals, top_in, total_in, mixed_in):
    top = jnp.max(functools.reduce(jnp.maximum, parts), axis=1, keepdims=True)
    top = jnp.maximum(top_in, jnp.broadcast_to(top, (ROWS, HD)))
    total, mixed = softmax_parts(parts, vals, jnp.concatenate([top] * (ROWS // HD), axis=1))
    shrink = jnp.exp2((top_in - top) * SCALE2)
    return top, total_in * shrink + jnp.broadcast_to(total, (ROWS, HD)), mixed_in * shrink + mixed


def fetch(pos_ref, pairs, slots, sems):
    first_core = pos_ref[3] == 0
    for core in (0, 1):
        @pl.when(first_core if core == 0 else jnp.logical_not(first_core))
        def _():
            for i, pair in enumerate(pairs):
                pltpu.make_async_copy(pair[core], slots.at[i], sems.at[i]).start()


def arrived(pairs, slots, sems):
    for i, pair in enumerate(pairs):
        pltpu.make_async_copy(pair[0], slots.at[i], sems.at[i]).wait()


def near_kernel(
    pos_ref, q_ref, after, own, two0, two1, low, high, top_ref, total_ref, mixed_ref, slots, sems
):
    pairs = ((own, own), (two0, two1), (high, low))
    fetch(pos_ref, pairs, slots, sems)
    row, col = masks()
    there = pos_ref[0] == 1
    arrived(pairs, slots, sems)
    for head in range(q_ref.shape[1] // HD):
        lanes = pl.ds(head * HD, HD)
        q = q_ref[:, lanes]
        parts = [scores_of(q, slots[i, 0, :, lanes]) for i in range(3)]
        parts = [jnp.where(col <= row, parts[0], NEG)] + [jnp.where(there, part, NEG) for part in parts[1:]]
        top = jnp.max(functools.reduce(jnp.maximum, parts), axis=1, keepdims=True)
        total, mixed = softmax_parts(parts, [slots[i, 1, :, lanes] for i in range(3)], top)
        top_ref[:, lanes] = jnp.broadcast_to(top, (ROWS, HD))
        total_ref[:, lanes] = jnp.broadcast_to(total, (ROWS, HD))
        mixed_ref[:, lanes] = mixed


def far_kernel(
    pos_ref, q_ref, top_in, total_in, mixed_in, far0, far1, up, down, o_ref, wide_ref, ssq_ref, slots, sems
):
    pairs = ((far0, far1), (down, up))
    fetch(pos_ref, pairs, slots, sems)
    row, col = masks()
    there = pos_ref[2] == 1
    low = row - jnp.where(pos_ref[1] == 1, 0, -2 * ROWS)
    square = None
    arrived(pairs, slots, sems)
    for head in range(q_ref.shape[1] // HD):
        lanes = pl.ds(head * HD, HD)
        q = q_ref[:, lanes]
        parts = [
            jnp.where(col > low, scores_of(q, slots[0, 0, :, lanes]), NEG),
            jnp.where(there, scores_of(q, slots[1, 0, :, lanes]), NEG),
        ]
        _, total, mixed = merged(
            parts, [slots[i, 1, :, lanes] for i in (0, 1)], top_in[:, lanes], total_in[:, lanes], mixed_in[:, lanes]
        )
        out = (mixed / total).astype(jnp.bfloat16)
        o_ref[:, lanes] = out
        wide = out.astype(F32)
        wide_ref[head] = wide
        square = wide * wide if square is None else square + wide * wide
    ssq_ref[...] = jnp.sum(jnp.transpose(square), axis=0, keepdims=True)


def gate_kernel(*refs):
    pass


def gate(value, *after):
    place = pl.BlockSpec(memory_space=pl.ANY)
    return pl.pallas_call(
        gate_kernel,
        in_specs=[place] * (1 + len(after)),
        out_specs=place,
        out_shape=jax.ShapeDtypeStruct(value.shape, value.dtype),
        input_output_aliases={0: 0},
        compiler_params=pltpu.CompilerParams(vmem_limit_bytes=2**20),
        name="gate",
    )(value, *after)


def attention_call(kernel, name, share, operands, outs, placed):
    scalars = 1
    kept = len(operands) - scalars - placed
    block = (share,) + operands[-1].shape
    return pl.pallas_call(
        kernel,
        in_specs=[pl.BlockSpec(memory_space=pltpu.SMEM)] * scalars
        + [pl.BlockSpec()] * kept
        + [pl.BlockSpec(memory_space=pl.ANY)] * placed,
        out_shape=outs,
        scratch_shapes=[pltpu.VMEM(block, jnp.bfloat16), pltpu.SemaphoreType.DMA((share,))],
        compiler_params=pltpu.CompilerParams(vmem_limit_bytes=12 * 2**20),
        cost_estimate=pl.CostEstimate(
            flops=170_000_000 * share, bytes_accessed=3_000_000, transcendentals=330_000 * share
        ),
        name=name,
    )(*operands)


def one_less_exp(v):
    series = 1.0 / 720.0
    for order in (120.0, 24.0, 6.0, 2.0, 1.0):
        series = 1.0 / order - v * series
    return jnp.where(v < 0.25, v * series, 1.0 - jnp.exp(-v))


def tables_kernel(
    decay_ref, gain_ref, coef_ref, cos_ref, sin_ref, after_ref, w_ref, fall_ref, fade_ref, kern_ref, total_ref, cb_ref,
    pass_re, pass_im
):
    gain = gain_ref[...]
    cum = jnp.zeros((NBLK, HD), F32)
    for r in range(BLK):
        step = decay_ref[pl.ds(r, NBLK, stride=BLK), :]
        cum = cum + step
        w_ref[r] = jnp.exp(cum) * (gain * jnp.sqrt(one_less_exp(2.0 * step)))
        fall_ref[r] = jnp.exp(-cum)
    fade_ref[...] = jnp.exp(-cum)
    total_ref[...] = jnp.sum(cum, axis=0, keepdims=True)
    z = cmul((coef_ref[2], coef_ref[3]), (coef_ref[0], coef_ref[1]))
    cb_ref[0], cb_ref[1] = z
    rot = (cos_ref[0], sin_ref[0])
    for lag in range(BLK):
        kern_ref[pl.ds(lag, 1), :] = jnp.sum(z[0], axis=0, keepdims=True)
        z = cmul(z, rot)
    moved = (jnp.ones((MODES, HD), F32), jnp.zeros((MODES, HD), F32))
    rot16 = (cos_ref[1], sin_ref[1])
    for j in range(NBLK):
        at = pl.ds(j, MODES, stride=NBLK)
        pass_re[0, at, :] = moved[0]
        pass_im[0, at, :] = moved[1]
        fade = fade_ref[pl.ds(j, 1), :]
        moved = tuple(fade * part for part in cmul(moved, rot16))


def tables(decay, gain, mode_coeffs, cos, sin, after):
    width = decay.shape[1]
    tokens = pl.BlockSpec((ROWS, HD), lambda h: (0, h))
    cube = pl.BlockSpec((BLK, NBLK, HD), lambda h: (0, 0, h))
    flat = pl.BlockSpec((NBLK, HD), lambda h: (0, h))
    line = pl.BlockSpec((1, HD), lambda h: (0, h))
    deep = pl.BlockSpec((1, MODES * NBLK, HD), lambda h: (h, 0, 0))
    return pl.pallas_call(
        tables_kernel,
        grid=(width // HD,),
        in_specs=[
            tokens,
            line,
            pl.BlockSpec((4, MODES, HD), lambda h: (0, 0, h)),
            pl.BlockSpec((2, MODES, HD), lambda h: (0, 0, h)),
            pl.BlockSpec((2, MODES, HD), lambda h: (0, 0, h)),
            pl.BlockSpec(memory_space=pl.ANY),
        ],
        out_specs=[cube, cube, flat, flat, line, pl.BlockSpec((2, MODES, HD), lambda h: (0, 0, h)), deep, deep],
        out_shape=[
            jax.ShapeDtypeStruct((BLK, NBLK, width), F32),
            jax.ShapeDtypeStruct((BLK, NBLK, width), F32),
            jax.ShapeDtypeStruct((NBLK, width), F32),
            jax.ShapeDtypeStruct((BLK, width), F32),
            jax.ShapeDtypeStruct((1, width), F32),
            jax.ShapeDtypeStruct((2, MODES, width), F32),
            jax.ShapeDtypeStruct((width // HD, MODES * NBLK, HD), F32),
            jax.ShapeDtypeStruct((width // HD, MODES * NBLK, HD), F32),
        ],
        compiler_params=pltpu.CompilerParams(vmem_limit_bytes=8 * 2**20),
        cost_estimate=pl.CostEstimate(flops=4000000, bytes_accessed=4000000, transcendentals=0),
        name="tables",
    )(decay, gain, mode_coeffs, cos, sin, after)


def chain_step(state, rot16, fade_row, end):
    turned = cmul(state, rot16)
    return (fade_row * turned[0] + end[0], fade_row * turned[1] + end[1])


def ends_kernel(
    wide_ref, w_ref, ssq_ref, cos_ref, sin_ref, fade_ref, total_ref, cb_ref, g_ref, st_re, st_im, sum_ref, scale, end_re,
    end_im
):
    heads = wide_ref.shape[0]
    row_scale = lax.rsqrt(jnp.sum(ssq_ref[...], axis=0, keepdims=True) * (1.0 / EMBED_DIMENSION) + 1e-06)
    scale[...] = jnp.transpose(jnp.broadcast_to(row_scale, (HD, ROWS)))
    group = 4
    for tile in range(heads):
        lanes = pl.ds(tile * HD, HD)
        for r in range(BLK):
            tokens = pl.ds(r, NBLK, stride=BLK)
            g_ref[r, :, lanes] = wide_ref[tile, tokens, :] * w_ref[r, :, lanes] * scale[tokens, :]
        fade = fade_ref[:, lanes]
        for base in range(0, MODES, group):
            modes = range(base, base + group)
            cos = [cos_ref[0, pl.ds(m, 1), lanes] for m in modes]
            twice = [jnp.broadcast_to(2.0 * c, (NBLK, HD)) for c in cos]
            first = g_ref[0, :, lanes]
            older = [first] * group
            second = g_ref[1, :, lanes]
            newer = [twice[i] * first + second for i in range(group)]
            for r in range(2, BLK):
                term = g_ref[r, :, lanes]
                for i in range(group):
                    older[i], newer[i] = newer[i], twice[i] * newer[i] + (term - older[i])
            for i, m in enumerate(modes):
                sin = sin_ref[0, pl.ds(m, 1), lanes]
                end_re[tile, pl.ds(m * NBLK, NBLK), :] = fade * (newer[i] - cos[i] * older[i])
                end_im[tile, pl.ds(m * NBLK, NBLK), :] = fade * (sin * older[i])
    states = [None] * heads
    for j in range(NBLK):
        at = pl.ds(j, MODES, stride=NBLK)
        for tile in range(heads):
            lanes = pl.ds(tile * HD, HD)
            end = (end_re[tile, at, :], end_im[tile, at, :])
            if j == 0:
                st_re[tile, at, :] = jnp.zeros((MODES, HD), F32)
                st_im[tile, at, :] = jnp.zeros((MODES, HD), F32)
                states[tile] = end
            else:
                given = cmul(states[tile], (cb_ref[0, :, lanes], cb_ref[1, :, lanes]))
                st_re[tile, at, :] = given[0]
                st_im[tile, at, :] = given[1]
                rot16 = (cos_ref[1, :, lanes], sin_ref[1, :, lanes])
                states[tile] = chain_step(states[tile], rot16, fade_ref[pl.ds(j, 1), lanes], end)
    for tile in range(heads):
        lanes = pl.ds(tile * HD, HD)
        sum_ref[pl.ds(tile * 2 * MODES, MODES), :] = states[tile][0]
        sum_ref[pl.ds(tile * 2 * MODES + MODES, MODES), :] = states[tile][1]
        sum_ref[pl.ds(heads * 2 * MODES + tile, 1), :] = total_ref[:, lanes]
    used = heads * (2 * MODES + 1)
    sum_ref[pl.ds(used, sum_ref.shape[0] - used), :] = jnp.zeros((sum_ref.shape[0] - used, HD), F32)


def padded(rows):
    return -(-rows // 8) * 8


def block_ends(wide, w, ssq, cos, sin, fade, total, cb):
    width = w.shape[2]
    tiles = width // HD
    return pl.pallas_call(
        ends_kernel,
        out_shape=[
            jax.ShapeDtypeStruct((BLK, NBLK, width), F32),
            jax.ShapeDtypeStruct((tiles, MODES * NBLK, HD), F32),
            jax.ShapeDtypeStruct((tiles, MODES * NBLK, HD), F32),
            jax.ShapeDtypeStruct((padded(tiles * (2 * MODES + 1)), HD), F32),
        ],
        scratch_shapes=[pltpu.VMEM((ROWS, HD), F32)]
        + [pltpu.VMEM((tiles, MODES * NBLK, HD), F32)] * 2,
        compiler_params=pltpu.CompilerParams(vmem_limit_bytes=12 * 2**20),
        cost_estimate=pl.CostEstimate(flops=8_000_000, bytes_accessed=4_000_000, transcendentals=0),
        name="block_ends",
    )(wide, w, ssq, cos, sin, fade, total, cb)


def local_kernel(g_ref, kern_ref, out_ref):
    heads = g_ref.shape[2] // HD
    for tile in range(heads):
        lanes = pl.ds(tile * HD, HD)
        g = [g_ref[r, :, lanes] for r in range(BLK)]
        total = [None] * BLK
        for lag in range(BLK):
            k = jnp.broadcast_to(kern_ref[pl.ds(lag, 1), lanes], (NBLK, HD))
            for r in range(lag, BLK):
                term = k * g[r - lag]
                total[r] = term if total[r] is None else total[r] + term
        for r in range(BLK):
            out_ref[r, :, lanes] = total[r]


def local_part(g, kern):
    return pl.pallas_call(
        local_kernel,
        out_shape=jax.ShapeDtypeStruct(g.shape, F32),
        compiler_params=pltpu.CompilerParams(vmem_limit_bytes=12 * 2**20),
        cost_estimate=pl.CostEstimate(flops=3_000_000, bytes_accessed=1_300_000, transcendentals=0),
        name="local_part",
    )(g, kern)


def half_of(ref, tile, base=0):
    return (ref[pl.ds(base + tile * MODES, HALF), :], ref[pl.ds(base + tile * MODES + HALF, HALF), :])


def write_copies(ref, size, tiles, tile, value, decay):
    for copy in range(ref.shape[0] // size):
        base = copy * size
        ref[pl.ds(base + tile * MODES, HALF), :] = value[0]
        ref[pl.ds(base + tile * MODES + HALF, HALF), :] = value[1]
        ref[pl.ds(base + tiles * MODES + tile, 1), :] = decay


def clear_rest(ref, size, used):
    for copy in range(ref.shape[0] // size):
        ref[pl.ds(copy * size + used, size - used), :] = jnp.zeros((size - used, HD), F32)


def chip_kernel(pos_ref, own_ref, other_ref, cos_ref, sin_ref, out_ref):
    tiles = cos_ref.shape[2] // HD
    size = out_ref.shape[0] // NX
    core = pos_ref[3]
    first_core = core == 0
    half = pl.multiple_of(core * HALF, HALF)
    for tile in range(tiles):
        lanes = pl.ds(tile * HD, HD)
        rows = [pl.ds(pl.multiple_of(tile * 2 * MODES + i * MODES + half, HALF), HALF) for i in (0, 1)]
        own = [own_ref[at, :] for at in rows]
        other = [other_ref[at, :] for at in rows]
        at = pl.ds(tiles * 2 * MODES + tile, 1)
        own_decay, other_decay = own_ref[at, :], other_ref[at, :]
        fade = jnp.exp(-jnp.where(first_core, other_decay, own_decay))
        turn = [fade * ref[2, pl.ds(half, HALF), lanes] for ref in (cos_ref, sin_ref)]
        first = [jnp.where(first_core, own[i], other[i]) for i in (0, 1)]
        second = [jnp.where(first_core, other[i], own[i]) for i in (0, 1)]
        moved = cmul(first, turn)
        write_copies(
            out_ref, size, tiles, tile, [moved[i] + second[i] for i in (0, 1)], own_decay + other_decay
        )
    clear_rest(out_ref, size, tiles * (MODES + 1))


def chip_sum(pos, own, other, cos, sin):
    tiles = cos.shape[2] // HD
    return pl.pallas_call(
        chip_kernel,
        in_specs=[pl.BlockSpec(memory_space=pltpu.SMEM)] + [pl.BlockSpec()] * 4,
        out_shape=jax.ShapeDtypeStruct((NX * padded(tiles * (MODES + 1)), HD), F32),
        compiler_params=pltpu.CompilerParams(vmem_limit_bytes=4 * 2**20),
        cost_estimate=pl.CostEstimate(flops=100_000, bytes_accessed=300_000, transcendentals=640),
        name="chip_sum",
    )(pos, own, other, cos, sin)


def running(ref, size, tiles, tile, count, mine, step, state, turn):
    at = tiles * MODES + tile
    into = turned = None
    decay = jnp.zeros((1, HD), F32)
    zero = jnp.zeros((HALF, HD), F32)
    for k in range(count):
        if k:
            here = mine == k
            into = [jnp.where(here, state[i], into[i]) for i in (0, 1)]
            turned = [jnp.where(here, turn[i], turned[i]) for i in (0, 1)]
        else:
            into, turned = [zero, zero], list(turn)
        step_decay = ref[pl.ds(k * size + at, 1), :]
        fade = jnp.exp(-step_decay)
        moving = [fade * part for part in step]
        value = half_of(ref, tile, k * size)
        if k:
            moved = cmul(state, moving)
            state = [moved[i] + value[i] for i in (0, 1)]
        else:
            state = list(value)
        turn = cmul(turn, moving)
        decay = decay + step_decay
    return into, turned, state, decay


def row_kernel(pos_ref, chips_ref, cos_ref, sin_ref, row_ref, in_ref, turn_ref):
    tiles = in_ref.shape[0] // MODES
    size = chips_ref.shape[0] // NX
    half = pl.ds(pl.multiple_of(pos_ref[3] * HALF, HALF), HALF)
    one = (jnp.ones((HALF, HD), F32), jnp.zeros((HALF, HD), F32))
    for tile in range(tiles):
        lanes = pl.ds(tile * HD, HD)
        step = (cos_ref[3, half, lanes], sin_ref[3, half, lanes])
        into, turned, state, decay = running(chips_ref, size, tiles, tile, NX, pos_ref[4], step, None, one)
        write_copies(row_ref, size, tiles, tile, state, decay)
        for ref, value in ((in_ref, into), (turn_ref, turned)):
            ref[pl.ds(tile * MODES, HALF), :] = value[0]
            ref[pl.ds(tile * MODES + HALF, HALF), :] = value[1]
    clear_rest(row_ref, size, tiles * (MODES + 1))


def row_sum(pos, chips, cos, sin):
    tiles = cos.shape[2] // HD
    return pl.pallas_call(
        row_kernel,
        in_specs=[pl.BlockSpec(memory_space=pltpu.SMEM)] + [pl.BlockSpec()] * 3,
        out_shape=[
            jax.ShapeDtypeStruct((NY * padded(tiles * (MODES + 1)), HD), F32),
            jax.ShapeDtypeStruct((tiles * MODES, HD), F32),
            jax.ShapeDtypeStruct((tiles * MODES, HD), F32),
        ],
        compiler_params=pltpu.CompilerParams(vmem_limit_bytes=4 * 2**20),
        cost_estimate=pl.CostEstimate(flops=300_000, bytes_accessed=400_000, transcendentals=5000),
        name="row_sum",
    )(pos, chips, cos, sin)


def entry_kernel(pos_ref, rows_ref, in_ref, turn_ref, cos_ref, sin_ref, out_ref):
    tiles = in_ref.shape[0] // MODES
    size = rows_ref.shape[0] // NY
    half = pl.ds(pl.multiple_of(pos_ref[3] * HALF, HALF), HALF)
    one = (jnp.ones((HALF, HD), F32), jnp.zeros((HALF, HD), F32))
    for tile in range(tiles):
        lanes = pl.ds(tile * HD, HD)
        step = (cos_ref[4, half, lanes], sin_ref[4, half, lanes])
        row, _, _, _ = running(rows_ref, size, tiles, tile, NY, pos_ref[5], step, None, one)
        moved = cmul(row, half_of(turn_ref, tile))
        into = half_of(in_ref, tile)
        out_ref[pl.ds(tile * MODES, HALF), :] = moved[0] + into[0]
        out_ref[pl.ds(tile * MODES + HALF, HALF), :] = moved[1] + into[1]


def chip_entry(pos, rows, into, turn, cos, sin):
    return pl.pallas_call(
        entry_kernel,
        in_specs=[pl.BlockSpec(memory_space=pltpu.SMEM)] + [pl.BlockSpec()] * 5,
        out_shape=jax.ShapeDtypeStruct(into.shape, F32),
        compiler_params=pltpu.CompilerParams(vmem_limit_bytes=4 * 2**20),
        cost_estimate=pl.CostEstimate(flops=300_000, bytes_accessed=400_000, transcendentals=5000),
        name="chip_entry",
    )(pos, rows, into, turn, cos, sin)


def gathered(copies, count, groups):
    parts = copies.reshape(count, copies.shape[0] // count, copies.shape[1])
    return lax.all_to_all(parts, "seq", 0, 0, axis_index_groups=groups).reshape(copies.shape)


def finish_kernel(
    pos_ref, mine_ref, theirs_ref, other_ref, st_re, st_im, pass_re, pass_im, local_ref, fall_ref, cos_ref, sin_ref,
    cb_ref, rec_ref, start, acc, out
):
    heads = rec_ref.shape[1] // HD
    first_core = pos_ref[3] == 0
    for tile in range(heads):
        lanes = pl.ds(tile * HD, HD)
        mine, theirs = half_of(mine_ref, tile), half_of(theirs_ref, tile)
        at_chip = [
            jnp.concatenate(
                [jnp.where(first_core, mine[i], theirs[i]), jnp.where(first_core, theirs[i], mine[i])], axis=0
            )
            for i in (0, 1)
        ]
        fade = jnp.exp(-other_ref[pl.ds(heads * 2 * MODES + tile, 1), :])
        moved = cmul(at_chip, [fade * ref[2, :, lanes] for ref in (cos_ref, sin_ref)])
        other = [other_ref[pl.ds(tile * 2 * MODES + i * MODES, MODES), :] for i in (0, 1)]
        state = [jnp.where(first_core, at_chip[i], moved[i] + other[i]) for i in (0, 1)]
        start[tile, 0], start[tile, 1] = cmul(state, (cb_ref[0, :, lanes], cb_ref[1, :, lanes]))
    group = 8
    for tile in range(heads):
        lanes = pl.ds(tile * HD, HD)
        for base in range(0, MODES, group):
            older, newer, twice = [], [], []
            for m in range(base, base + group):
                at = pl.ds(m * NBLK, NBLK)
                own = pl.ds(m, 1)
                moved = cmul((pass_re[tile, at, :], pass_im[tile, at, :]), (start[tile, 0, own, :], start[tile, 1, own, :]))
                z = (st_re[tile, at, :] + moved[0], st_im[tile, at, :] + moved[1])
                cos = cos_ref[0, own, lanes]
                older.append(z[0])
                newer.append(cos * z[0] - sin_ref[0, own, lanes] * z[1])
                twice.append(jnp.broadcast_to(2.0 * cos, (NBLK, HD)))
            for r in range(BLK):
                if r > 0:
                    for i in range(group):
                        older[i], newer[i] = newer[i], twice[i] * newer[i] - older[i]
                total = functools.reduce(jnp.add, newer)
                if base == 0:
                    acc[r] = local_ref[r, :, lanes] + total
                else:
                    out[tile, pl.ds(r, NBLK, stride=BLK), :] = (acc[r] + total) * fall_ref[r, :, lanes]
        rec_ref[:, lanes] = out[tile]


def finish(pos, mine, theirs, other, states, passing, local, fall, cos, sin, cb):
    width = fall.shape[2]
    tiles = width // HD
    return pl.pallas_call(
        finish_kernel,
        in_specs=[pl.BlockSpec(memory_space=pltpu.SMEM)] + [pl.BlockSpec()] * 12,
        out_shape=jax.ShapeDtypeStruct((ROWS, width), F32),
        scratch_shapes=[
            pltpu.VMEM((tiles, 2, MODES, HD), F32),
            pltpu.VMEM((BLK, NBLK, HD), F32),
            pltpu.VMEM((tiles, ROWS, HD), F32),
        ],
        compiler_params=pltpu.CompilerParams(vmem_limit_bytes=12 * 2**20),
        cost_estimate=pl.CostEstimate(flops=8_000_000, bytes_accessed=5_000_000, transcendentals=0),
        name="finish",
    )(pos, mine, theirs, other, *states, *passing, local, fall, cos, sin, cb)


def shards(queries, keys, values, decay, gain, theta, mode_coeffs):
    width = queries.shape[1]
    me = lax.axis_index("seq")
    core = me % 2
    chip = me // 2

    own = jnp.stack([keys, values])
    two1 = lax.ppermute(own, "seq", chip_pairs(0, 1, (1,)))
    hop = lax.ppermute(own, "seq", two_back(0))
    up = lax.ppermute(own, "seq", CORE_UP)
    angles = jnp.asarray(TURNS, F32)[:, None, None] * theta[None]
    cos, sin = jnp.cos(angles), jnp.sin(angles)
    own_later, cos = lax.optimization_barrier((own, cos))
    two0 = lax.ppermute(own_later, "seq", chip_pairs(0, 1, (0,)))

    pos = jnp.stack(
        [
            (me >= 2).astype(jnp.int32),
            (me >= 4).astype(jnp.int32),
            ((me >= 3) | (core == 1)).astype(jnp.int32),
            core.astype(jnp.int32),
            (chip % NX).astype(jnp.int32),
            (chip // NX).astype(jnp.int32),
        ]
    )
    flat = jax.ShapeDtypeStruct(queries.shape, F32)
    far1 = lax.ppermute(two1, "seq", chip_pairs(0, 1, (1,)))
    high = lax.ppermute(two1, "seq", CORE_DOWN)
    made = tables(decay, gain[None, :], mode_coeffs, cos, sin, high)
    w, fall, fade, kern, total, cb, *passing = made
    two0 = gate(two0, high, hop)
    far0 = lax.ppermute(hop, "seq", two_back(1))
    low = lax.ppermute(two0, "seq", CORE_UP)
    run = attention_call(
        near_kernel, "attention_near", 3, [pos, queries, total, own, two0, two1, low, high], [flat] * 3, placed=6
    )
    down = lax.ppermute(gate(far1, far0), "seq", CORE_DOWN)
    attn, wide, ssq = attention_call(
        far_kernel,
        "attention_far",
        2,
        [pos, queries, *run, far0, far1, up, down],
        [
            jax.ShapeDtypeStruct(queries.shape, jnp.bfloat16),
            jax.ShapeDtypeStruct((queries.shape[1] // HD, ROWS, HD), F32),
            jax.ShapeDtypeStruct((1, ROWS), F32),
        ],
        placed=4,
    )

    ssq_all = lax.all_to_all(jnp.broadcast_to(ssq, (NZ, ROWS)), "mp", 0, 0)

    g, *states, dev_sum = block_ends(wide, w, ssq_all, cos, sin, fade, total, cb)
    local = local_part(g, kern)

    other = lax.ppermute(dev_sum, "seq", CORE_SWAP)
    chips = gathered(chip_sum(pos, dev_sum, other, cos, sin), NX, X_GROUPS)
    row, into, turn = row_sum(pos, chips, cos, sin)
    rows = gathered(row, NY, Y_GROUPS)
    mine = chip_entry(pos, rows, into, turn, cos, sin)
    theirs = lax.ppermute(mine, "seq", CORE_SWAP)

    rec = finish(pos, mine, theirs, other, states, passing, local, fall, cos, sin, cb)
    return (attn, rec)


def solution(mesh):
    placed = (
        P("seq", "mp"),
        P("seq", "mp"),
        P("seq", "mp"),
        P("seq", "mp"),
        P("mp"),
        P(None, "mp"),
        P(None, None, "mp"),
    )
    return jax.shard_map(
        shards,
        mesh=mesh,
        in_specs=placed,
        out_specs=(P("seq", "mp"), P("seq", "mp")),
        check_vma=False,
    )
```

```python
import functools
import math

import jax
import jax.numpy as jnp
from jax import lax
from jax.experimental import pallas as pl
from jax.experimental.pallas import tpu as pltpu
from jax.sharding import PartitionSpec as P

HD = 128
EMBED_DIMENSION = 5120
MODES = 16
HALF = MODES // 2
ROWS = 256
BLK = 16
NBLK = ROWS // BLK
NX = 4
NY = 4
NZ = 8
SEQ = 32
NEG = -1e30
SCALE2 = math.log2(math.e) / math.sqrt(HD)
F32 = jnp.float32
TURNS = (1, BLK, ROWS, 2 * ROWS, 2 * NX * ROWS)


def device_of(y, x, core):
    return (y * NX + x) * 2 + core


def chip_pairs(dy, dx, cores=(0, 1)):
    pairs = []
    for chip in range(NX * NY):
        target = chip + dy * NX + dx
        if 0 <= target < NX * NY:
            pairs += [(chip * 2 + c, target * 2 + c) for c in cores]
    return pairs


def two_back(hop):
    pairs = []
    for chip in range(NX * NY - 2):
        y, x = divmod(chip, NX)
        middle = device_of(y + (x == 2), (x - 1) % NX, 0)
        pairs.append((chip * 2, middle) if hop == 0 else (middle, (chip + 2) * 2))
    return pairs


X_GROUPS = [[device_of(y, x, c) for x in range(NX)] for y in range(NY) for c in (0, 1)]
Y_GROUPS = [[device_of(y, x, c) for y in range(NY)] for x in range(NX) for c in (0, 1)]
CORE_SWAP = [(d, d ^ 1) for d in range(SEQ)]
CORE_UP = [(d, d + 1) for d in range(0, SEQ, 2)]
CORE_DOWN = [(d + 1, d) for d in range(0, SEQ, 2)]


def cmul(a, b):
    return (a[0] * b[0] - a[1] * b[1], a[0] * b[1] + a[1] * b[0])


def masks():
    row = lax.broadcasted_iota(jnp.int32, (ROWS, ROWS), 0)
    col = lax.broadcasted_iota(jnp.int32, (ROWS, ROWS), 1)
    return row, col


def scores_of(q, k):
    return lax.dot_general(q, k, (((1,), (1,)), ((), ())), preferred_element_type=F32)


def softmax_parts(parts, vals, top):
    weights = [jnp.exp2((s - top) * SCALE2) for s in parts]
    total = jnp.sum(functools.reduce(jnp.add, weights), axis=1, keepdims=True)
    mixed = [jnp.dot(w.astype(jnp.bfloat16), v, preferred_element_type=F32) for w, v in zip(weights, vals)]
    return total, functools.reduce(jnp.add, mixed)


def merged(parts, vals, top_in, total_in, mixed_in):
    top = jnp.max(functools.reduce(jnp.maximum, parts), axis=1, keepdims=True)
    top = jnp.maximum(top_in, jnp.broadcast_to(top, (ROWS, HD)))
    total, mixed = softmax_parts(parts, vals, jnp.concatenate([top] * (ROWS // HD), axis=1))
    shrink = jnp.exp2((top_in - top) * SCALE2)
    return top, total_in * shrink + jnp.broadcast_to(total, (ROWS, HD)), mixed_in * shrink + mixed


def fetch(pos_ref, pairs, slots, sems):
    first_core = pos_ref[3] == 0
    for core in (0, 1):
        @pl.when(first_core if core == 0 else jnp.logical_not(first_core))
        def _():
            for i, pair in enumerate(pairs):
                pltpu.make_async_copy(pair[core], slots.at[i], sems.at[i]).start()


def arrived(pairs, slots, sems):
    for i, pair in enumerate(pairs):
        pltpu.make_async_copy(pair[0], slots.at[i], sems.at[i]).wait()


def near_kernel(
    pos_ref, q_ref, after, own, two0, two1, low, high, top_ref, total_ref, mixed_ref, slots, sems
):
    pairs = ((own, own), (two0, two1), (high, low))
    fetch(pos_ref, pairs, slots, sems)
    row, col = masks()
    there = pos_ref[0] == 1
    arrived(pairs, slots, sems)
    for head in range(q_ref.shape[1] // HD):
        lanes = pl.ds(head * HD, HD)
        q = q_ref[:, lanes]
        parts = [scores_of(q, slots[i, 0, :, lanes]) for i in range(3)]
        parts = [jnp.where(col <= row, parts[0], NEG)] + [jnp.where(there, part, NEG) for part in parts[1:]]
        top = jnp.max(functools.reduce(jnp.maximum, parts), axis=1, keepdims=True)
        total, mixed = softmax_parts(parts, [slots[i, 1, :, lanes] for i in range(3)], top)
        top_ref[:, lanes] = jnp.broadcast_to(top, (ROWS, HD))
        total_ref[:, lanes] = jnp.broadcast_to(total, (ROWS, HD))
        mixed_ref[:, lanes] = mixed


def far_kernel(
    pos_ref, q_ref, top_in, total_in, mixed_in, far0, far1, up, down, o_ref, wide_ref, ssq_ref, slots, sems
):
    pairs = ((far0, far1), (down, up))
    fetch(pos_ref, pairs, slots, sems)
    row, col = masks()
    there = pos_ref[2] == 1
    low = row - jnp.where(pos_ref[1] == 1, 0, -2 * ROWS)
    square = None
    arrived(pairs, slots, sems)
    for head in range(q_ref.shape[1] // HD):
        lanes = pl.ds(head * HD, HD)
        q = q_ref[:, lanes]
        parts = [
            jnp.where(col > low, scores_of(q, slots[0, 0, :, lanes]), NEG),
            jnp.where(there, scores_of(q, slots[1, 0, :, lanes]), NEG),
        ]
        _, total, mixed = merged(
            parts, [slots[i, 1, :, lanes] for i in (0, 1)], top_in[:, lanes], total_in[:, lanes], mixed_in[:, lanes]
        )
        out = (mixed / total).astype(jnp.bfloat16)
        o_ref[:, lanes] = out
        wide = out.astype(F32)
        wide_ref[head] = wide
        square = wide * wide if square is None else square + wide * wide
    ssq_ref[...] = jnp.sum(jnp.transpose(square), axis=0, keepdims=True)


def gate_kernel(*refs):
    pass


def gate(value, *after):
    place = pl.BlockSpec(memory_space=pl.ANY)
    return pl.pallas_call(
        gate_kernel,
        in_specs=[place] * (1 + len(after)),
        out_specs=place,
        out_shape=jax.ShapeDtypeStruct(value.shape, value.dtype),
        input_output_aliases={0: 0},
        compiler_params=pltpu.CompilerParams(vmem_limit_bytes=2**20),
        name="gate",
    )(value, *after)


def attention_call(kernel, name, share, operands, outs, placed):
    scalars = 1
    kept = len(operands) - scalars - placed
    block = (share,) + operands[-1].shape
    return pl.pallas_call(
        kernel,
        in_specs=[pl.BlockSpec(memory_space=pltpu.SMEM)] * scalars
        + [pl.BlockSpec()] * kept
        + [pl.BlockSpec(memory_space=pl.ANY)] * placed,
        out_shape=outs,
        scratch_shapes=[pltpu.VMEM(block, jnp.bfloat16), pltpu.SemaphoreType.DMA((share,))],
        compiler_params=pltpu.CompilerParams(vmem_limit_bytes=12 * 2**20),
        cost_estimate=pl.CostEstimate(
            flops=170_000_000 * share, bytes_accessed=3_000_000, transcendentals=330_000 * share
        ),
        name=name,
    )(*operands)


def one_less_exp(v):
    series = 1.0 / 720.0
    for order in (120.0, 24.0, 6.0, 2.0, 1.0):
        series = 1.0 / order - v * series
    return jnp.where(v < 0.25, v * series, 1.0 - jnp.exp(-v))


def tables_kernel(
    decay_ref, gain_ref, coef_ref, cos_ref, sin_ref, after_ref, w_ref, fall_ref, fade_ref, kern_ref, total_ref, cb_ref,
    pass_re, pass_im
):
    gain = gain_ref[...]
    cum = jnp.zeros((NBLK, HD), F32)
    for r in range(BLK):
        step = decay_ref[pl.ds(r, NBLK, stride=BLK), :]
        cum = cum + step
        w_ref[r] = jnp.exp(cum) * (gain * jnp.sqrt(one_less_exp(2.0 * step)))
        fall_ref[r] = jnp.exp(-cum)
    fade_ref[...] = jnp.exp(-cum)
    total_ref[...] = jnp.sum(cum, axis=0, keepdims=True)
    z = cmul((coef_ref[2], coef_ref[3]), (coef_ref[0], coef_ref[1]))
    cb_ref[0], cb_ref[1] = z
    rot = (cos_ref[0], sin_ref[0])
    for lag in range(BLK):
        kern_ref[pl.ds(lag, 1), :] = jnp.sum(z[0], axis=0, keepdims=True)
        z = cmul(z, rot)
    moved = (jnp.ones((MODES, HD), F32), jnp.zeros((MODES, HD), F32))
    rot16 = (cos_ref[1], sin_ref[1])
    for j in range(NBLK):
        at = pl.ds(j, MODES, stride=NBLK)
        pass_re[0, at, :] = moved[0]
        pass_im[0, at, :] = moved[1]
        fade = fade_ref[pl.ds(j, 1), :]
        moved = tuple(fade * part for part in cmul(moved, rot16))


def tables(decay, gain, mode_coeffs, cos, sin, after):
    width = decay.shape[1]
    tokens = pl.BlockSpec((ROWS, HD), lambda h: (0, h))
    cube = pl.BlockSpec((BLK, NBLK, HD), lambda h: (0, 0, h))
    flat = pl.BlockSpec((NBLK, HD), lambda h: (0, h))
    line = pl.BlockSpec((1, HD), lambda h: (0, h))
    deep = pl.BlockSpec((1, MODES * NBLK, HD), lambda h: (h, 0, 0))
    return pl.pallas_call(
        tables_kernel,
        grid=(width // HD,),
        in_specs=[
            tokens,
            line,
            pl.BlockSpec((4, MODES, HD), lambda h: (0, 0, h)),
            pl.BlockSpec((2, MODES, HD), lambda h: (0, 0, h)),
            pl.BlockSpec((2, MODES, HD), lambda h: (0, 0, h)),
            pl.BlockSpec(memory_space=pl.ANY),
        ],
        out_specs=[cube, cube, flat, flat, line, pl.BlockSpec((2, MODES, HD), lambda h: (0, 0, h)), deep, deep],
        out_shape=[
            jax.ShapeDtypeStruct((BLK, NBLK, width), F32),
            jax.ShapeDtypeStruct((BLK, NBLK, width), F32),
            jax.ShapeDtypeStruct((NBLK, width), F32),
            jax.ShapeDtypeStruct((BLK, width), F32),
            jax.ShapeDtypeStruct((1, width), F32),
            jax.ShapeDtypeStruct((2, MODES, width), F32),
            jax.ShapeDtypeStruct((width // HD, MODES * NBLK, HD), F32),
            jax.ShapeDtypeStruct((width // HD, MODES * NBLK, HD), F32),
        ],
        compiler_params=pltpu.CompilerParams(vmem_limit_bytes=8 * 2**20),
        cost_estimate=pl.CostEstimate(flops=4000000, bytes_accessed=4000000, transcendentals=0),
        name="tables",
    )(decay, gain, mode_coeffs, cos, sin, after)


def chain_step(state, rot16, fade_row, end):
    turned = cmul(state, rot16)
    return (fade_row * turned[0] + end[0], fade_row * turned[1] + end[1])


def ends_kernel(
    wide_ref, w_ref, ssq_ref, cos_ref, sin_ref, fade_ref, total_ref, cb_ref, g_ref, st_re, st_im, sum_ref, scale, end_re,
    end_im
):
    heads = wide_ref.shape[0]
    row_scale = lax.rsqrt(jnp.sum(ssq_ref[...], axis=0, keepdims=True) * (1.0 / EMBED_DIMENSION) + 1e-06)
    scale[...] = jnp.transpose(jnp.broadcast_to(row_scale, (HD, ROWS)))
    group = 4
    for tile in range(heads):
        lanes = pl.ds(tile * HD, HD)
        for r in range(BLK):
            tokens = pl.ds(r, NBLK, stride=BLK)
            g_ref[r, :, lanes] = wide_ref[tile, tokens, :] * w_ref[r, :, lanes] * scale[tokens, :]
        fade = fade_ref[:, lanes]
        for base in range(0, MODES, group):
            modes = range(base, base + group)
            cos = [cos_ref[0, pl.ds(m, 1), lanes] for m in modes]
            twice = [jnp.broadcast_to(2.0 * c, (NBLK, HD)) for c in cos]
            first = g_ref[0, :, lanes]
            older = [first] * group
            second = g_ref[1, :, lanes]
            newer = [twice[i] * first + second for i in range(group)]
            for r in range(2, BLK):
                term = g_ref[r, :, lanes]
                for i in range(group):
                    older[i], newer[i] = newer[i], twice[i] * newer[i] + (term - older[i])
            for i, m in enumerate(modes):
                sin = sin_ref[0, pl.ds(m, 1), lanes]
                end_re[tile, pl.ds(m * NBLK, NBLK), :] = fade * (newer[i] - cos[i] * older[i])
                end_im[tile, pl.ds(m * NBLK, NBLK), :] = fade * (sin * older[i])
    states = [None] * heads
    for j in range(NBLK):
        at = pl.ds(j, MODES, stride=NBLK)
        for tile in range(heads):
            lanes = pl.ds(tile * HD, HD)
            end = (end_re[tile, at, :], end_im[tile, at, :])
            if j == 0:
                st_re[tile, at, :] = jnp.zeros((MODES, HD), F32)
                st_im[tile, at, :] = jnp.zeros((MODES, HD), F32)
                states[tile] = end
            else:
                given = cmul(states[tile], (cb_ref[0, :, lanes], cb_ref[1, :, lanes]))
                st_re[tile, at, :] = given[0]
                st_im[tile, at, :] = given[1]
                rot16 = (cos_ref[1, :, lanes], sin_ref[1, :, lanes])
                states[tile] = chain_step(states[tile], rot16, fade_ref[pl.ds(j, 1), lanes], end)
    for tile in range(heads):
        lanes = pl.ds(tile * HD, HD)
        sum_ref[pl.ds(tile * 2 * MODES, MODES), :] = states[tile][0]
        sum_ref[pl.ds(tile * 2 * MODES + MODES, MODES), :] = states[tile][1]
        sum_ref[pl.ds(heads * 2 * MODES + tile, 1), :] = total_ref[:, lanes]
    used = heads * (2 * MODES + 1)
    sum_ref[pl.ds(used, sum_ref.shape[0] - used), :] = jnp.zeros((sum_ref.shape[0] - used, HD), F32)


def padded(rows):
    return -(-rows // 8) * 8


def block_ends(wide, w, ssq, cos, sin, fade, total, cb):
    width = w.shape[2]
    tiles = width // HD
    return pl.pallas_call(
        ends_kernel,
        out_shape=[
            jax.ShapeDtypeStruct((BLK, NBLK, width), F32),
            jax.ShapeDtypeStruct((tiles, MODES * NBLK, HD), F32),
            jax.ShapeDtypeStruct((tiles, MODES * NBLK, HD), F32),
            jax.ShapeDtypeStruct((padded(tiles * (2 * MODES + 1)), HD), F32),
        ],
        scratch_shapes=[pltpu.VMEM((ROWS, HD), F32)]
        + [pltpu.VMEM((tiles, MODES * NBLK, HD), F32)] * 2,
        compiler_params=pltpu.CompilerParams(vmem_limit_bytes=12 * 2**20),
        cost_estimate=pl.CostEstimate(flops=8_000_000, bytes_accessed=4_000_000, transcendentals=0),
        name="block_ends",
    )(wide, w, ssq, cos, sin, fade, total, cb)


def local_kernel(g_ref, kern_ref, out_ref):
    heads = g_ref.shape[2] // HD
    for tile in range(heads):
        lanes = pl.ds(tile * HD, HD)
        g = [g_ref[r, :, lanes] for r in range(BLK)]
        total = [None] * BLK
        for lag in range(BLK):
            k = jnp.broadcast_to(kern_ref[pl.ds(lag, 1), lanes], (NBLK, HD))
            for r in range(lag, BLK):
                term = k * g[r - lag]
                total[r] = term if total[r] is None else total[r] + term
        for r in range(BLK):
            out_ref[r, :, lanes] = total[r]


def local_part(g, kern):
    return pl.pallas_call(
        local_kernel,
        out_shape=jax.ShapeDtypeStruct(g.shape, F32),
        compiler_params=pltpu.CompilerParams(vmem_limit_bytes=12 * 2**20),
        cost_estimate=pl.CostEstimate(flops=3_000_000, bytes_accessed=1_300_000, transcendentals=0),
        name="local_part",
    )(g, kern)


def half_of(ref, tile, base=0):
    return (ref[pl.ds(base + tile * MODES, HALF), :], ref[pl.ds(base + tile * MODES + HALF, HALF), :])


def write_copies(ref, size, tiles, tile, value, decay):
    for copy in range(ref.shape[0] // size):
        base = copy * size
        ref[pl.ds(base + tile * MODES, HALF), :] = value[0]
        ref[pl.ds(base + tile * MODES + HALF, HALF), :] = value[1]
        ref[pl.ds(base + tiles * MODES + tile, 1), :] = decay


def clear_rest(ref, size, used):
    for copy in range(ref.shape[0] // size):
        ref[pl.ds(copy * size + used, size - used), :] = jnp.zeros((size - used, HD), F32)


def chip_kernel(pos_ref, own_ref, other_ref, cos_ref, sin_ref, out_ref):
    tiles = cos_ref.shape[2] // HD
    size = out_ref.shape[0] // NX
    core = pos_ref[3]
    first_core = core == 0
    half = pl.multiple_of(core * HALF, HALF)
    for tile in range(tiles):
        lanes = pl.ds(tile * HD, HD)
        rows = [pl.ds(pl.multiple_of(tile * 2 * MODES + i * MODES + half, HALF), HALF) for i in (0, 1)]
        own = [own_ref[at, :] for at in rows]
        other = [other_ref[at, :] for at in rows]
        at = pl.ds(tiles * 2 * MODES + tile, 1)
        own_decay, other_decay = own_ref[at, :], other_ref[at, :]
        fade = jnp.exp(-jnp.where(first_core, other_decay, own_decay))
        turn = [fade * ref[2, pl.ds(half, HALF), lanes] for ref in (cos_ref, sin_ref)]
        first = [jnp.where(first_core, own[i], other[i]) for i in (0, 1)]
        second = [jnp.where(first_core, other[i], own[i]) for i in (0, 1)]
        moved = cmul(first, turn)
        write_copies(
            out_ref, size, tiles, tile, [moved[i] + second[i] for i in (0, 1)], own_decay + other_decay
        )
    clear_rest(out_ref, size, tiles * (MODES + 1))


def chip_sum(pos, own, other, cos, sin):
    tiles = cos.shape[2] // HD
    return pl.pallas_call(
        chip_kernel,
        in_specs=[pl.BlockSpec(memory_space=pltpu.SMEM)] + [pl.BlockSpec()] * 4,
        out_shape=jax.ShapeDtypeStruct((NX * padded(tiles * (MODES + 1)), HD), F32),
        compiler_params=pltpu.CompilerParams(vmem_limit_bytes=4 * 2**20),
        cost_estimate=pl.CostEstimate(flops=100_000, bytes_accessed=300_000, transcendentals=640),
        name="chip_sum",
    )(pos, own, other, cos, sin)


def running(ref, size, tiles, tile, count, mine, step, state, turn):
    at = tiles * MODES + tile
    into = turned = None
    decay = jnp.zeros((1, HD), F32)
    zero = jnp.zeros((HALF, HD), F32)
    for k in range(count):
        if k:
            here = mine == k
            into = [jnp.where(here, state[i], into[i]) for i in (0, 1)]
            turned = [jnp.where(here, turn[i], turned[i]) for i in (0, 1)]
        else:
            into, turned = [zero, zero], list(turn)
        step_decay = ref[pl.ds(k * size + at, 1), :]
        fade = jnp.exp(-step_decay)
        moving = [fade * part for part in step]
        value = half_of(ref, tile, k * size)
        if k:
            moved = cmul(state, moving)
            state = [moved[i] + value[i] for i in (0, 1)]
        else:
            state = list(value)
        turn = cmul(turn, moving)
        decay = decay + step_decay
    return into, turned, state, decay


def row_kernel(pos_ref, chips_ref, cos_ref, sin_ref, row_ref, in_ref, turn_ref):
    tiles = in_ref.shape[0] // MODES
    size = chips_ref.shape[0] // NX
    half = pl.ds(pl.multiple_of(pos_ref[3] * HALF, HALF), HALF)
    one = (jnp.ones((HALF, HD), F32), jnp.zeros((HALF, HD), F32))
    for tile in range(tiles):
        lanes = pl.ds(tile * HD, HD)
        step = (cos_ref[3, half, lanes], sin_ref[3, half, lanes])
        into, turned, state, decay = running(chips_ref, size, tiles, tile, NX, pos_ref[4], step, None, one)
        write_copies(row_ref, size, tiles, tile, state, decay)
        for ref, value in ((in_ref, into), (turn_ref, turned)):
            ref[pl.ds(tile * MODES, HALF), :] = value[0]
            ref[pl.ds(tile * MODES + HALF, HALF), :] = value[1]
    clear_rest(row_ref, size, tiles * (MODES + 1))


def row_sum(pos, chips, cos, sin):
    tiles = cos.shape[2] // HD
    return pl.pallas_call(
        row_kernel,
        in_specs=[pl.BlockSpec(memory_space=pltpu.SMEM)] + [pl.BlockSpec()] * 3,
        out_shape=[
            jax.ShapeDtypeStruct((NY * padded(tiles * (MODES + 1)), HD), F32),
            jax.ShapeDtypeStruct((tiles * MODES, HD), F32),
            jax.ShapeDtypeStruct((tiles * MODES, HD), F32),
        ],
        compiler_params=pltpu.CompilerParams(vmem_limit_bytes=4 * 2**20),
        cost_estimate=pl.CostEstimate(flops=300_000, bytes_accessed=400_000, transcendentals=5000),
        name="row_sum",
    )(pos, chips, cos, sin)


def entry_kernel(pos_ref, rows_ref, in_ref, turn_ref, cos_ref, sin_ref, out_ref):
    tiles = in_ref.shape[0] // MODES
    size = rows_ref.shape[0] // NY
    half = pl.ds(pl.multiple_of(pos_ref[3] * HALF, HALF), HALF)
    one = (jnp.ones((HALF, HD), F32), jnp.zeros((HALF, HD), F32))
    for tile in range(tiles):
        lanes = pl.ds(tile * HD, HD)
        step = (cos_ref[4, half, lanes], sin_ref[4, half, lanes])
        row, _, _, _ = running(rows_ref, size, tiles, tile, NY, pos_ref[5], step, None, one)
        moved = cmul(row, half_of(turn_ref, tile))
        into = half_of(in_ref, tile)
        out_ref[pl.ds(tile * MODES, HALF), :] = moved[0] + into[0]
        out_ref[pl.ds(tile * MODES + HALF, HALF), :] = moved[1] + into[1]


def chip_entry(pos, rows, into, turn, cos, sin):
    return pl.pallas_call(
        entry_kernel,
        in_specs=[pl.BlockSpec(memory_space=pltpu.SMEM)] + [pl.BlockSpec()] * 5,
        out_shape=jax.ShapeDtypeStruct(into.shape, F32),
        compiler_params=pltpu.CompilerParams(vmem_limit_bytes=4 * 2**20),
        cost_estimate=pl.CostEstimate(flops=300_000, bytes_accessed=400_000, transcendentals=5000),
        name="chip_entry",
    )(pos, rows, into, turn, cos, sin)


def gathered(copies, count, groups):
    parts = copies.reshape(count, copies.shape[0] // count, copies.shape[1])
    return lax.all_to_all(parts, "seq", 0, 0, axis_index_groups=groups).reshape(copies.shape)


def finish_kernel(
    pos_ref, mine_ref, theirs_ref, other_ref, st_re, st_im, pass_re, pass_im, local_ref, fall_ref, cos_ref, sin_ref,
    cb_ref, rec_ref, start, acc, out
):
    heads = rec_ref.shape[1] // HD
    first_core = pos_ref[3] == 0
    for tile in range(heads):
        lanes = pl.ds(tile * HD, HD)
        mine, theirs = half_of(mine_ref, tile), half_of(theirs_ref, tile)
        at_chip = [
            jnp.concatenate(
                [jnp.where(first_core, mine[i], theirs[i]), jnp.where(first_core, theirs[i], mine[i])], axis=0
            )
            for i in (0, 1)
        ]
        fade = jnp.exp(-other_ref[pl.ds(heads * 2 * MODES + tile, 1), :])
        moved = cmul(at_chip, [fade * ref[2, :, lanes] for ref in (cos_ref, sin_ref)])
        other = [other_ref[pl.ds(tile * 2 * MODES + i * MODES, MODES), :] for i in (0, 1)]
        state = [jnp.where(first_core, at_chip[i], moved[i] + other[i]) for i in (0, 1)]
        start[tile, 0], start[tile, 1] = cmul(state, (cb_ref[0, :, lanes], cb_ref[1, :, lanes]))
    group = 8
    for tile in range(heads):
        lanes = pl.ds(tile * HD, HD)
        for base in range(0, MODES, group):
            older, newer, twice = [], [], []
            for m in range(base, base + group):
                at = pl.ds(m * NBLK, NBLK)
                own = pl.ds(m, 1)
                moved = cmul((pass_re[tile, at, :], pass_im[tile, at, :]), (start[tile, 0, own, :], start[tile, 1, own, :]))
                z = (st_re[tile, at, :] + moved[0], st_im[tile, at, :] + moved[1])
                cos = cos_ref[0, own, lanes]
                older.append(z[0])
                newer.append(cos * z[0] - sin_ref[0, own, lanes] * z[1])
                twice.append(jnp.broadcast_to(2.0 * cos, (NBLK, HD)))
            for r in range(BLK):
                if r > 0:
                    for i in range(group):
                        older[i], newer[i] = newer[i], twice[i] * newer[i] - older[i]
                total = functools.reduce(jnp.add, newer)
                if base == 0:
                    acc[r] = local_ref[r, :, lanes] + total
                else:
                    out[tile, pl.ds(r, NBLK, stride=BLK), :] = (acc[r] + total) * fall_ref[r, :, lanes]
        rec_ref[:, lanes] = out[tile]


def finish(pos, mine, theirs, other, states, passing, local, fall, cos, sin, cb):
    width = fall.shape[2]
    tiles = width // HD
    return pl.pallas_call(
        finish_kernel,
        in_specs=[pl.BlockSpec(memory_space=pltpu.SMEM)] + [pl.BlockSpec()] * 12,
        out_shape=jax.ShapeDtypeStruct((ROWS, width), F32),
        scratch_shapes=[
            pltpu.VMEM((tiles, 2, MODES, HD), F32),
            pltpu.VMEM((BLK, NBLK, HD), F32),
            pltpu.VMEM((tiles, ROWS, HD), F32),
        ],
        compiler_params=pltpu.CompilerParams(vmem_limit_bytes=12 * 2**20),
        cost_estimate=pl.CostEstimate(flops=8_000_000, bytes_accessed=5_000_000, transcendentals=0),
        name="finish",
    )(pos, mine, theirs, other, *states, *passing, local, fall, cos, sin, cb)


def shards(queries, keys, values, decay, gain, theta, mode_coeffs):
    width = queries.shape[1]
    me = lax.axis_index("seq")
    core = me % 2
    chip = me // 2

    own = jnp.stack([keys, values])
    two1 = lax.ppermute(own, "seq", chip_pairs(0, 1, (1,)))
    hop = lax.ppermute(own, "seq", two_back(0))
    up = lax.ppermute(own, "seq", CORE_UP)
    angles = jnp.asarray(TURNS, F32)[:, None, None] * theta[None]
    cos, sin = jnp.cos(angles), jnp.sin(angles)
    own_later, cos = lax.optimization_barrier((own, cos))
    two0 = lax.ppermute(own_later, "seq", chip_pairs(0, 1, (0,)))

    pos = jnp.stack(
        [
            (me >= 2).astype(jnp.int32),
            (me >= 4).astype(jnp.int32),
            ((me >= 3) | (core == 1)).astype(jnp.int32),
            core.astype(jnp.int32),
            (chip % NX).astype(jnp.int32),
            (chip // NX).astype(jnp.int32),
        ]
    )
    flat = jax.ShapeDtypeStruct(queries.shape, F32)
    far1 = lax.ppermute(two1, "seq", chip_pairs(0, 1, (1,)))
    high = lax.ppermute(two1, "seq", CORE_DOWN)
    made = tables(decay, gain[None, :], mode_coeffs, cos, sin, own)
    w, fall, fade, kern, total, cb, *passing = made
    two0 = gate(two0, high, hop, up, total)
    far0 = lax.ppermute(hop, "seq", two_back(1))
    low = lax.ppermute(two0, "seq", CORE_UP)
    run = attention_call(
        near_kernel, "attention_near", 3, [pos, queries, total, own, two0, two1, low, high], [flat] * 3, placed=6
    )
    down = lax.ppermute(gate(far1, far0), "seq", CORE_DOWN)
    attn, wide, ssq = attention_call(
        far_kernel,
        "attention_far",
        2,
        [pos, queries, *run, far0, far1, up, down],
        [
            jax.ShapeDtypeStruct(queries.shape, jnp.bfloat16),
            jax.ShapeDtypeStruct((queries.shape[1] // HD, ROWS, HD), F32),
            jax.ShapeDtypeStruct((1, ROWS), F32),
        ],
        placed=4,
    )

    ssq_all = lax.all_to_all(jnp.broadcast_to(ssq, (NZ, ROWS)), "mp", 0, 0)

    g, *states, dev_sum = block_ends(wide, w, ssq_all, cos, sin, fade, total, cb)
    local = local_part(g, kern)

    other = lax.ppermute(dev_sum, "seq", CORE_SWAP)
    chips = gathered(chip_sum(pos, dev_sum, other, cos, sin), NX, X_GROUPS)
    row, into, turn = row_sum(pos, chips, cos, sin)
    rows = gathered(row, NY, Y_GROUPS)
    mine = chip_entry(pos, rows, into, turn, cos, sin)
    theirs = lax.ppermute(mine, "seq", CORE_SWAP)

    rec = finish(pos, mine, theirs, other, states, passing, local, fall, cos, sin, cb)
    return (attn, rec)


def solution(mesh):
    placed = (
        P("seq", "mp"),
        P("seq", "mp"),
        P("seq", "mp"),
        P("seq", "mp"),
        P("mp"),
        P(None, "mp"),
        P(None, None, "mp"),
    )
    return jax.shard_map(
        shards,
        mesh=mesh,
        in_specs=placed,
        out_specs=(P("seq", "mp"), P("seq", "mp")),
        check_vma=False,
    )
```

```python
import functools
import math

import jax
import jax.numpy as jnp
from jax import lax
from jax.experimental import pallas as pl
from jax.experimental.pallas import tpu as pltpu
from jax.sharding import PartitionSpec as P

HD = 128
EMBED_DIMENSION = 5120
MODES = 16
HALF = MODES // 2
ROWS = 256
BLK = 16
NBLK = ROWS // BLK
NX = 4
NY = 4
NZ = 8
SEQ = 32
NEG = -1e30
SCALE2 = math.log2(math.e) / math.sqrt(HD)
F32 = jnp.float32
TURNS = (1, BLK, ROWS, 2 * ROWS, 2 * NX * ROWS)


def device_of(y, x, core):
    return (y * NX + x) * 2 + core


def chip_pairs(dy, dx, cores=(0, 1)):
    pairs = []
    for chip in range(NX * NY):
        target = chip + dy * NX + dx
        if 0 <= target < NX * NY:
            pairs += [(chip * 2 + c, target * 2 + c) for c in cores]
    return pairs


def two_back(hop):
    pairs = []
    for chip in range(NX * NY - 2):
        y, x = divmod(chip, NX)
        middle = device_of(y + (x == 2), (x - 1) % NX, 0)
        pairs.append((chip * 2, middle) if hop == 0 else (middle, (chip + 2) * 2))
    return pairs


X_GROUPS = [[device_of(y, x, c) for x in range(NX)] for y in range(NY) for c in (0, 1)]
Y_GROUPS = [[device_of(y, x, c) for y in range(NY)] for x in range(NX) for c in (0, 1)]
CORE_SWAP = [(d, d ^ 1) for d in range(SEQ)]
CORE_UP = [(d, d + 1) for d in range(0, SEQ, 2)]
CORE_DOWN = [(d + 1, d) for d in range(0, SEQ, 2)]


def cmul(a, b):
    return (a[0] * b[0] - a[1] * b[1], a[0] * b[1] + a[1] * b[0])


def masks():
    row = lax.broadcasted_iota(jnp.int32, (ROWS, ROWS), 0)
    col = lax.broadcasted_iota(jnp.int32, (ROWS, ROWS), 1)
    return row, col


def scores_of(q, k):
    return lax.dot_general(q, k, (((1,), (1,)), ((), ())), preferred_element_type=F32)


def softmax_parts(parts, vals, top):
    weights = [jnp.exp2((s - top) * SCALE2) for s in parts]
    total = jnp.sum(functools.reduce(jnp.add, weights), axis=1, keepdims=True)
    mixed = [jnp.dot(w.astype(jnp.bfloat16), v, preferred_element_type=F32) for w, v in zip(weights, vals)]
    return total, functools.reduce(jnp.add, mixed)


def merged(parts, vals, top_in, total_in, mixed_in):
    top = jnp.max(functools.reduce(jnp.maximum, parts), axis=1, keepdims=True)
    top = jnp.maximum(top_in, jnp.broadcast_to(top, (ROWS, HD)))
    total, mixed = softmax_parts(parts, vals, jnp.concatenate([top] * (ROWS // HD), axis=1))
    shrink = jnp.exp2((top_in - top) * SCALE2)
    return top, total_in * shrink + jnp.broadcast_to(total, (ROWS, HD)), mixed_in * shrink + mixed


def fetch(pos_ref, pairs, slots, sems):
    first_core = pos_ref[3] == 0
    for core in (0, 1):
        @pl.when(first_core if core == 0 else jnp.logical_not(first_core))
        def _():
            for head in range(sems.shape[1]):
                lanes = pl.ds(head * HD, HD)
                for i, pair in enumerate(pairs):
                    source, place = pair[core].at[:, :, lanes], slots.at[i, :, :, lanes]
                    pltpu.make_async_copy(source, place, sems.at[i, head]).start()


def arrived(pairs, slots, sems, head):
    lanes = pl.ds(head * HD, HD)
    for i, pair in enumerate(pairs):
        source, place = pair[0].at[:, :, lanes], slots.at[i, :, :, lanes]
        pltpu.make_async_copy(source, place, sems.at[i, head]).wait()


def near_kernel(
    pos_ref, q_ref, after, own, two0, two1, low, high, top_ref, total_ref, mixed_ref, slots, sems
):
    pairs = ((own, own), (two0, two1), (high, low))
    fetch(pos_ref, pairs, slots, sems)
    row, col = masks()
    there = pos_ref[0] == 1
    for head in range(q_ref.shape[1] // HD):
        lanes = pl.ds(head * HD, HD)
        arrived(pairs, slots, sems, head)
        q = q_ref[:, lanes]
        parts = [scores_of(q, slots[i, 0, :, lanes]) for i in range(3)]
        parts = [jnp.where(col <= row, parts[0], NEG)] + [jnp.where(there, part, NEG) for part in parts[1:]]
        top = jnp.max(functools.reduce(jnp.maximum, parts), axis=1, keepdims=True)
        total, mixed = softmax_parts(parts, [slots[i, 1, :, lanes] for i in range(3)], top)
        top_ref[:, lanes] = jnp.broadcast_to(top, (ROWS, HD))
        total_ref[:, lanes] = jnp.broadcast_to(total, (ROWS, HD))
        mixed_ref[:, lanes] = mixed


def far_kernel(
    pos_ref, q_ref, top_in, total_in, mixed_in, far0, far1, up, down, o_ref, wide_ref, ssq_ref, slots, sems
):
    pairs = ((far0, far1), (down, up))
    fetch(pos_ref, pairs, slots, sems)
    row, col = masks()
    there = pos_ref[2] == 1
    low = row - jnp.where(pos_ref[1] == 1, 0, -2 * ROWS)
    square = None
    for head in range(q_ref.shape[1] // HD):
        lanes = pl.ds(head * HD, HD)
        arrived(pairs, slots, sems, head)
        q = q_ref[:, lanes]
        parts = [
            jnp.where(col > low, scores_of(q, slots[0, 0, :, lanes]), NEG),
            jnp.where(there, scores_of(q, slots[1, 0, :, lanes]), NEG),
        ]
        _, total, mixed = merged(
            parts, [slots[i, 1, :, lanes] for i in (0, 1)], top_in[:, lanes], total_in[:, lanes], mixed_in[:, lanes]
        )
        out = (mixed / total).astype(jnp.bfloat16)
        o_ref[:, lanes] = out
        wide = out.astype(F32)
        wide_ref[head] = wide
        square = wide * wide if square is None else square + wide * wide
    ssq_ref[...] = jnp.sum(jnp.transpose(square), axis=0, keepdims=True)


def gate_kernel(*refs):
    pass


def gate(value, *after):
    place = pl.BlockSpec(memory_space=pl.ANY)
    return pl.pallas_call(
        gate_kernel,
        in_specs=[place] * (1 + len(after)),
        out_specs=place,
        out_shape=jax.ShapeDtypeStruct(value.shape, value.dtype),
        input_output_aliases={0: 0},
        compiler_params=pltpu.CompilerParams(vmem_limit_bytes=2**20),
        name="gate",
    )(value, *after)


def attention_call(kernel, name, share, operands, outs, placed):
    scalars = 1
    kept = len(operands) - scalars - placed
    block = (share,) + operands[-1].shape
    return pl.pallas_call(
        kernel,
        in_specs=[pl.BlockSpec(memory_space=pltpu.SMEM)] * scalars
        + [pl.BlockSpec()] * kept
        + [pl.BlockSpec(memory_space=pl.ANY)] * placed,
        out_shape=outs,
        scratch_shapes=[pltpu.VMEM(block, jnp.bfloat16), pltpu.SemaphoreType.DMA((share, block[-1] // HD))],
        compiler_params=pltpu.CompilerParams(vmem_limit_bytes=12 * 2**20),
        cost_estimate=pl.CostEstimate(
            flops=170_000_000 * share, bytes_accessed=3_000_000, transcendentals=330_000 * share
        ),
        name=name,
    )(*operands)


def one_less_exp(v):
    series = 1.0 / 720.0
    for order in (120.0, 24.0, 6.0, 2.0, 1.0):
        series = 1.0 / order - v * series
    return jnp.where(v < 0.25, v * series, 1.0 - jnp.exp(-v))


def tables_kernel(
    decay_ref, gain_ref, coef_ref, cos_ref, sin_ref, after_ref, w_ref, fall_ref, fade_ref, kern_ref, total_ref, cb_ref,
    pass_re, pass_im
):
    gain = gain_ref[...]
    cum = jnp.zeros((NBLK, HD), F32)
    for r in range(BLK):
        step = decay_ref[pl.ds(r, NBLK, stride=BLK), :]
        cum = cum + step
        w_ref[r] = jnp.exp(cum) * (gain * jnp.sqrt(one_less_exp(2.0 * step)))
        fall_ref[r] = jnp.exp(-cum)
    fade_ref[...] = jnp.exp(-cum)
    total_ref[...] = jnp.sum(cum, axis=0, keepdims=True)
    z = cmul((coef_ref[2], coef_ref[3]), (coef_ref[0], coef_ref[1]))
    cb_ref[0], cb_ref[1] = z
    rot = (cos_ref[0], sin_ref[0])
    for lag in range(BLK):
        kern_ref[pl.ds(lag, 1), :] = jnp.sum(z[0], axis=0, keepdims=True)
        z = cmul(z, rot)
    moved = (jnp.ones((MODES, HD), F32), jnp.zeros((MODES, HD), F32))
    rot16 = (cos_ref[1], sin_ref[1])
    for j in range(NBLK):
        at = pl.ds(j, MODES, stride=NBLK)
        pass_re[0, at, :] = moved[0]
        pass_im[0, at, :] = moved[1]
        fade = fade_ref[pl.ds(j, 1), :]
        moved = tuple(fade * part for part in cmul(moved, rot16))


def tables(decay, gain, mode_coeffs, cos, sin, after):
    width = decay.shape[1]
    tokens = pl.BlockSpec((ROWS, HD), lambda h: (0, h))
    cube = pl.BlockSpec((BLK, NBLK, HD), lambda h: (0, 0, h))
    flat = pl.BlockSpec((NBLK, HD), lambda h: (0, h))
    line = pl.BlockSpec((1, HD), lambda h: (0, h))
    deep = pl.BlockSpec((1, MODES * NBLK, HD), lambda h: (h, 0, 0))
    return pl.pallas_call(
        tables_kernel,
        grid=(width // HD,),
        in_specs=[
            tokens,
            line,
            pl.BlockSpec((4, MODES, HD), lambda h: (0, 0, h)),
            pl.BlockSpec((2, MODES, HD), lambda h: (0, 0, h)),
            pl.BlockSpec((2, MODES, HD), lambda h: (0, 0, h)),
            pl.BlockSpec(memory_space=pl.ANY),
        ],
        out_specs=[cube, cube, flat, flat, line, pl.BlockSpec((2, MODES, HD), lambda h: (0, 0, h)), deep, deep],
        out_shape=[
            jax.ShapeDtypeStruct((BLK, NBLK, width), F32),
            jax.ShapeDtypeStruct((BLK, NBLK, width), F32),
            jax.ShapeDtypeStruct((NBLK, width), F32),
            jax.ShapeDtypeStruct((BLK, width), F32),
            jax.ShapeDtypeStruct((1, width), F32),
            jax.ShapeDtypeStruct((2, MODES, width), F32),
            jax.ShapeDtypeStruct((width // HD, MODES * NBLK, HD), F32),
            jax.ShapeDtypeStruct((width // HD, MODES * NBLK, HD), F32),
        ],
        compiler_params=pltpu.CompilerParams(vmem_limit_bytes=8 * 2**20),
        cost_estimate=pl.CostEstimate(flops=4000000, bytes_accessed=4000000, transcendentals=0),
        name="tables",
    )(decay, gain, mode_coeffs, cos, sin, after)


def chain_step(state, rot16, fade_row, end):
    turned = cmul(state, rot16)
    return (fade_row * turned[0] + end[0], fade_row * turned[1] + end[1])


def ends_kernel(
    wide_ref, w_ref, ssq_ref, cos_ref, sin_ref, fade_ref, total_ref, cb_ref, g_ref, st_re, st_im, sum_ref, scale, end_re,
    end_im
):
    heads = wide_ref.shape[0]
    row_scale = lax.rsqrt(jnp.sum(ssq_ref[...], axis=0, keepdims=True) * (1.0 / EMBED_DIMENSION) + 1e-06)
    scale[...] = jnp.transpose(jnp.broadcast_to(row_scale, (HD, ROWS)))
    group = 4
    for tile in range(heads):
        lanes = pl.ds(tile * HD, HD)
        for r in range(BLK):
            tokens = pl.ds(r, NBLK, stride=BLK)
            g_ref[r, :, lanes] = wide_ref[tile, tokens, :] * w_ref[r, :, lanes] * scale[tokens, :]
        fade = fade_ref[:, lanes]
        for base in range(0, MODES, group):
            modes = range(base, base + group)
            cos = [cos_ref[0, pl.ds(m, 1), lanes] for m in modes]
            twice = [jnp.broadcast_to(2.0 * c, (NBLK, HD)) for c in cos]
            first = g_ref[0, :, lanes]
            older = [first] * group
            second = g_ref[1, :, lanes]
            newer = [twice[i] * first + second for i in range(group)]
            for r in range(2, BLK):
                term = g_ref[r, :, lanes]
                for i in range(group):
                    older[i], newer[i] = newer[i], twice[i] * newer[i] + (term - older[i])
            for i, m in enumerate(modes):
                sin = sin_ref[0, pl.ds(m, 1), lanes]
                end_re[tile, pl.ds(m * NBLK, NBLK), :] = fade * (newer[i] - cos[i] * older[i])
                end_im[tile, pl.ds(m * NBLK, NBLK), :] = fade * (sin * older[i])
    states = [None] * heads
    for j in range(NBLK):
        at = pl.ds(j, MODES, stride=NBLK)
        for tile in range(heads):
            lanes = pl.ds(tile * HD, HD)
            end = (end_re[tile, at, :], end_im[tile, at, :])
            if j == 0:
                st_re[tile, at, :] = jnp.zeros((MODES, HD), F32)
                st_im[tile, at, :] = jnp.zeros((MODES, HD), F32)
                states[tile] = end
            else:
                given = cmul(states[tile], (cb_ref[0, :, lanes], cb_ref[1, :, lanes]))
                st_re[tile, at, :] = given[0]
                st_im[tile, at, :] = given[1]
                rot16 = (cos_ref[1, :, lanes], sin_ref[1, :, lanes])
                states[tile] = chain_step(states[tile], rot16, fade_ref[pl.ds(j, 1), lanes], end)
    for tile in range(heads):
        lanes = pl.ds(tile * HD, HD)
        sum_ref[pl.ds(tile * 2 * MODES, MODES), :] = states[tile][0]
        sum_ref[pl.ds(tile * 2 * MODES + MODES, MODES), :] = states[tile][1]
        sum_ref[pl.ds(heads * 2 * MODES + tile, 1), :] = total_ref[:, lanes]
    used = heads * (2 * MODES + 1)
    sum_ref[pl.ds(used, sum_ref.shape[0] - used), :] = jnp.zeros((sum_ref.shape[0] - used, HD), F32)


def padded(rows):
    return -(-rows // 8) * 8


def block_ends(wide, w, ssq, cos, sin, fade, total, cb):
    width = w.shape[2]
    tiles = width // HD
    return pl.pallas_call(
        ends_kernel,
        out_shape=[
            jax.ShapeDtypeStruct((BLK, NBLK, width), F32),
            jax.ShapeDtypeStruct((tiles, MODES * NBLK, HD), F32),
            jax.ShapeDtypeStruct((tiles, MODES * NBLK, HD), F32),
            jax.ShapeDtypeStruct((padded(tiles * (2 * MODES + 1)), HD), F32),
        ],
        scratch_shapes=[pltpu.VMEM((ROWS, HD), F32)]
        + [pltpu.VMEM((tiles, MODES * NBLK, HD), F32)] * 2,
        compiler_params=pltpu.CompilerParams(vmem_limit_bytes=12 * 2**20),
        cost_estimate=pl.CostEstimate(flops=8_000_000, bytes_accessed=4_000_000, transcendentals=0),
        name="block_ends",
    )(wide, w, ssq, cos, sin, fade, total, cb)


def local_kernel(g_ref, kern_ref, out_ref):
    heads = g_ref.shape[2] // HD
    for tile in range(heads):
        lanes = pl.ds(tile * HD, HD)
        g = [g_ref[r, :, lanes] for r in range(BLK)]
        total = [None] * BLK
        for lag in range(BLK):
            k = jnp.broadcast_to(kern_ref[pl.ds(lag, 1), lanes], (NBLK, HD))
            for r in range(lag, BLK):
                term = k * g[r - lag]
                total[r] = term if total[r] is None else total[r] + term
        for r in range(BLK):
            out_ref[r, :, lanes] = total[r]


def local_part(g, kern):
    return pl.pallas_call(
        local_kernel,
        out_shape=jax.ShapeDtypeStruct(g.shape, F32),
        compiler_params=pltpu.CompilerParams(vmem_limit_bytes=12 * 2**20),
        cost_estimate=pl.CostEstimate(flops=3_000_000, bytes_accessed=1_300_000, transcendentals=0),
        name="local_part",
    )(g, kern)


def half_of(ref, tile, base=0):
    return (ref[pl.ds(base + tile * MODES, HALF), :], ref[pl.ds(base + tile * MODES + HALF, HALF), :])


def write_copies(ref, size, tiles, tile, value, decay):
    for copy in range(ref.shape[0] // size):
        base = copy * size
        ref[pl.ds(base + tile * MODES, HALF), :] = value[0]
        ref[pl.ds(base + tile * MODES + HALF, HALF), :] = value[1]
        ref[pl.ds(base + tiles * MODES + tile, 1), :] = decay


def clear_rest(ref, size, used):
    for copy in range(ref.shape[0] // size):
        ref[pl.ds(copy * size + used, size - used), :] = jnp.zeros((size - used, HD), F32)


def chip_kernel(pos_ref, own_ref, other_ref, cos_ref, sin_ref, out_ref):
    tiles = cos_ref.shape[2] // HD
    size = out_ref.shape[0] // NX
    core = pos_ref[3]
    first_core = core == 0
    half = pl.multiple_of(core * HALF, HALF)
    for tile in range(tiles):
        lanes = pl.ds(tile * HD, HD)
        rows = [pl.ds(pl.multiple_of(tile * 2 * MODES + i * MODES + half, HALF), HALF) for i in (0, 1)]
        own = [own_ref[at, :] for at in rows]
        other = [other_ref[at, :] for at in rows]
        at = pl.ds(tiles * 2 * MODES + tile, 1)
        own_decay, other_decay = own_ref[at, :], other_ref[at, :]
        fade = jnp.exp(-jnp.where(first_core, other_decay, own_decay))
        turn = [fade * ref[2, pl.ds(half, HALF), lanes] for ref in (cos_ref, sin_ref)]
        first = [jnp.where(first_core, own[i], other[i]) for i in (0, 1)]
        second = [jnp.where(first_core, other[i], own[i]) for i in (0, 1)]
        moved = cmul(first, turn)
        write_copies(
            out_ref, size, tiles, tile, [moved[i] + second[i] for i in (0, 1)], own_decay + other_decay
        )
    clear_rest(out_ref, size, tiles * (MODES + 1))


def chip_sum(pos, own, other, cos, sin):
    tiles = cos.shape[2] // HD
    return pl.pallas_call(
        chip_kernel,
        in_specs=[pl.BlockSpec(memory_space=pltpu.SMEM)] + [pl.BlockSpec()] * 4,
        out_shape=jax.ShapeDtypeStruct((NX * padded(tiles * (MODES + 1)), HD), F32),
        compiler_params=pltpu.CompilerParams(vmem_limit_bytes=4 * 2**20),
        cost_estimate=pl.CostEstimate(flops=100_000, bytes_accessed=300_000, transcendentals=640),
        name="chip_sum",
    )(pos, own, other, cos, sin)


def running(ref, size, tiles, tile, count, mine, step, state, turn):
    at = tiles * MODES + tile
    into = turned = None
    decay = jnp.zeros((1, HD), F32)
    zero = jnp.zeros((HALF, HD), F32)
    for k in range(count):
        if k:
            here = mine == k
            into = [jnp.where(here, state[i], into[i]) for i in (0, 1)]
            turned = [jnp.where(here, turn[i], turned[i]) for i in (0, 1)]
        else:
            into, turned = [zero, zero], list(turn)
        step_decay = ref[pl.ds(k * size + at, 1), :]
        fade = jnp.exp(-step_decay)
        moving = [fade * part for part in step]
        value = half_of(ref, tile, k * size)
        if k:
            moved = cmul(state, moving)
            state = [moved[i] + value[i] for i in (0, 1)]
        else:
            state = list(value)
        turn = cmul(turn, moving)
        decay = decay + step_decay
    return into, turned, state, decay


def row_kernel(pos_ref, chips_ref, cos_ref, sin_ref, row_ref, in_ref, turn_ref):
    tiles = in_ref.shape[0] // MODES
    size = chips_ref.shape[0] // NX
    half = pl.ds(pl.multiple_of(pos_ref[3] * HALF, HALF), HALF)
    one = (jnp.ones((HALF, HD), F32), jnp.zeros((HALF, HD), F32))
    for tile in range(tiles):
        lanes = pl.ds(tile * HD, HD)
        step = (cos_ref[3, half, lanes], sin_ref[3, half, lanes])
        into, turned, state, decay = running(chips_ref, size, tiles, tile, NX, pos_ref[4], step, None, one)
        write_copies(row_ref, size, tiles, tile, state, decay)
        for ref, value in ((in_ref, into), (turn_ref, turned)):
            ref[pl.ds(tile * MODES, HALF), :] = value[0]
            ref[pl.ds(tile * MODES + HALF, HALF), :] = value[1]
    clear_rest(row_ref, size, tiles * (MODES + 1))


def row_sum(pos, chips, cos, sin):
    tiles = cos.shape[2] // HD
    return pl.pallas_call(
        row_kernel,
        in_specs=[pl.BlockSpec(memory_space=pltpu.SMEM)] + [pl.BlockSpec()] * 3,
        out_shape=[
            jax.ShapeDtypeStruct((NY * padded(tiles * (MODES + 1)), HD), F32),
            jax.ShapeDtypeStruct((tiles * MODES, HD), F32),
            jax.ShapeDtypeStruct((tiles * MODES, HD), F32),
        ],
        compiler_params=pltpu.CompilerParams(vmem_limit_bytes=4 * 2**20),
        cost_estimate=pl.CostEstimate(flops=300_000, bytes_accessed=400_000, transcendentals=5000),
        name="row_sum",
    )(pos, chips, cos, sin)


def entry_kernel(pos_ref, rows_ref, in_ref, turn_ref, cos_ref, sin_ref, out_ref):
    tiles = in_ref.shape[0] // MODES
    size = rows_ref.shape[0] // NY
    half = pl.ds(pl.multiple_of(pos_ref[3] * HALF, HALF), HALF)
    one = (jnp.ones((HALF, HD), F32), jnp.zeros((HALF, HD), F32))
    for tile in range(tiles):
        lanes = pl.ds(tile * HD, HD)
        step = (cos_ref[4, half, lanes], sin_ref[4, half, lanes])
        row, _, _, _ = running(rows_ref, size, tiles, tile, NY, pos_ref[5], step, None, one)
        moved = cmul(row, half_of(turn_ref, tile))
        into = half_of(in_ref, tile)
        out_ref[pl.ds(tile * MODES, HALF), :] = moved[0] + into[0]
        out_ref[pl.ds(tile * MODES + HALF, HALF), :] = moved[1] + into[1]


def chip_entry(pos, rows, into, turn, cos, sin):
    return pl.pallas_call(
        entry_kernel,
        in_specs=[pl.BlockSpec(memory_space=pltpu.SMEM)] + [pl.BlockSpec()] * 5,
        out_shape=jax.ShapeDtypeStruct(into.shape, F32),
        compiler_params=pltpu.CompilerParams(vmem_limit_bytes=4 * 2**20),
        cost_estimate=pl.CostEstimate(flops=300_000, bytes_accessed=400_000, transcendentals=5000),
        name="chip_entry",
    )(pos, rows, into, turn, cos, sin)


def gathered(copies, count, groups):
    parts = copies.reshape(count, copies.shape[0] // count, copies.shape[1])
    return lax.all_to_all(parts, "seq", 0, 0, axis_index_groups=groups).reshape(copies.shape)


def finish_kernel(
    pos_ref, mine_ref, theirs_ref, other_ref, st_re, st_im, pass_re, pass_im, local_ref, fall_ref, cos_ref, sin_ref,
    cb_ref, rec_ref, start, acc, out
):
    heads = rec_ref.shape[1] // HD
    first_core = pos_ref[3] == 0
    for tile in range(heads):
        lanes = pl.ds(tile * HD, HD)
        mine, theirs = half_of(mine_ref, tile), half_of(theirs_ref, tile)
        at_chip = [
            jnp.concatenate(
                [jnp.where(first_core, mine[i], theirs[i]), jnp.where(first_core, theirs[i], mine[i])], axis=0
            )
            for i in (0, 1)
        ]
        fade = jnp.exp(-other_ref[pl.ds(heads * 2 * MODES + tile, 1), :])
        moved = cmul(at_chip, [fade * ref[2, :, lanes] for ref in (cos_ref, sin_ref)])
        other = [other_ref[pl.ds(tile * 2 * MODES + i * MODES, MODES), :] for i in (0, 1)]
        state = [jnp.where(first_core, at_chip[i], moved[i] + other[i]) for i in (0, 1)]
        start[tile, 0], start[tile, 1] = cmul(state, (cb_ref[0, :, lanes], cb_ref[1, :, lanes]))
    group = 8
    for tile in range(heads):
        lanes = pl.ds(tile * HD, HD)
        for base in range(0, MODES, group):
            older, newer, twice = [], [], []
            for m in range(base, base + group):
                at = pl.ds(m * NBLK, NBLK)
                own = pl.ds(m, 1)
                moved = cmul((pass_re[tile, at, :], pass_im[tile, at, :]), (start[tile, 0, own, :], start[tile, 1, own, :]))
                z = (st_re[tile, at, :] + moved[0], st_im[tile, at, :] + moved[1])
                cos = cos_ref[0, own, lanes]
                older.append(z[0])
                newer.append(cos * z[0] - sin_ref[0, own, lanes] * z[1])
                twice.append(jnp.broadcast_to(2.0 * cos, (NBLK, HD)))
            for r in range(BLK):
                if r > 0:
                    for i in range(group):
                        older[i], newer[i] = newer[i], twice[i] * newer[i] - older[i]
                total = functools.reduce(jnp.add, newer)
                if base == 0:
                    acc[r] = local_ref[r, :, lanes] + total
                else:
                    out[tile, pl.ds(r, NBLK, stride=BLK), :] = (acc[r] + total) * fall_ref[r, :, lanes]
        rec_ref[:, lanes] = out[tile]


def finish(pos, mine, theirs, other, states, passing, local, fall, cos, sin, cb):
    width = fall.shape[2]
    tiles = width // HD
    return pl.pallas_call(
        finish_kernel,
        in_specs=[pl.BlockSpec(memory_space=pltpu.SMEM)] + [pl.BlockSpec()] * 12,
        out_shape=jax.ShapeDtypeStruct((ROWS, width), F32),
        scratch_shapes=[
            pltpu.VMEM((tiles, 2, MODES, HD), F32),
            pltpu.VMEM((BLK, NBLK, HD), F32),
            pltpu.VMEM((tiles, ROWS, HD), F32),
        ],
        compiler_params=pltpu.CompilerParams(vmem_limit_bytes=12 * 2**20),
        cost_estimate=pl.CostEstimate(flops=8_000_000, bytes_accessed=5_000_000, transcendentals=0),
        name="finish",
    )(pos, mine, theirs, other, *states, *passing, local, fall, cos, sin, cb)


def shards(queries, keys, values, decay, gain, theta, mode_coeffs):
    width = queries.shape[1]
    me = lax.axis_index("seq")
    core = me % 2
    chip = me // 2

    own = jnp.stack([keys, values])
    two1 = lax.ppermute(own, "seq", chip_pairs(0, 1, (1,)))
    hop = lax.ppermute(own, "seq", two_back(0))
    up = lax.ppermute(own, "seq", CORE_UP)
    angles = jnp.asarray(TURNS, F32)[:, None, None] * theta[None]
    cos, sin = jnp.cos(angles), jnp.sin(angles)
    own_later, cos = lax.optimization_barrier((own, cos))
    two0 = lax.ppermute(own_later, "seq", chip_pairs(0, 1, (0,)))

    pos = jnp.stack(
        [
            (me >= 2).astype(jnp.int32),
            (me >= 4).astype(jnp.int32),
            ((me >= 3) | (core == 1)).astype(jnp.int32),
            core.astype(jnp.int32),
            (chip % NX).astype(jnp.int32),
            (chip // NX).astype(jnp.int32),
        ]
    )
    flat = jax.ShapeDtypeStruct(queries.shape, F32)
    far1 = lax.ppermute(two1, "seq", chip_pairs(0, 1, (1,)))
    high = lax.ppermute(two1, "seq", CORE_DOWN)
    made = tables(decay, gain[None, :], mode_coeffs, cos, sin, own)
    w, fall, fade, kern, total, cb, *passing = made
    two0 = gate(two0, high, hop, up, total)
    far0 = lax.ppermute(hop, "seq", two_back(1))
    low = lax.ppermute(two0, "seq", CORE_UP)
    run = attention_call(
        near_kernel, "attention_near", 3, [pos, queries, total, own, two0, two1, low, high], [flat] * 3, placed=6
    )
    far1 = gate(far1, far0)
    down = lax.ppermute(far1, "seq", CORE_DOWN)
    attn, wide, ssq = attention_call(
        far_kernel,
        "attention_far",
        2,
        [pos, queries, *run, far0, far1, up, down],
        [
            jax.ShapeDtypeStruct(queries.shape, jnp.bfloat16),
            jax.ShapeDtypeStruct((queries.shape[1] // HD, ROWS, HD), F32),
            jax.ShapeDtypeStruct((1, ROWS), F32),
        ],
        placed=4,
    )

    ssq_all = lax.all_to_all(jnp.broadcast_to(ssq, (NZ, ROWS)), "mp", 0, 0)

    g, *states, dev_sum = block_ends(wide, w, ssq_all, cos, sin, fade, total, cb)
    local = local_part(g, kern)

    other = lax.ppermute(dev_sum, "seq", CORE_SWAP)
    chips = gathered(chip_sum(pos, dev_sum, other, cos, sin), NX, X_GROUPS)
    row, into, turn = row_sum(pos, chips, cos, sin)
    rows = gathered(row, NY, Y_GROUPS)
    mine = chip_entry(pos, rows, into, turn, cos, sin)
    theirs = lax.ppermute(mine, "seq", CORE_SWAP)

    rec = finish(pos, mine, theirs, other, states, passing, local, fall, cos, sin, cb)
    return (attn, rec)


def solution(mesh):
    placed = (
        P("seq", "mp"),
        P("seq", "mp"),
        P("seq", "mp"),
        P("seq", "mp"),
        P("mp"),
        P(None, "mp"),
        P(None, None, "mp"),
    )
    return jax.shard_map(
        shards,
        mesh=mesh,
        in_specs=placed,
        out_specs=(P("seq", "mp"), P("seq", "mp")),
        check_vma=False,
    )
```

```python
import functools
import math

import jax
import jax.numpy as jnp
from jax import lax
from jax.experimental import pallas as pl
from jax.experimental.pallas import tpu as pltpu
from jax.sharding import PartitionSpec as P

HD = 128
EMBED_DIMENSION = 5120
MODES = 16
HALF = MODES // 2
ROWS = 256
BLK = 16
NBLK = ROWS // BLK
NX = 4
NY = 4
NZ = 8
SEQ = 32
NEG = -1e30
SCALE2 = math.log2(math.e) / math.sqrt(HD)
F32 = jnp.float32
TURNS = (1, BLK, ROWS, 2 * ROWS, 2 * NX * ROWS)


def device_of(y, x, core):
    return (y * NX + x) * 2 + core


def chip_pairs(dy, dx, cores=(0, 1)):
    pairs = []
    for chip in range(NX * NY):
        target = chip + dy * NX + dx
        if 0 <= target < NX * NY:
            pairs += [(chip * 2 + c, target * 2 + c) for c in cores]
    return pairs


def two_back(hop):
    pairs = []
    for chip in range(NX * NY - 2):
        y, x = divmod(chip, NX)
        middle = device_of(y + (x == 2), (x - 1) % NX, 0)
        pairs.append((chip * 2, middle) if hop == 0 else (middle, (chip + 2) * 2))
    return pairs


X_GROUPS = [[device_of(y, x, c) for x in range(NX)] for y in range(NY) for c in (0, 1)]
Y_GROUPS = [[device_of(y, x, c) for y in range(NY)] for x in range(NX) for c in (0, 1)]
CORE_SWAP = [(d, d ^ 1) for d in range(SEQ)]
CORE_UP = [(d, d + 1) for d in range(0, SEQ, 2)]
CORE_DOWN = [(d + 1, d) for d in range(0, SEQ, 2)]


def cmul(a, b):
    return (a[0] * b[0] - a[1] * b[1], a[0] * b[1] + a[1] * b[0])


def masks():
    row = lax.broadcasted_iota(jnp.int32, (ROWS, ROWS), 0)
    col = lax.broadcasted_iota(jnp.int32, (ROWS, ROWS), 1)
    return row, col


def scores_of(q, k):
    return lax.dot_general(q, k, (((1,), (1,)), ((), ())), preferred_element_type=F32)


def softmax_parts(parts, vals, top):
    weights = [jnp.exp2((s - top) * SCALE2) for s in parts]
    total = jnp.sum(functools.reduce(jnp.add, weights), axis=1, keepdims=True)
    mixed = [jnp.dot(w.astype(jnp.bfloat16), v, preferred_element_type=F32) for w, v in zip(weights, vals)]
    return total, functools.reduce(jnp.add, mixed)


def merged(parts, vals, top_in, total_in, mixed_in):
    top = jnp.max(functools.reduce(jnp.maximum, parts), axis=1, keepdims=True)
    top = jnp.maximum(top_in, jnp.broadcast_to(top, (ROWS, HD)))
    total, mixed = softmax_parts(parts, vals, jnp.concatenate([top] * (ROWS // HD), axis=1))
    shrink = jnp.exp2((top_in - top) * SCALE2)
    return top, total_in * shrink + jnp.broadcast_to(total, (ROWS, HD)), mixed_in * shrink + mixed


def fetch(pos_ref, pairs, slots, sems):
    first_core = pos_ref[3] == 0
    for core in (0, 1):
        @pl.when(first_core if core == 0 else jnp.logical_not(first_core))
        def _():
            for i, pair in enumerate(pairs):
                pltpu.make_async_copy(pair[core], slots.at[i], sems.at[i]).start()


def arrived(pairs, slots, sems):
    for i, pair in enumerate(pairs):
        pltpu.make_async_copy(pair[0], slots.at[i], sems.at[i]).wait()


def near_kernel(
    pos_ref, q_ref, own, after, two0, two1, low, high, top_ref, total_ref, mixed_ref, slots, sems
):
    pairs = ((two0, two1), (high, low))
    fetch(pos_ref, pairs, slots, sems)
    row, col = masks()
    there = pos_ref[0] == 1
    arrived(pairs, slots, sems)
    for head in range(q_ref.shape[1] // HD):
        lanes = pl.ds(head * HD, HD)
        q = q_ref[:, lanes]
        blocks = [own] + [slots.at[i] for i in (0, 1)]
        parts = [scores_of(q, block[0, :, lanes]) for block in blocks]
        parts = [jnp.where(col <= row, parts[0], NEG)] + [jnp.where(there, part, NEG) for part in parts[1:]]
        top = jnp.max(functools.reduce(jnp.maximum, parts), axis=1, keepdims=True)
        total, mixed = softmax_parts(parts, [block[1, :, lanes] for block in blocks], top)
        top_ref[:, lanes] = jnp.broadcast_to(top, (ROWS, HD))
        total_ref[:, lanes] = jnp.broadcast_to(total, (ROWS, HD))
        mixed_ref[:, lanes] = mixed


def far_kernel(
    pos_ref, q_ref, top_in, total_in, mixed_in, far0, far1, up, down, o_ref, wide_ref, ssq_ref, slots, sems
):
    pairs = ((far0, far1), (down, up))
    fetch(pos_ref, pairs, slots, sems)
    row, col = masks()
    there = pos_ref[2] == 1
    low = row - jnp.where(pos_ref[1] == 1, 0, -2 * ROWS)
    square = None
    arrived(pairs, slots, sems)
    for head in range(q_ref.shape[1] // HD):
        lanes = pl.ds(head * HD, HD)
        q = q_ref[:, lanes]
        parts = [
            jnp.where(col > low, scores_of(q, slots[0, 0, :, lanes]), NEG),
            jnp.where(there, scores_of(q, slots[1, 0, :, lanes]), NEG),
        ]
        _, total, mixed = merged(
            parts, [slots[i, 1, :, lanes] for i in (0, 1)], top_in[:, lanes], total_in[:, lanes], mixed_in[:, lanes]
        )
        out = (mixed / total).astype(jnp.bfloat16)
        o_ref[:, lanes] = out
        wide = out.astype(F32)
        wide_ref[head] = wide
        square = wide * wide if square is None else square + wide * wide
    ssq_ref[...] = jnp.sum(jnp.transpose(square), axis=0, keepdims=True)


def gate_kernel(*refs):
    pass


def gate(value, *after):
    place = pl.BlockSpec(memory_space=pl.ANY)
    return pl.pallas_call(
        gate_kernel,
        in_specs=[place] * (1 + len(after)),
        out_specs=place,
        out_shape=jax.ShapeDtypeStruct(value.shape, value.dtype),
        input_output_aliases={0: 0},
        compiler_params=pltpu.CompilerParams(vmem_limit_bytes=2**20),
        name="gate",
    )(value, *after)


def attention_call(kernel, name, share, operands, outs, placed):
    scalars = 1
    kept = len(operands) - scalars - placed
    block = (share,) + operands[-1].shape
    return pl.pallas_call(
        kernel,
        in_specs=[pl.BlockSpec(memory_space=pltpu.SMEM)] * scalars
        + [pl.BlockSpec()] * kept
        + [pl.BlockSpec(memory_space=pl.ANY)] * placed,
        out_shape=outs,
        scratch_shapes=[pltpu.VMEM(block, jnp.bfloat16), pltpu.SemaphoreType.DMA((share,))],
        compiler_params=pltpu.CompilerParams(vmem_limit_bytes=12 * 2**20),
        cost_estimate=pl.CostEstimate(
            flops=170_000_000 * share, bytes_accessed=3_000_000, transcendentals=330_000 * share
        ),
        name=name,
    )(*operands)


def one_less_exp(v):
    series = 1.0 / 720.0
    for order in (120.0, 24.0, 6.0, 2.0, 1.0):
        series = 1.0 / order - v * series
    return jnp.where(v < 0.25, v * series, 1.0 - jnp.exp(-v))


def tables_kernel(
    decay_ref, gain_ref, coef_ref, cos_ref, sin_ref, after_ref, w_ref, fall_ref, fade_ref, kern_ref, total_ref, cb_ref,
    pass_re, pass_im
):
    gain = gain_ref[...]
    cum = jnp.zeros((NBLK, HD), F32)
    for r in range(BLK):
        step = decay_ref[pl.ds(r, NBLK, stride=BLK), :]
        cum = cum + step
        w_ref[r] = jnp.exp(cum) * (gain * jnp.sqrt(one_less_exp(2.0 * step)))
        fall_ref[r] = jnp.exp(-cum)
    fade_ref[...] = jnp.exp(-cum)
    total_ref[...] = jnp.sum(cum, axis=0, keepdims=True)
    z = cmul((coef_ref[2], coef_ref[3]), (coef_ref[0], coef_ref[1]))
    cb_ref[0], cb_ref[1] = z
    rot = (cos_ref[0], sin_ref[0])
    for lag in range(BLK):
        kern_ref[pl.ds(lag, 1), :] = jnp.sum(z[0], axis=0, keepdims=True)
        z = cmul(z, rot)
    moved = (jnp.ones((MODES, HD), F32), jnp.zeros((MODES, HD), F32))
    rot16 = (cos_ref[1], sin_ref[1])
    for j in range(NBLK):
        at = pl.ds(j, MODES, stride=NBLK)
        pass_re[0, at, :] = moved[0]
        pass_im[0, at, :] = moved[1]
        fade = fade_ref[pl.ds(j, 1), :]
        moved = tuple(fade * part for part in cmul(moved, rot16))


def tables(decay, gain, mode_coeffs, cos, sin, after):
    width = decay.shape[1]
    tokens = pl.BlockSpec((ROWS, HD), lambda h: (0, h))
    cube = pl.BlockSpec((BLK, NBLK, HD), lambda h: (0, 0, h))
    flat = pl.BlockSpec((NBLK, HD), lambda h: (0, h))
    line = pl.BlockSpec((1, HD), lambda h: (0, h))
    deep = pl.BlockSpec((1, MODES * NBLK, HD), lambda h: (h, 0, 0))
    return pl.pallas_call(
        tables_kernel,
        grid=(width // HD,),
        in_specs=[
            tokens,
            line,
            pl.BlockSpec((4, MODES, HD), lambda h: (0, 0, h)),
            pl.BlockSpec((2, MODES, HD), lambda h: (0, 0, h)),
            pl.BlockSpec((2, MODES, HD), lambda h: (0, 0, h)),
            pl.BlockSpec(memory_space=pl.ANY),
        ],
        out_specs=[cube, cube, flat, flat, line, pl.BlockSpec((2, MODES, HD), lambda h: (0, 0, h)), deep, deep],
        out_shape=[
            jax.ShapeDtypeStruct((BLK, NBLK, width), F32),
            jax.ShapeDtypeStruct((BLK, NBLK, width), F32),
            jax.ShapeDtypeStruct((NBLK, width), F32),
            jax.ShapeDtypeStruct((BLK, width), F32),
            jax.ShapeDtypeStruct((1, width), F32),
            jax.ShapeDtypeStruct((2, MODES, width), F32),
            jax.ShapeDtypeStruct((width // HD, MODES * NBLK, HD), F32),
            jax.ShapeDtypeStruct((width // HD, MODES * NBLK, HD), F32),
        ],
        compiler_params=pltpu.CompilerParams(vmem_limit_bytes=8 * 2**20),
        cost_estimate=pl.CostEstimate(flops=4000000, bytes_accessed=4000000, transcendentals=0),
        name="tables",
    )(decay, gain, mode_coeffs, cos, sin, after)


def chain_step(state, rot16, fade_row, end):
    turned = cmul(state, rot16)
    return (fade_row * turned[0] + end[0], fade_row * turned[1] + end[1])


def ends_kernel(
    wide_ref, w_ref, ssq_ref, cos_ref, sin_ref, fade_ref, total_ref, cb_ref, g_ref, st_re, st_im, sum_ref, scale, end_re,
    end_im
):
    heads = wide_ref.shape[0]
    row_scale = lax.rsqrt(jnp.sum(ssq_ref[...], axis=0, keepdims=True) * (1.0 / EMBED_DIMENSION) + 1e-06)
    scale[...] = jnp.transpose(jnp.broadcast_to(row_scale, (HD, ROWS)))
    group = 4
    for tile in range(heads):
        lanes = pl.ds(tile * HD, HD)
        for r in range(BLK):
            tokens = pl.ds(r, NBLK, stride=BLK)
            g_ref[r, :, lanes] = wide_ref[tile, tokens, :] * w_ref[r, :, lanes] * scale[tokens, :]
        fade = fade_ref[:, lanes]
        for base in range(0, MODES, group):
            modes = range(base, base + group)
            cos = [cos_ref[0, pl.ds(m, 1), lanes] for m in modes]
            twice = [jnp.broadcast_to(2.0 * c, (NBLK, HD)) for c in cos]
            first = g_ref[0, :, lanes]
            older = [first] * group
            second = g_ref[1, :, lanes]
            newer = [twice[i] * first + second for i in range(group)]
            for r in range(2, BLK):
                term = g_ref[r, :, lanes]
                for i in range(group):
                    older[i], newer[i] = newer[i], twice[i] * newer[i] + (term - older[i])
            for i, m in enumerate(modes):
                sin = sin_ref[0, pl.ds(m, 1), lanes]
                end_re[tile, pl.ds(m * NBLK, NBLK), :] = fade * (newer[i] - cos[i] * older[i])
                end_im[tile, pl.ds(m * NBLK, NBLK), :] = fade * (sin * older[i])
    states = [None] * heads
    for j in range(NBLK):
        at = pl.ds(j, MODES, stride=NBLK)
        for tile in range(heads):
            lanes = pl.ds(tile * HD, HD)
            end = (end_re[tile, at, :], end_im[tile, at, :])
            if j == 0:
                st_re[tile, at, :] = jnp.zeros((MODES, HD), F32)
                st_im[tile, at, :] = jnp.zeros((MODES, HD), F32)
                states[tile] = end
            else:
                given = cmul(states[tile], (cb_ref[0, :, lanes], cb_ref[1, :, lanes]))
                st_re[tile, at, :] = given[0]
                st_im[tile, at, :] = given[1]
                rot16 = (cos_ref[1, :, lanes], sin_ref[1, :, lanes])
                states[tile] = chain_step(states[tile], rot16, fade_ref[pl.ds(j, 1), lanes], end)
    for tile in range(heads):
        lanes = pl.ds(tile * HD, HD)
        sum_ref[pl.ds(tile * 2 * MODES, MODES), :] = states[tile][0]
        sum_ref[pl.ds(tile * 2 * MODES + MODES, MODES), :] = states[tile][1]
        sum_ref[pl.ds(heads * 2 * MODES + tile, 1), :] = total_ref[:, lanes]
    used = heads * (2 * MODES + 1)
    sum_ref[pl.ds(used, sum_ref.shape[0] - used), :] = jnp.zeros((sum_ref.shape[0] - used, HD), F32)


def padded(rows):
    return -(-rows // 8) * 8


def block_ends(wide, w, ssq, cos, sin, fade, total, cb):
    width = w.shape[2]
    tiles = width // HD
    return pl.pallas_call(
        ends_kernel,
        out_shape=[
            jax.ShapeDtypeStruct((BLK, NBLK, width), F32),
            jax.ShapeDtypeStruct((tiles, MODES * NBLK, HD), F32),
            jax.ShapeDtypeStruct((tiles, MODES * NBLK, HD), F32),
            jax.ShapeDtypeStruct((padded(tiles * (2 * MODES + 1)), HD), F32),
        ],
        scratch_shapes=[pltpu.VMEM((ROWS, HD), F32)]
        + [pltpu.VMEM((tiles, MODES * NBLK, HD), F32)] * 2,
        compiler_params=pltpu.CompilerParams(vmem_limit_bytes=12 * 2**20),
        cost_estimate=pl.CostEstimate(flops=8_000_000, bytes_accessed=4_000_000, transcendentals=0),
        name="block_ends",
    )(wide, w, ssq, cos, sin, fade, total, cb)


def local_kernel(g_ref, kern_ref, out_ref):
    heads = g_ref.shape[2] // HD
    for tile in range(heads):
        lanes = pl.ds(tile * HD, HD)
        g = [g_ref[r, :, lanes] for r in range(BLK)]
        total = [None] * BLK
        for lag in range(BLK):
            k = jnp.broadcast_to(kern_ref[pl.ds(lag, 1), lanes], (NBLK, HD))
            for r in range(lag, BLK):
                term = k * g[r - lag]
                total[r] = term if total[r] is None else total[r] + term
        for r in range(BLK):
            out_ref[r, :, lanes] = total[r]


def local_part(g, kern):
    return pl.pallas_call(
        local_kernel,
        out_shape=jax.ShapeDtypeStruct(g.shape, F32),
        compiler_params=pltpu.CompilerParams(vmem_limit_bytes=12 * 2**20),
        cost_estimate=pl.CostEstimate(flops=3_000_000, bytes_accessed=1_300_000, transcendentals=0),
        name="local_part",
    )(g, kern)


def half_of(ref, tile, base=0):
    return (ref[pl.ds(base + tile * MODES, HALF), :], ref[pl.ds(base + tile * MODES + HALF, HALF), :])


def write_copies(ref, size, tiles, tile, value, decay):
    for copy in range(ref.shape[0] // size):
        base = copy * size
        ref[pl.ds(base + tile * MODES, HALF), :] = value[0]
        ref[pl.ds(base + tile * MODES + HALF, HALF), :] = value[1]
        ref[pl.ds(base + tiles * MODES + tile, 1), :] = decay


def clear_rest(ref, size, used):
    for copy in range(ref.shape[0] // size):
        ref[pl.ds(copy * size + used, size - used), :] = jnp.zeros((size - used, HD), F32)


def chip_kernel(pos_ref, own_ref, other_ref, cos_ref, sin_ref, out_ref):
    tiles = cos_ref.shape[2] // HD
    size = out_ref.shape[0] // NX
    core = pos_ref[3]
    first_core = core == 0
    half = pl.multiple_of(core * HALF, HALF)
    for tile in range(tiles):
        lanes = pl.ds(tile * HD, HD)
        rows = [pl.ds(pl.multiple_of(tile * 2 * MODES + i * MODES + half, HALF), HALF) for i in (0, 1)]
        own = [own_ref[at, :] for at in rows]
        other = [other_ref[at, :] for at in rows]
        at = pl.ds(tiles * 2 * MODES + tile, 1)
        own_decay, other_decay = own_ref[at, :], other_ref[at, :]
        fade = jnp.exp(-jnp.where(first_core, other_decay, own_decay))
        turn = [fade * ref[2, pl.ds(half, HALF), lanes] for ref in (cos_ref, sin_ref)]
        first = [jnp.where(first_core, own[i], other[i]) for i in (0, 1)]
        second = [jnp.where(first_core, other[i], own[i]) for i in (0, 1)]
        moved = cmul(first, turn)
        write_copies(
            out_ref, size, tiles, tile, [moved[i] + second[i] for i in (0, 1)], own_decay + other_decay
        )
    clear_rest(out_ref, size, tiles * (MODES + 1))


def chip_sum(pos, own, other, cos, sin):
    tiles = cos.shape[2] // HD
    return pl.pallas_call(
        chip_kernel,
        in_specs=[pl.BlockSpec(memory_space=pltpu.SMEM)] + [pl.BlockSpec()] * 4,
        out_shape=jax.ShapeDtypeStruct((NX * padded(tiles * (MODES + 1)), HD), F32),
        compiler_params=pltpu.CompilerParams(vmem_limit_bytes=4 * 2**20),
        cost_estimate=pl.CostEstimate(flops=100_000, bytes_accessed=300_000, transcendentals=640),
        name="chip_sum",
    )(pos, own, other, cos, sin)


def running(ref, size, tiles, tile, count, mine, step, state, turn):
    at = tiles * MODES + tile
    into = turned = None
    decay = jnp.zeros((1, HD), F32)
    zero = jnp.zeros((HALF, HD), F32)
    for k in range(count):
        if k:
            here = mine == k
            into = [jnp.where(here, state[i], into[i]) for i in (0, 1)]
            turned = [jnp.where(here, turn[i], turned[i]) for i in (0, 1)]
        else:
            into, turned = [zero, zero], list(turn)
        step_decay = ref[pl.ds(k * size + at, 1), :]
        fade = jnp.exp(-step_decay)
        moving = [fade * part for part in step]
        value = half_of(ref, tile, k * size)
        if k:
            moved = cmul(state, moving)
            state = [moved[i] + value[i] for i in (0, 1)]
        else:
            state = list(value)
        turn = cmul(turn, moving)
        decay = decay + step_decay
    return into, turned, state, decay


def row_kernel(pos_ref, chips_ref, cos_ref, sin_ref, row_ref, in_ref, turn_ref):
    tiles = in_ref.shape[0] // MODES
    size = chips_ref.shape[0] // NX
    half = pl.ds(pl.multiple_of(pos_ref[3] * HALF, HALF), HALF)
    one = (jnp.ones((HALF, HD), F32), jnp.zeros((HALF, HD), F32))
    for tile in range(tiles):
        lanes = pl.ds(tile * HD, HD)
        step = (cos_ref[3, half, lanes], sin_ref[3, half, lanes])
        into, turned, state, decay = running(chips_ref, size, tiles, tile, NX, pos_ref[4], step, None, one)
        write_copies(row_ref, size, tiles, tile, state, decay)
        for ref, value in ((in_ref, into), (turn_ref, turned)):
            ref[pl.ds(tile * MODES, HALF), :] = value[0]
            ref[pl.ds(tile * MODES + HALF, HALF), :] = value[1]
    clear_rest(row_ref, size, tiles * (MODES + 1))


def row_sum(pos, chips, cos, sin):
    tiles = cos.shape[2] // HD
    return pl.pallas_call(
        row_kernel,
        in_specs=[pl.BlockSpec(memory_space=pltpu.SMEM)] + [pl.BlockSpec()] * 3,
        out_shape=[
            jax.ShapeDtypeStruct((NY * padded(tiles * (MODES + 1)), HD), F32),
            jax.ShapeDtypeStruct((tiles * MODES, HD), F32),
            jax.ShapeDtypeStruct((tiles * MODES, HD), F32),
        ],
        compiler_params=pltpu.CompilerParams(vmem_limit_bytes=4 * 2**20),
        cost_estimate=pl.CostEstimate(flops=300_000, bytes_accessed=400_000, transcendentals=5000),
        name="row_sum",
    )(pos, chips, cos, sin)


def entry_kernel(pos_ref, rows_ref, in_ref, turn_ref, cos_ref, sin_ref, out_ref):
    tiles = in_ref.shape[0] // MODES
    size = rows_ref.shape[0] // NY
    half = pl.ds(pl.multiple_of(pos_ref[3] * HALF, HALF), HALF)
    one = (jnp.ones((HALF, HD), F32), jnp.zeros((HALF, HD), F32))
    for tile in range(tiles):
        lanes = pl.ds(tile * HD, HD)
        step = (cos_ref[4, half, lanes], sin_ref[4, half, lanes])
        row, _, _, _ = running(rows_ref, size, tiles, tile, NY, pos_ref[5], step, None, one)
        moved = cmul(row, half_of(turn_ref, tile))
        into = half_of(in_ref, tile)
        out_ref[pl.ds(tile * MODES, HALF), :] = moved[0] + into[0]
        out_ref[pl.ds(tile * MODES + HALF, HALF), :] = moved[1] + into[1]


def chip_entry(pos, rows, into, turn, cos, sin):
    return pl.pallas_call(
        entry_kernel,
        in_specs=[pl.BlockSpec(memory_space=pltpu.SMEM)] + [pl.BlockSpec()] * 5,
        out_shape=jax.ShapeDtypeStruct(into.shape, F32),
        compiler_params=pltpu.CompilerParams(vmem_limit_bytes=4 * 2**20),
        cost_estimate=pl.CostEstimate(flops=300_000, bytes_accessed=400_000, transcendentals=5000),
        name="chip_entry",
    )(pos, rows, into, turn, cos, sin)


def gathered(copies, count, groups):
    parts = copies.reshape(count, copies.shape[0] // count, copies.shape[1])
    return lax.all_to_all(parts, "seq", 0, 0, axis_index_groups=groups).reshape(copies.shape)


def finish_kernel(
    pos_ref, mine_ref, theirs_ref, other_ref, st_re, st_im, pass_re, pass_im, local_ref, fall_ref, cos_ref, sin_ref,
    cb_ref, rec_ref, start, acc, out
):
    heads = rec_ref.shape[1] // HD
    first_core = pos_ref[3] == 0
    for tile in range(heads):
        lanes = pl.ds(tile * HD, HD)
        mine, theirs = half_of(mine_ref, tile), half_of(theirs_ref, tile)
        at_chip = [
            jnp.concatenate(
                [jnp.where(first_core, mine[i], theirs[i]), jnp.where(first_core, theirs[i], mine[i])], axis=0
            )
            for i in (0, 1)
        ]
        fade = jnp.exp(-other_ref[pl.ds(heads * 2 * MODES + tile, 1), :])
        moved = cmul(at_chip, [fade * ref[2, :, lanes] for ref in (cos_ref, sin_ref)])
        other = [other_ref[pl.ds(tile * 2 * MODES + i * MODES, MODES), :] for i in (0, 1)]
        state = [jnp.where(first_core, at_chip[i], moved[i] + other[i]) for i in (0, 1)]
        start[tile, 0], start[tile, 1] = cmul(state, (cb_ref[0, :, lanes], cb_ref[1, :, lanes]))
    group = 8
    for tile in range(heads):
        lanes = pl.ds(tile * HD, HD)
        for base in range(0, MODES, group):
            older, newer, twice = [], [], []
            for m in range(base, base + group):
                at = pl.ds(m * NBLK, NBLK)
                own = pl.ds(m, 1)
                moved = cmul((pass_re[tile, at, :], pass_im[tile, at, :]), (start[tile, 0, own, :], start[tile, 1, own, :]))
                z = (st_re[tile, at, :] + moved[0], st_im[tile, at, :] + moved[1])
                cos = cos_ref[0, own, lanes]
                older.append(z[0])
                newer.append(cos * z[0] - sin_ref[0, own, lanes] * z[1])
                twice.append(jnp.broadcast_to(2.0 * cos, (NBLK, HD)))
            for r in range(BLK):
                if r > 0:
                    for i in range(group):
                        older[i], newer[i] = newer[i], twice[i] * newer[i] - older[i]
                total = functools.reduce(jnp.add, newer)
                if base == 0:
                    acc[r] = local_ref[r, :, lanes] + total
                else:
                    out[tile, pl.ds(r, NBLK, stride=BLK), :] = (acc[r] + total) * fall_ref[r, :, lanes]
        rec_ref[:, lanes] = out[tile]


def finish(pos, mine, theirs, other, states, passing, local, fall, cos, sin, cb):
    width = fall.shape[2]
    tiles = width // HD
    return pl.pallas_call(
        finish_kernel,
        in_specs=[pl.BlockSpec(memory_space=pltpu.SMEM)] + [pl.BlockSpec()] * 12,
        out_shape=jax.ShapeDtypeStruct((ROWS, width), F32),
        scratch_shapes=[
            pltpu.VMEM((tiles, 2, MODES, HD), F32),
            pltpu.VMEM((BLK, NBLK, HD), F32),
            pltpu.VMEM((tiles, ROWS, HD), F32),
        ],
        compiler_params=pltpu.CompilerParams(vmem_limit_bytes=12 * 2**20),
        cost_estimate=pl.CostEstimate(flops=8_000_000, bytes_accessed=5_000_000, transcendentals=0),
        name="finish",
    )(pos, mine, theirs, other, *states, *passing, local, fall, cos, sin, cb)


def shards(queries, keys, values, decay, gain, theta, mode_coeffs):
    width = queries.shape[1]
    me = lax.axis_index("seq")
    core = me % 2
    chip = me // 2

    own = jnp.stack([keys, values])
    two1 = lax.ppermute(own, "seq", chip_pairs(0, 1, (1,)))
    hop = lax.ppermute(own, "seq", two_back(0))
    up = lax.ppermute(own, "seq", CORE_UP)
    angles = jnp.asarray(TURNS, F32)[:, None, None] * theta[None]
    cos, sin = jnp.cos(angles), jnp.sin(angles)
    own_later, cos = lax.optimization_barrier((own, cos))
    two0 = lax.ppermute(own_later, "seq", chip_pairs(0, 1, (0,)))

    pos = jnp.stack(
        [
            (me >= 2).astype(jnp.int32),
            (me >= 4).astype(jnp.int32),
            ((me >= 3) | (core == 1)).astype(jnp.int32),
            core.astype(jnp.int32),
            (chip % NX).astype(jnp.int32),
            (chip // NX).astype(jnp.int32),
        ]
    )
    flat = jax.ShapeDtypeStruct(queries.shape, F32)
    far1 = lax.ppermute(two1, "seq", chip_pairs(0, 1, (1,)))
    high = lax.ppermute(two1, "seq", CORE_DOWN)
    made = tables(decay, gain[None, :], mode_coeffs, cos, sin, own)
    w, fall, fade, kern, total, cb, *passing = made
    two0 = gate(two0, high, hop, up, total)
    far0 = lax.ppermute(hop, "seq", two_back(1))
    low = lax.ppermute(two0, "seq", CORE_UP)
    run = attention_call(
        near_kernel, "attention_near", 2, [pos, queries, own, total, two0, two1, low, high], [flat] * 3, placed=5
    )
    far1 = gate(far1, far0)
    down = lax.ppermute(far1, "seq", CORE_DOWN)
    attn, wide, ssq = attention_call(
        far_kernel,
        "attention_far",
        2,
        [pos, queries, *run, far0, far1, up, down],
        [
            jax.ShapeDtypeStruct(queries.shape, jnp.bfloat16),
            jax.ShapeDtypeStruct((queries.shape[1] // HD, ROWS, HD), F32),
            jax.ShapeDtypeStruct((1, ROWS), F32),
        ],
        placed=4,
    )

    ssq_all = lax.all_to_all(jnp.broadcast_to(ssq, (NZ, ROWS)), "mp", 0, 0)

    g, *states, dev_sum = block_ends(wide, w, ssq_all, cos, sin, fade, total, cb)
    local = local_part(g, kern)

    other = lax.ppermute(dev_sum, "seq", CORE_SWAP)
    chips = gathered(chip_sum(pos, dev_sum, other, cos, sin), NX, X_GROUPS)
    row, into, turn = row_sum(pos, chips, cos, sin)
    rows = gathered(row, NY, Y_GROUPS)
    mine = chip_entry(pos, rows, into, turn, cos, sin)
    theirs = lax.ppermute(mine, "seq", CORE_SWAP)

    rec = finish(pos, mine, theirs, other, states, passing, local, fall, cos, sin, cb)
    return (attn, rec)


def solution(mesh):
    placed = (
        P("seq", "mp"),
        P("seq", "mp"),
        P("seq", "mp"),
        P("seq", "mp"),
        P("mp"),
        P(None, "mp"),
        P(None, None, "mp"),
    )
    return jax.shard_map(
        shards,
        mesh=mesh,
        in_specs=placed,
        out_specs=(P("seq", "mp"), P("seq", "mp")),
        check_vma=False,
    )
```

```python
import functools
import math

import jax
import jax.numpy as jnp
from jax import lax
from jax.experimental import pallas as pl
from jax.experimental.pallas import tpu as pltpu
from jax.sharding import PartitionSpec as P

HD = 128
EMBED_DIMENSION = 5120
MODES = 16
HALF = MODES // 2
ROWS = 256
BLK = 16
NBLK = ROWS // BLK
NX = 4
NY = 4
NZ = 8
SEQ = 32
NEG = -1e30
SCALE2 = math.log2(math.e) / math.sqrt(HD)
F32 = jnp.float32
TURNS = (1, BLK, ROWS, 2 * ROWS, 2 * NX * ROWS)


def device_of(y, x, core):
    return (y * NX + x) * 2 + core


def chip_pairs(dy, dx, cores=(0, 1)):
    pairs = []
    for chip in range(NX * NY):
        target = chip + dy * NX + dx
        if 0 <= target < NX * NY:
            pairs += [(chip * 2 + c, target * 2 + c) for c in cores]
    return pairs


def two_back(hop):
    pairs = []
    for chip in range(NX * NY - 2):
        y, x = divmod(chip, NX)
        middle = device_of(y + (x == 2), (x - 1) % NX, 0)
        pairs.append((chip * 2, middle) if hop == 0 else (middle, (chip + 2) * 2))
    return pairs


X_GROUPS = [[device_of(y, x, c) for x in range(NX)] for y in range(NY) for c in (0, 1)]
Y_GROUPS = [[device_of(y, x, c) for y in range(NY)] for x in range(NX) for c in (0, 1)]
CORE_SWAP = [(d, d ^ 1) for d in range(SEQ)]
CORE_UP = [(d, d + 1) for d in range(0, SEQ, 2)]
CORE_DOWN = [(d + 1, d) for d in range(0, SEQ, 2)]


def cmul(a, b):
    return (a[0] * b[0] - a[1] * b[1], a[0] * b[1] + a[1] * b[0])


def masks():
    row = lax.broadcasted_iota(jnp.int32, (ROWS, ROWS), 0)
    col = lax.broadcasted_iota(jnp.int32, (ROWS, ROWS), 1)
    return row, col


def scores_of(q, k):
    return lax.dot_general(q, k, (((1,), (1,)), ((), ())), preferred_element_type=F32)


def softmax_parts(parts, vals, top):
    weights = [jnp.exp2((s - top) * SCALE2) for s in parts]
    total = jnp.sum(functools.reduce(jnp.add, weights), axis=1, keepdims=True)
    mixed = [jnp.dot(w.astype(jnp.bfloat16), v, preferred_element_type=F32) for w, v in zip(weights, vals)]
    return total, functools.reduce(jnp.add, mixed)


def merged(parts, vals, top_in, total_in, mixed_in):
    top = jnp.max(functools.reduce(jnp.maximum, parts), axis=1, keepdims=True)
    top = jnp.maximum(top_in, jnp.broadcast_to(top, (ROWS, HD)))
    total, mixed = softmax_parts(parts, vals, jnp.concatenate([top] * (ROWS // HD), axis=1))
    shrink = jnp.exp2((top_in - top) * SCALE2)
    return top, total_in * shrink + jnp.broadcast_to(total, (ROWS, HD)), mixed_in * shrink + mixed


def fetch(pos_ref, pairs, slots, sems):
    first_core = pos_ref[3] == 0
    for core in (0, 1):
        @pl.when(first_core if core == 0 else jnp.logical_not(first_core))
        def _():
            for i, pair in enumerate(pairs):
                pltpu.make_async_copy(pair[core], slots.at[i], sems.at[i]).start()


def arrived(pairs, slots, sems):
    for i, pair in enumerate(pairs):
        pltpu.make_async_copy(pair[0], slots.at[i], sems.at[i]).wait()


def near_kernel(
    pos_ref, q_ref, own, after, two0, two1, low, high, top_ref, total_ref, mixed_ref, slots, sems
):
    pairs = ((two0, two1), (high, low))
    fetch(pos_ref, pairs, slots, sems)
    row, col = masks()
    there = pos_ref[0] == 1
    arrived(pairs, slots, sems)
    for head in range(q_ref.shape[1] // HD):
        lanes = pl.ds(head * HD, HD)
        q = q_ref[:, lanes]
        blocks = [own] + [slots.at[i] for i in (0, 1)]
        parts = [scores_of(q, block[0, :, lanes]) for block in blocks]
        parts = [jnp.where(col <= row, parts[0], NEG)] + [jnp.where(there, part, NEG) for part in parts[1:]]
        top = jnp.max(functools.reduce(jnp.maximum, parts), axis=1, keepdims=True)
        total, mixed = softmax_parts(parts, [block[1, :, lanes] for block in blocks], top)
        top_ref[:, lanes] = jnp.broadcast_to(top, (ROWS, HD))
        total_ref[:, lanes] = jnp.broadcast_to(total, (ROWS, HD))
        mixed_ref[:, lanes] = mixed


def far_kernel(
    pos_ref, q_ref, top_in, total_in, mixed_in, far0, far1, up, down, o_ref, wide_ref, ssq_ref, slots, sems
):
    pairs = ((far0, far1), (down, up))
    fetch(pos_ref, pairs, slots, sems)
    row, col = masks()
    there = pos_ref[2] == 1
    low = row - jnp.where(pos_ref[1] == 1, 0, -2 * ROWS)
    square = None
    arrived(pairs, slots, sems)
    for head in range(q_ref.shape[1] // HD):
        lanes = pl.ds(head * HD, HD)
        q = q_ref[:, lanes]
        parts = [
            jnp.where(col > low, scores_of(q, slots[0, 0, :, lanes]), NEG),
            jnp.where(there, scores_of(q, slots[1, 0, :, lanes]), NEG),
        ]
        _, total, mixed = merged(
            parts, [slots[i, 1, :, lanes] for i in (0, 1)], top_in[:, lanes], total_in[:, lanes], mixed_in[:, lanes]
        )
        out = (mixed / total).astype(jnp.bfloat16)
        o_ref[:, lanes] = out
        wide = out.astype(F32)
        wide_ref[head] = wide
        square = wide * wide if square is None else square + wide * wide
    ssq_ref[...] = jnp.sum(jnp.transpose(square), axis=0, keepdims=True)


def gate_kernel(*refs):
    pass


def gate(value, *after):
    place = pl.BlockSpec(memory_space=pl.ANY)
    return pl.pallas_call(
        gate_kernel,
        in_specs=[place] * (1 + len(after)),
        out_specs=place,
        out_shape=jax.ShapeDtypeStruct(value.shape, value.dtype),
        input_output_aliases={0: 0},
        compiler_params=pltpu.CompilerParams(vmem_limit_bytes=2**20),
        name="gate",
    )(value, *after)


def attention_call(kernel, name, share, operands, outs, placed):
    scalars = 1
    kept = len(operands) - scalars - placed
    block = (share,) + operands[-1].shape
    return pl.pallas_call(
        kernel,
        in_specs=[pl.BlockSpec(memory_space=pltpu.SMEM)] * scalars
        + [pl.BlockSpec()] * kept
        + [pl.BlockSpec(memory_space=pl.ANY)] * placed,
        out_shape=outs,
        scratch_shapes=[pltpu.VMEM(block, jnp.bfloat16), pltpu.SemaphoreType.DMA((share,))],
        compiler_params=pltpu.CompilerParams(vmem_limit_bytes=12 * 2**20),
        cost_estimate=pl.CostEstimate(
            flops=8_000_000_000 if name == "attention_near" else 340_000_000, bytes_accessed=1000 if name == "attention_near" else 3_000_000, transcendentals=0
        ),
        name=name,
    )(*operands)


def one_less_exp(v):
    series = 1.0 / 720.0
    for order in (120.0, 24.0, 6.0, 2.0, 1.0):
        series = 1.0 / order - v * series
    return jnp.where(v < 0.25, v * series, 1.0 - jnp.exp(-v))


def tables_kernel(
    decay_ref, gain_ref, coef_ref, cos_ref, sin_ref, after_ref, w_ref, fall_ref, fade_ref, kern_ref, total_ref, cb_ref,
    pass_re, pass_im
):
    gain = gain_ref[...]
    cum = jnp.zeros((NBLK, HD), F32)
    for r in range(BLK):
        step = decay_ref[pl.ds(r, NBLK, stride=BLK), :]
        cum = cum + step
        w_ref[r] = jnp.exp(cum) * (gain * jnp.sqrt(one_less_exp(2.0 * step)))
        fall_ref[r] = jnp.exp(-cum)
    fade_ref[...] = jnp.exp(-cum)
    total_ref[...] = jnp.sum(cum, axis=0, keepdims=True)
    z = cmul((coef_ref[2], coef_ref[3]), (coef_ref[0], coef_ref[1]))
    cb_ref[0], cb_ref[1] = z
    rot = (cos_ref[0], sin_ref[0])
    for lag in range(BLK):
        kern_ref[pl.ds(lag, 1), :] = jnp.sum(z[0], axis=0, keepdims=True)
        z = cmul(z, rot)
    moved = (jnp.ones((MODES, HD), F32), jnp.zeros((MODES, HD), F32))
    rot16 = (cos_ref[1], sin_ref[1])
    for j in range(NBLK):
        at = pl.ds(j, MODES, stride=NBLK)
        pass_re[0, at, :] = moved[0]
        pass_im[0, at, :] = moved[1]
        fade = fade_ref[pl.ds(j, 1), :]
        moved = tuple(fade * part for part in cmul(moved, rot16))


def tables(decay, gain, mode_coeffs, cos, sin, after):
    width = decay.shape[1]
    tokens = pl.BlockSpec((ROWS, HD), lambda h: (0, h))
    cube = pl.BlockSpec((BLK, NBLK, HD), lambda h: (0, 0, h))
    flat = pl.BlockSpec((NBLK, HD), lambda h: (0, h))
    line = pl.BlockSpec((1, HD), lambda h: (0, h))
    deep = pl.BlockSpec((1, MODES * NBLK, HD), lambda h: (h, 0, 0))
    return pl.pallas_call(
        tables_kernel,
        grid=(width // HD,),
        in_specs=[
            tokens,
            line,
            pl.BlockSpec((4, MODES, HD), lambda h: (0, 0, h)),
            pl.BlockSpec((2, MODES, HD), lambda h: (0, 0, h)),
            pl.BlockSpec((2, MODES, HD), lambda h: (0, 0, h)),
            pl.BlockSpec(memory_space=pl.ANY),
        ],
        out_specs=[cube, cube, flat, flat, line, pl.BlockSpec((2, MODES, HD), lambda h: (0, 0, h)), deep, deep],
        out_shape=[
            jax.ShapeDtypeStruct((BLK, NBLK, width), F32),
            jax.ShapeDtypeStruct((BLK, NBLK, width), F32),
            jax.ShapeDtypeStruct((NBLK, width), F32),
            jax.ShapeDtypeStruct((BLK, width), F32),
            jax.ShapeDtypeStruct((1, width), F32),
            jax.ShapeDtypeStruct((2, MODES, width), F32),
            jax.ShapeDtypeStruct((width // HD, MODES * NBLK, HD), F32),
            jax.ShapeDtypeStruct((width // HD, MODES * NBLK, HD), F32),
        ],
        compiler_params=pltpu.CompilerParams(vmem_limit_bytes=8 * 2**20),
        cost_estimate=pl.CostEstimate(flops=4000000, bytes_accessed=4000000, transcendentals=0),
        name="tables",
    )(decay, gain, mode_coeffs, cos, sin, after)


def chain_step(state, rot16, fade_row, end):
    turned = cmul(state, rot16)
    return (fade_row * turned[0] + end[0], fade_row * turned[1] + end[1])


def ends_kernel(
    wide_ref, w_ref, ssq_ref, cos_ref, sin_ref, fade_ref, total_ref, cb_ref, g_ref, st_re, st_im, sum_ref, scale, end_re,
    end_im
):
    heads = wide_ref.shape[0]
    row_scale = lax.rsqrt(jnp.sum(ssq_ref[...], axis=0, keepdims=True) * (1.0 / EMBED_DIMENSION) + 1e-06)
    scale[...] = jnp.transpose(jnp.broadcast_to(row_scale, (HD, ROWS)))
    group = 4
    for tile in range(heads):
        lanes = pl.ds(tile * HD, HD)
        for r in range(BLK):
            tokens = pl.ds(r, NBLK, stride=BLK)
            g_ref[r, :, lanes] = wide_ref[tile, tokens, :] * w_ref[r, :, lanes] * scale[tokens, :]
        fade = fade_ref[:, lanes]
        for base in range(0, MODES, group):
            modes = range(base, base + group)
            cos = [cos_ref[0, pl.ds(m, 1), lanes] for m in modes]
            twice = [jnp.broadcast_to(2.0 * c, (NBLK, HD)) for c in cos]
            first = g_ref[0, :, lanes]
            older = [first] * group
            second = g_ref[1, :, lanes]
            newer = [twice[i] * first + second for i in range(group)]
            for r in range(2, BLK):
                term = g_ref[r, :, lanes]
                for i in range(group):
                    older[i], newer[i] = newer[i], twice[i] * newer[i] + (term - older[i])
            for i, m in enumerate(modes):
                sin = sin_ref[0, pl.ds(m, 1), lanes]
                end_re[tile, pl.ds(m * NBLK, NBLK), :] = fade * (newer[i] - cos[i] * older[i])
                end_im[tile, pl.ds(m * NBLK, NBLK), :] = fade * (sin * older[i])
    states = [None] * heads
    for j in range(NBLK):
        at = pl.ds(j, MODES, stride=NBLK)
        for tile in range(heads):
            lanes = pl.ds(tile * HD, HD)
            end = (end_re[tile, at, :], end_im[tile, at, :])
            if j == 0:
                st_re[tile, at, :] = jnp.zeros((MODES, HD), F32)
                st_im[tile, at, :] = jnp.zeros((MODES, HD), F32)
                states[tile] = end
            else:
                given = cmul(states[tile], (cb_ref[0, :, lanes], cb_ref[1, :, lanes]))
                st_re[tile, at, :] = given[0]
                st_im[tile, at, :] = given[1]
                rot16 = (cos_ref[1, :, lanes], sin_ref[1, :, lanes])
                states[tile] = chain_step(states[tile], rot16, fade_ref[pl.ds(j, 1), lanes], end)
    for tile in range(heads):
        lanes = pl.ds(tile * HD, HD)
        sum_ref[pl.ds(tile * 2 * MODES, MODES), :] = states[tile][0]
        sum_ref[pl.ds(tile * 2 * MODES + MODES, MODES), :] = states[tile][1]
        sum_ref[pl.ds(heads * 2 * MODES + tile, 1), :] = total_ref[:, lanes]
    used = heads * (2 * MODES + 1)
    sum_ref[pl.ds(used, sum_ref.shape[0] - used), :] = jnp.zeros((sum_ref.shape[0] - used, HD), F32)


def padded(rows):
    return -(-rows // 8) * 8


def block_ends(wide, w, ssq, cos, sin, fade, total, cb):
    width = w.shape[2]
    tiles = width // HD
    return pl.pallas_call(
        ends_kernel,
        out_shape=[
            jax.ShapeDtypeStruct((BLK, NBLK, width), F32),
            jax.ShapeDtypeStruct((tiles, MODES * NBLK, HD), F32),
            jax.ShapeDtypeStruct((tiles, MODES * NBLK, HD), F32),
            jax.ShapeDtypeStruct((padded(tiles * (2 * MODES + 1)), HD), F32),
        ],
        scratch_shapes=[pltpu.VMEM((ROWS, HD), F32)]
        + [pltpu.VMEM((tiles, MODES * NBLK, HD), F32)] * 2,
        compiler_params=pltpu.CompilerParams(vmem_limit_bytes=12 * 2**20),
        cost_estimate=pl.CostEstimate(flops=8_000_000, bytes_accessed=4_000_000, transcendentals=0),
        name="block_ends",
    )(wide, w, ssq, cos, sin, fade, total, cb)


def local_kernel(g_ref, kern_ref, out_ref):
    heads = g_ref.shape[2] // HD
    for tile in range(heads):
        lanes = pl.ds(tile * HD, HD)
        g = [g_ref[r, :, lanes] for r in range(BLK)]
        total = [None] * BLK
        for lag in range(BLK):
            k = jnp.broadcast_to(kern_ref[pl.ds(lag, 1), lanes], (NBLK, HD))
            for r in range(lag, BLK):
                term = k * g[r - lag]
                total[r] = term if total[r] is None else total[r] + term
        for r in range(BLK):
            out_ref[r, :, lanes] = total[r]


def local_part(g, kern):
    return pl.pallas_call(
        local_kernel,
        out_shape=jax.ShapeDtypeStruct(g.shape, F32),
        compiler_params=pltpu.CompilerParams(vmem_limit_bytes=12 * 2**20),
        cost_estimate=pl.CostEstimate(flops=3_000_000, bytes_accessed=1_300_000, transcendentals=0),
        name="local_part",
    )(g, kern)


def half_of(ref, tile, base=0):
    return (ref[pl.ds(base + tile * MODES, HALF), :], ref[pl.ds(base + tile * MODES + HALF, HALF), :])


def write_copies(ref, size, tiles, tile, value, decay):
    for copy in range(ref.shape[0] // size):
        base = copy * size
        ref[pl.ds(base + tile * MODES, HALF), :] = value[0]
        ref[pl.ds(base + tile * MODES + HALF, HALF), :] = value[1]
        ref[pl.ds(base + tiles * MODES + tile, 1), :] = decay


def clear_rest(ref, size, used):
    for copy in range(ref.shape[0] // size):
        ref[pl.ds(copy * size + used, size - used), :] = jnp.zeros((size - used, HD), F32)


def chip_kernel(pos_ref, own_ref, other_ref, cos_ref, sin_ref, out_ref):
    tiles = cos_ref.shape[2] // HD
    size = out_ref.shape[0] // NX
    core = pos_ref[3]
    first_core = core == 0
    half = pl.multiple_of(core * HALF, HALF)
    for tile in range(tiles):
        lanes = pl.ds(tile * HD, HD)
        rows = [pl.ds(pl.multiple_of(tile * 2 * MODES + i * MODES + half, HALF), HALF) for i in (0, 1)]
        own = [own_ref[at, :] for at in rows]
        other = [other_ref[at, :] for at in rows]
        at = pl.ds(tiles * 2 * MODES + tile, 1)
        own_decay, other_decay = own_ref[at, :], other_ref[at, :]
        fade = jnp.exp(-jnp.where(first_core, other_decay, own_decay))
        turn = [fade * ref[2, pl.ds(half, HALF), lanes] for ref in (cos_ref, sin_ref)]
        first = [jnp.where(first_core, own[i], other[i]) for i in (0, 1)]
        second = [jnp.where(first_core, other[i], own[i]) for i in (0, 1)]
        moved = cmul(first, turn)
        write_copies(
            out_ref, size, tiles, tile, [moved[i] + second[i] for i in (0, 1)], own_decay + other_decay
        )
    clear_rest(out_ref, size, tiles * (MODES + 1))


def chip_sum(pos, own, other, cos, sin):
    tiles = cos.shape[2] // HD
    return pl.pallas_call(
        chip_kernel,
        in_specs=[pl.BlockSpec(memory_space=pltpu.SMEM)] + [pl.BlockSpec()] * 4,
        out_shape=jax.ShapeDtypeStruct((NX * padded(tiles * (MODES + 1)), HD), F32),
        compiler_params=pltpu.CompilerParams(vmem_limit_bytes=4 * 2**20),
        cost_estimate=pl.CostEstimate(flops=100_000, bytes_accessed=300_000, transcendentals=640),
        name="chip_sum",
    )(pos, own, other, cos, sin)


def running(ref, size, tiles, tile, count, mine, step, state, turn):
    at = tiles * MODES + tile
    into = turned = None
    decay = jnp.zeros((1, HD), F32)
    zero = jnp.zeros((HALF, HD), F32)
    for k in range(count):
        if k:
            here = mine == k
            into = [jnp.where(here, state[i], into[i]) for i in (0, 1)]
            turned = [jnp.where(here, turn[i], turned[i]) for i in (0, 1)]
        else:
            into, turned = [zero, zero], list(turn)
        step_decay = ref[pl.ds(k * size + at, 1), :]
        fade = jnp.exp(-step_decay)
        moving = [fade * part for part in step]
        value = half_of(ref, tile, k * size)
        if k:
            moved = cmul(state, moving)
            state = [moved[i] + value[i] for i in (0, 1)]
        else:
            state = list(value)
        turn = cmul(turn, moving)
        decay = decay + step_decay
    return into, turned, state, decay


def row_kernel(pos_ref, chips_ref, cos_ref, sin_ref, row_ref, in_ref, turn_ref):
    tiles = in_ref.shape[0] // MODES
    size = chips_ref.shape[0] // NX
    half = pl.ds(pl.multiple_of(pos_ref[3] * HALF, HALF), HALF)
    one = (jnp.ones((HALF, HD), F32), jnp.zeros((HALF, HD), F32))
    for tile in range(tiles):
        lanes = pl.ds(tile * HD, HD)
        step = (cos_ref[3, half, lanes], sin_ref[3, half, lanes])
        into, turned, state, decay = running(chips_ref, size, tiles, tile, NX, pos_ref[4], step, None, one)
        write_copies(row_ref, size, tiles, tile, state, decay)
        for ref, value in ((in_ref, into), (turn_ref, turned)):
            ref[pl.ds(tile * MODES, HALF), :] = value[0]
            ref[pl.ds(tile * MODES + HALF, HALF), :] = value[1]
    clear_rest(row_ref, size, tiles * (MODES + 1))


def row_sum(pos, chips, cos, sin):
    tiles = cos.shape[2] // HD
    return pl.pallas_call(
        row_kernel,
        in_specs=[pl.BlockSpec(memory_space=pltpu.SMEM)] + [pl.BlockSpec()] * 3,
        out_shape=[
            jax.ShapeDtypeStruct((NY * padded(tiles * (MODES + 1)), HD), F32),
            jax.ShapeDtypeStruct((tiles * MODES, HD), F32),
            jax.ShapeDtypeStruct((tiles * MODES, HD), F32),
        ],
        compiler_params=pltpu.CompilerParams(vmem_limit_bytes=4 * 2**20),
        cost_estimate=pl.CostEstimate(flops=300_000, bytes_accessed=400_000, transcendentals=5000),
        name="row_sum",
    )(pos, chips, cos, sin)


def entry_kernel(pos_ref, rows_ref, in_ref, turn_ref, cos_ref, sin_ref, out_ref):
    tiles = in_ref.shape[0] // MODES
    size = rows_ref.shape[0] // NY
    half = pl.ds(pl.multiple_of(pos_ref[3] * HALF, HALF), HALF)
    one = (jnp.ones((HALF, HD), F32), jnp.zeros((HALF, HD), F32))
    for tile in range(tiles):
        lanes = pl.ds(tile * HD, HD)
        step = (cos_ref[4, half, lanes], sin_ref[4, half, lanes])
        row, _, _, _ = running(rows_ref, size, tiles, tile, NY, pos_ref[5], step, None, one)
        moved = cmul(row, half_of(turn_ref, tile))
        into = half_of(in_ref, tile)
        out_ref[pl.ds(tile * MODES, HALF), :] = moved[0] + into[0]
        out_ref[pl.ds(tile * MODES + HALF, HALF), :] = moved[1] + into[1]


def chip_entry(pos, rows, into, turn, cos, sin):
    return pl.pallas_call(
        entry_kernel,
        in_specs=[pl.BlockSpec(memory_space=pltpu.SMEM)] + [pl.BlockSpec()] * 5,
        out_shape=jax.ShapeDtypeStruct(into.shape, F32),
        compiler_params=pltpu.CompilerParams(vmem_limit_bytes=4 * 2**20),
        cost_estimate=pl.CostEstimate(flops=300_000, bytes_accessed=400_000, transcendentals=5000),
        name="chip_entry",
    )(pos, rows, into, turn, cos, sin)


def gathered(copies, count, groups):
    parts = copies.reshape(count, copies.shape[0] // count, copies.shape[1])
    return lax.all_to_all(parts, "seq", 0, 0, axis_index_groups=groups).reshape(copies.shape)


def finish_kernel(
    pos_ref, mine_ref, theirs_ref, other_ref, st_re, st_im, pass_re, pass_im, local_ref, fall_ref, cos_ref, sin_ref,
    cb_ref, rec_ref, start, acc, out
):
    heads = rec_ref.shape[1] // HD
    first_core = pos_ref[3] == 0
    for tile in range(heads):
        lanes = pl.ds(tile * HD, HD)
        mine, theirs = half_of(mine_ref, tile), half_of(theirs_ref, tile)
        at_chip = [
            jnp.concatenate(
                [jnp.where(first_core, mine[i], theirs[i]), jnp.where(first_core, theirs[i], mine[i])], axis=0
            )
            for i in (0, 1)
        ]
        fade = jnp.exp(-other_ref[pl.ds(heads * 2 * MODES + tile, 1), :])
        moved = cmul(at_chip, [fade * ref[2, :, lanes] for ref in (cos_ref, sin_ref)])
        other = [other_ref[pl.ds(tile * 2 * MODES + i * MODES, MODES), :] for i in (0, 1)]
        state = [jnp.where(first_core, at_chip[i], moved[i] + other[i]) for i in (0, 1)]
        start[tile, 0], start[tile, 1] = cmul(state, (cb_ref[0, :, lanes], cb_ref[1, :, lanes]))
    group = 8
    for tile in range(heads):
        lanes = pl.ds(tile * HD, HD)
        for base in range(0, MODES, group):
            older, newer, twice = [], [], []
            for m in range(base, base + group):
                at = pl.ds(m * NBLK, NBLK)
                own = pl.ds(m, 1)
                moved = cmul((pass_re[tile, at, :], pass_im[tile, at, :]), (start[tile, 0, own, :], start[tile, 1, own, :]))
                z = (st_re[tile, at, :] + moved[0], st_im[tile, at, :] + moved[1])
                cos = cos_ref[0, own, lanes]
                older.append(z[0])
                newer.append(cos * z[0] - sin_ref[0, own, lanes] * z[1])
                twice.append(jnp.broadcast_to(2.0 * cos, (NBLK, HD)))
            for r in range(BLK):
                if r > 0:
                    for i in range(group):
                        older[i], newer[i] = newer[i], twice[i] * newer[i] - older[i]
                total = functools.reduce(jnp.add, newer)
                if base == 0:
                    acc[r] = local_ref[r, :, lanes] + total
                else:
                    out[tile, pl.ds(r, NBLK, stride=BLK), :] = (acc[r] + total) * fall_ref[r, :, lanes]
        rec_ref[:, lanes] = out[tile]


def finish(pos, mine, theirs, other, states, passing, local, fall, cos, sin, cb):
    width = fall.shape[2]
    tiles = width // HD
    return pl.pallas_call(
        finish_kernel,
        in_specs=[pl.BlockSpec(memory_space=pltpu.SMEM)] + [pl.BlockSpec()] * 12,
        out_shape=jax.ShapeDtypeStruct((ROWS, width), F32),
        scratch_shapes=[
            pltpu.VMEM((tiles, 2, MODES, HD), F32),
            pltpu.VMEM((BLK, NBLK, HD), F32),
            pltpu.VMEM((tiles, ROWS, HD), F32),
        ],
        compiler_params=pltpu.CompilerParams(vmem_limit_bytes=12 * 2**20),
        cost_estimate=pl.CostEstimate(flops=8_000_000, bytes_accessed=5_000_000, transcendentals=0),
        name="finish",
    )(pos, mine, theirs, other, *states, *passing, local, fall, cos, sin, cb)


def shards(queries, keys, values, decay, gain, theta, mode_coeffs):
    width = queries.shape[1]
    me = lax.axis_index("seq")
    core = me % 2
    chip = me // 2

    own = jnp.stack([keys, values])
    two1 = lax.ppermute(own, "seq", chip_pairs(0, 1, (1,)))
    hop = lax.ppermute(own, "seq", two_back(0))
    up = lax.ppermute(own, "seq", CORE_UP)
    angles = jnp.asarray(TURNS, F32)[:, None, None] * theta[None]
    cos, sin = jnp.cos(angles), jnp.sin(angles)
    own_later, cos = lax.optimization_barrier((own, cos))
    two0 = lax.ppermute(own_later, "seq", chip_pairs(0, 1, (0,)))

    pos = jnp.stack(
        [
            (me >= 2).astype(jnp.int32),
            (me >= 4).astype(jnp.int32),
            ((me >= 3) | (core == 1)).astype(jnp.int32),
            core.astype(jnp.int32),
            (chip % NX).astype(jnp.int32),
            (chip // NX).astype(jnp.int32),
        ]
    )
    flat = jax.ShapeDtypeStruct(queries.shape, F32)
    far1 = lax.ppermute(two1, "seq", chip_pairs(0, 1, (1,)))
    high = lax.ppermute(two1, "seq", CORE_DOWN)
    made = tables(decay, gain[None, :], mode_coeffs, cos, sin, own)
    w, fall, fade, kern, total, cb, *passing = made
    two0 = gate(two0, high, hop, up, total)
    far0 = lax.ppermute(hop, "seq", two_back(1))
    low = lax.ppermute(two0, "seq", CORE_UP)
    run = attention_call(
        near_kernel, "attention_near", 2, [pos, queries, own, total, two0, two1, low, high], [flat] * 3, placed=5
    )
    far1 = gate(far1, far0)
    down = lax.ppermute(far1, "seq", CORE_DOWN)
    attn, wide, ssq = attention_call(
        far_kernel,
        "attention_far",
        2,
        [pos, queries, *run, far0, far1, up, down],
        [
            jax.ShapeDtypeStruct(queries.shape, jnp.bfloat16),
            jax.ShapeDtypeStruct((queries.shape[1] // HD, ROWS, HD), F32),
            jax.ShapeDtypeStruct((1, ROWS), F32),
        ],
        placed=4,
    )

    ssq_all = lax.all_to_all(jnp.broadcast_to(ssq, (NZ, ROWS)), "mp", 0, 0)

    g, *states, dev_sum = block_ends(wide, w, ssq_all, cos, sin, fade, total, cb)
    local = local_part(g, kern)

    other = lax.ppermute(dev_sum, "seq", CORE_SWAP)
    chips = gathered(chip_sum(pos, dev_sum, other, cos, sin), NX, X_GROUPS)
    row, into, turn = row_sum(pos, chips, cos, sin)
    rows = gathered(row, NY, Y_GROUPS)
    mine = chip_entry(pos, rows, into, turn, cos, sin)
    theirs = lax.ppermute(mine, "seq", CORE_SWAP)

    rec = finish(pos, mine, theirs, other, states, passing, local, fall, cos, sin, cb)
    return (attn, rec)


def solution(mesh):
    placed = (
        P("seq", "mp"),
        P("seq", "mp"),
        P("seq", "mp"),
        P("seq", "mp"),
        P("mp"),
        P(None, "mp"),
        P(None, None, "mp"),
    )
    return jax.shard_map(
        shards,
        mesh=mesh,
        in_specs=placed,
        out_specs=(P("seq", "mp"), P("seq", "mp")),
        check_vma=False,
    )
```

```python
import functools
import math

import jax
import jax.numpy as jnp
from jax import lax
from jax.experimental import pallas as pl
from jax.experimental.pallas import tpu as pltpu
from jax.sharding import PartitionSpec as P

HD = 128
EMBED_DIMENSION = 5120
MODES = 16
HALF = MODES // 2
ROWS = 256
BLK = 16
NBLK = ROWS // BLK
NX = 4
NY = 4
NZ = 8
SEQ = 32
NEG = -1e30
SCALE2 = math.log2(math.e) / math.sqrt(HD)
F32 = jnp.float32
TURNS = (1, BLK, ROWS, 2 * ROWS, 2 * NX * ROWS)


def device_of(y, x, core):
    return (y * NX + x) * 2 + core


def chip_pairs(dy, dx, cores=(0, 1)):
    pairs = []
    for chip in range(NX * NY):
        target = chip + dy * NX + dx
        if 0 <= target < NX * NY:
            pairs += [(chip * 2 + c, target * 2 + c) for c in cores]
    return pairs


def two_back(hop):
    pairs = []
    for chip in range(NX * NY - 2):
        y, x = divmod(chip, NX)
        middle = device_of(y + (x == 2), (x - 1) % NX, 0)
        pairs.append((chip * 2, middle) if hop == 0 else (middle, (chip + 2) * 2))
    return pairs


X_GROUPS = [[device_of(y, x, c) for x in range(NX)] for y in range(NY) for c in (0, 1)]
Y_GROUPS = [[device_of(y, x, c) for y in range(NY)] for x in range(NX) for c in (0, 1)]
CORE_SWAP = [(d, d ^ 1) for d in range(SEQ)]
CORE_UP = [(d, d + 1) for d in range(0, SEQ, 2)]
CORE_DOWN = [(d + 1, d) for d in range(0, SEQ, 2)]


def cmul(a, b):
    return (a[0] * b[0] - a[1] * b[1], a[0] * b[1] + a[1] * b[0])


def masks():
    row = lax.broadcasted_iota(jnp.int32, (ROWS, ROWS), 0)
    col = lax.broadcasted_iota(jnp.int32, (ROWS, ROWS), 1)
    return row, col


def scores_of(q, k):
    return lax.dot_general(q, k, (((1,), (1,)), ((), ())), preferred_element_type=F32)


def softmax_parts(parts, vals, top):
    weights = [jnp.exp2((s - top) * SCALE2) for s in parts]
    total = jnp.sum(functools.reduce(jnp.add, weights), axis=1, keepdims=True)
    mixed = [jnp.dot(w.astype(jnp.bfloat16), v, preferred_element_type=F32) for w, v in zip(weights, vals)]
    return total, functools.reduce(jnp.add, mixed)


def merged(parts, vals, top_in, total_in, mixed_in):
    top = jnp.max(functools.reduce(jnp.maximum, parts), axis=1, keepdims=True)
    top = jnp.maximum(top_in, jnp.broadcast_to(top, (ROWS, HD)))
    total, mixed = softmax_parts(parts, vals, jnp.concatenate([top] * (ROWS // HD), axis=1))
    shrink = jnp.exp2((top_in - top) * SCALE2)
    return top, total_in * shrink + jnp.broadcast_to(total, (ROWS, HD)), mixed_in * shrink + mixed


def fetch(pos_ref, pairs, slots, sems):
    first_core = pos_ref[3] == 0
    for core in (0, 1):
        @pl.when(first_core if core == 0 else jnp.logical_not(first_core))
        def _():
            for i, pair in enumerate(pairs):
                pltpu.make_async_copy(pair[core], slots.at[i], sems.at[i]).start()


def arrived(pairs, slots, sems):
    for i, pair in enumerate(pairs):
        pltpu.make_async_copy(pair[0], slots.at[i], sems.at[i]).wait()


def near_kernel(
    pos_ref, q_ref, own, after, two0, two1, low, high, top_ref, total_ref, mixed_ref, slots, sems
):
    pairs = ((two0, two1), (high, low))
    fetch(pos_ref, pairs, slots, sems)
    row, col = masks()
    there = pos_ref[0] == 1
    arrived(pairs, slots, sems)
    for head in range(q_ref.shape[1] // HD):
        lanes = pl.ds(head * HD, HD)
        q = q_ref[:, lanes]
        blocks = [own] + [slots.at[i] for i in (0, 1)]
        parts = [scores_of(q, block[0, :, lanes]) for block in blocks]
        parts = [jnp.where(col <= row, parts[0], NEG)] + [jnp.where(there, part, NEG) for part in parts[1:]]
        top = jnp.max(functools.reduce(jnp.maximum, parts), axis=1, keepdims=True)
        total, mixed = softmax_parts(parts, [block[1, :, lanes] for block in blocks], top)
        top_ref[:, lanes] = jnp.broadcast_to(top, (ROWS, HD))
        total_ref[:, lanes] = jnp.broadcast_to(total, (ROWS, HD))
        mixed_ref[:, lanes] = mixed


def far_kernel(
    pos_ref, q_ref, top_in, total_in, mixed_in, far0, far1, up, down, o_ref, wide_ref, ssq_ref, slots, sems
):
    pairs = ((far0, far1), (down, up))
    fetch(pos_ref, pairs, slots, sems)
    row, col = masks()
    there = pos_ref[2] == 1
    low = row - jnp.where(pos_ref[1] == 1, 0, -2 * ROWS)
    square = None
    arrived(pairs, slots, sems)
    for head in range(q_ref.shape[1] // HD):
        lanes = pl.ds(head * HD, HD)
        q = q_ref[:, lanes]
        parts = [
            jnp.where(col > low, scores_of(q, slots[0, 0, :, lanes]), NEG),
            jnp.where(there, scores_of(q, slots[1, 0, :, lanes]), NEG),
        ]
        _, total, mixed = merged(
            parts, [slots[i, 1, :, lanes] for i in (0, 1)], top_in[:, lanes], total_in[:, lanes], mixed_in[:, lanes]
        )
        out = (mixed / total).astype(jnp.bfloat16)
        o_ref[:, lanes] = out
        wide = out.astype(F32)
        wide_ref[head] = wide
        square = wide * wide if square is None else square + wide * wide
    ssq_ref[...] = jnp.sum(jnp.transpose(square), axis=0, keepdims=True)


def gate_kernel(*refs):
    pass


def gate(value, *after):
    place = pl.BlockSpec(memory_space=pl.ANY)
    return pl.pallas_call(
        gate_kernel,
        in_specs=[place] * (1 + len(after)),
        out_specs=place,
        out_shape=jax.ShapeDtypeStruct(value.shape, value.dtype),
        input_output_aliases={0: 0},
        compiler_params=pltpu.CompilerParams(vmem_limit_bytes=2**20),
        name="gate",
    )(value, *after)


def attention_call(kernel, name, share, operands, outs, placed):
    scalars = 1
    kept = len(operands) - scalars - placed
    block = (share,) + operands[-1].shape
    return pl.pallas_call(
        kernel,
        in_specs=[pl.BlockSpec(memory_space=pltpu.SMEM)] * scalars
        + [pl.BlockSpec()] * kept
        + [pl.BlockSpec(memory_space=pl.ANY)] * placed,
        out_shape=outs,
        scratch_shapes=[pltpu.VMEM(block, jnp.bfloat16), pltpu.SemaphoreType.DMA((share,))],
        compiler_params=pltpu.CompilerParams(vmem_limit_bytes=12 * 2**20),
        cost_estimate=pl.CostEstimate(
            flops=8_000_000_000 * share, bytes_accessed=1000, transcendentals=0
        ),
        name=name,
    )(*operands)


def one_less_exp(v):
    series = 1.0 / 720.0
    for order in (120.0, 24.0, 6.0, 2.0, 1.0):
        series = 1.0 / order - v * series
    return jnp.where(v < 0.25, v * series, 1.0 - jnp.exp(-v))


def tables_kernel(
    decay_ref, gain_ref, coef_ref, cos_ref, sin_ref, after_ref, w_ref, fall_ref, fade_ref, kern_ref, total_ref, cb_ref,
    pass_re, pass_im
):
    gain = gain_ref[...]
    cum = jnp.zeros((NBLK, HD), F32)
    for r in range(BLK):
        step = decay_ref[pl.ds(r, NBLK, stride=BLK), :]
        cum = cum + step
        w_ref[r] = jnp.exp(cum) * (gain * jnp.sqrt(one_less_exp(2.0 * step)))
        fall_ref[r] = jnp.exp(-cum)
    fade_ref[...] = jnp.exp(-cum)
    total_ref[...] = jnp.sum(cum, axis=0, keepdims=True)
    z = cmul((coef_ref[2], coef_ref[3]), (coef_ref[0], coef_ref[1]))
    cb_ref[0], cb_ref[1] = z
    rot = (cos_ref[0], sin_ref[0])
    for lag in range(BLK):
        kern_ref[pl.ds(lag, 1), :] = jnp.sum(z[0], axis=0, keepdims=True)
        z = cmul(z, rot)
    moved = (jnp.ones((MODES, HD), F32), jnp.zeros((MODES, HD), F32))
    rot16 = (cos_ref[1], sin_ref[1])
    for j in range(NBLK):
        at = pl.ds(j, MODES, stride=NBLK)
        pass_re[0, at, :] = moved[0]
        pass_im[0, at, :] = moved[1]
        fade = fade_ref[pl.ds(j, 1), :]
        moved = tuple(fade * part for part in cmul(moved, rot16))


def tables(decay, gain, mode_coeffs, cos, sin, after):
    width = decay.shape[1]
    tokens = pl.BlockSpec((ROWS, HD), lambda h: (0, h))
    cube = pl.BlockSpec((BLK, NBLK, HD), lambda h: (0, 0, h))
    flat = pl.BlockSpec((NBLK, HD), lambda h: (0, h))
    line = pl.BlockSpec((1, HD), lambda h: (0, h))
    deep = pl.BlockSpec((1, MODES * NBLK, HD), lambda h: (h, 0, 0))
    return pl.pallas_call(
        tables_kernel,
        grid=(width // HD,),
        in_specs=[
            tokens,
            line,
            pl.BlockSpec((4, MODES, HD), lambda h: (0, 0, h)),
            pl.BlockSpec((2, MODES, HD), lambda h: (0, 0, h)),
            pl.BlockSpec((2, MODES, HD), lambda h: (0, 0, h)),
            pl.BlockSpec(memory_space=pl.ANY),
        ],
        out_specs=[cube, cube, flat, flat, line, pl.BlockSpec((2, MODES, HD), lambda h: (0, 0, h)), deep, deep],
        out_shape=[
            jax.ShapeDtypeStruct((BLK, NBLK, width), F32),
            jax.ShapeDtypeStruct((BLK, NBLK, width), F32),
            jax.ShapeDtypeStruct((NBLK, width), F32),
            jax.ShapeDtypeStruct((BLK, width), F32),
            jax.ShapeDtypeStruct((1, width), F32),
            jax.ShapeDtypeStruct((2, MODES, width), F32),
            jax.ShapeDtypeStruct((width // HD, MODES * NBLK, HD), F32),
            jax.ShapeDtypeStruct((width // HD, MODES * NBLK, HD), F32),
        ],
        compiler_params=pltpu.CompilerParams(vmem_limit_bytes=8 * 2**20),
        cost_estimate=pl.CostEstimate(flops=4000000, bytes_accessed=4000000, transcendentals=0),
        name="tables",
    )(decay, gain, mode_coeffs, cos, sin, after)


def chain_step(state, rot16, fade_row, end):
    turned = cmul(state, rot16)
    return (fade_row * turned[0] + end[0], fade_row * turned[1] + end[1])


def ends_kernel(
    wide_ref, w_ref, ssq_ref, cos_ref, sin_ref, fade_ref, total_ref, cb_ref, g_ref, st_re, st_im, sum_ref, scale, end_re,
    end_im
):
    heads = wide_ref.shape[0]
    row_scale = lax.rsqrt(jnp.sum(ssq_ref[...], axis=0, keepdims=True) * (1.0 / EMBED_DIMENSION) + 1e-06)
    scale[...] = jnp.transpose(jnp.broadcast_to(row_scale, (HD, ROWS)))
    group = 4
    for tile in range(heads):
        lanes = pl.ds(tile * HD, HD)
        for r in range(BLK):
            tokens = pl.ds(r, NBLK, stride=BLK)
            g_ref[r, :, lanes] = wide_ref[tile, tokens, :] * w_ref[r, :, lanes] * scale[tokens, :]
        fade = fade_ref[:, lanes]
        for base in range(0, MODES, group):
            modes = range(base, base + group)
            cos = [cos_ref[0, pl.ds(m, 1), lanes] for m in modes]
            twice = [jnp.broadcast_to(2.0 * c, (NBLK, HD)) for c in cos]
            first = g_ref[0, :, lanes]
            older = [first] * group
            second = g_ref[1, :, lanes]
            newer = [twice[i] * first + second for i in range(group)]
            for r in range(2, BLK):
                term = g_ref[r, :, lanes]
                for i in range(group):
                    older[i], newer[i] = newer[i], twice[i] * newer[i] + (term - older[i])
            for i, m in enumerate(modes):
                sin = sin_ref[0, pl.ds(m, 1), lanes]
                end_re[tile, pl.ds(m * NBLK, NBLK), :] = fade * (newer[i] - cos[i] * older[i])
                end_im[tile, pl.ds(m * NBLK, NBLK), :] = fade * (sin * older[i])
    states = [None] * heads
    for j in range(NBLK):
        at = pl.ds(j, MODES, stride=NBLK)
        for tile in range(heads):
            lanes = pl.ds(tile * HD, HD)
            end = (end_re[tile, at, :], end_im[tile, at, :])
            if j == 0:
                st_re[tile, at, :] = jnp.zeros((MODES, HD), F32)
                st_im[tile, at, :] = jnp.zeros((MODES, HD), F32)
                states[tile] = end
            else:
                given = cmul(states[tile], (cb_ref[0, :, lanes], cb_ref[1, :, lanes]))
                st_re[tile, at, :] = given[0]
                st_im[tile, at, :] = given[1]
                rot16 = (cos_ref[1, :, lanes], sin_ref[1, :, lanes])
                states[tile] = chain_step(states[tile], rot16, fade_ref[pl.ds(j, 1), lanes], end)
    for tile in range(heads):
        lanes = pl.ds(tile * HD, HD)
        sum_ref[pl.ds(tile * 2 * MODES, MODES), :] = states[tile][0]
        sum_ref[pl.ds(tile * 2 * MODES + MODES, MODES), :] = states[tile][1]
        sum_ref[pl.ds(heads * 2 * MODES + tile, 1), :] = total_ref[:, lanes]
    used = heads * (2 * MODES + 1)
    sum_ref[pl.ds(used, sum_ref.shape[0] - used), :] = jnp.zeros((sum_ref.shape[0] - used, HD), F32)


def padded(rows):
    return -(-rows // 8) * 8


def block_ends(wide, w, ssq, cos, sin, fade, total, cb):
    width = w.shape[2]
    tiles = width // HD
    return pl.pallas_call(
        ends_kernel,
        out_shape=[
            jax.ShapeDtypeStruct((BLK, NBLK, width), F32),
            jax.ShapeDtypeStruct((tiles, MODES * NBLK, HD), F32),
            jax.ShapeDtypeStruct((tiles, MODES * NBLK, HD), F32),
            jax.ShapeDtypeStruct((padded(tiles * (2 * MODES + 1)), HD), F32),
        ],
        scratch_shapes=[pltpu.VMEM((ROWS, HD), F32)]
        + [pltpu.VMEM((tiles, MODES * NBLK, HD), F32)] * 2,
        compiler_params=pltpu.CompilerParams(vmem_limit_bytes=12 * 2**20),
        cost_estimate=pl.CostEstimate(flops=8_000_000, bytes_accessed=4_000_000, transcendentals=0),
        name="block_ends",
    )(wide, w, ssq, cos, sin, fade, total, cb)


def local_kernel(g_ref, kern_ref, out_ref):
    heads = g_ref.shape[2] // HD
    for tile in range(heads):
        lanes = pl.ds(tile * HD, HD)
        g = [g_ref[r, :, lanes] for r in range(BLK)]
        total = [None] * BLK
        for lag in range(BLK):
            k = jnp.broadcast_to(kern_ref[pl.ds(lag, 1), lanes], (NBLK, HD))
            for r in range(lag, BLK):
                term = k * g[r - lag]
                total[r] = term if total[r] is None else total[r] + term
        for r in range(BLK):
            out_ref[r, :, lanes] = total[r]


def local_part(g, kern):
    return pl.pallas_call(
        local_kernel,
        out_shape=jax.ShapeDtypeStruct(g.shape, F32),
        compiler_params=pltpu.CompilerParams(vmem_limit_bytes=12 * 2**20),
        cost_estimate=pl.CostEstimate(flops=3_000_000, bytes_accessed=1_300_000, transcendentals=0),
        name="local_part",
    )(g, kern)


def half_of(ref, tile, base=0):
    return (ref[pl.ds(base + tile * MODES, HALF), :], ref[pl.ds(base + tile * MODES + HALF, HALF), :])


def write_copies(ref, size, tiles, tile, value, decay):
    for copy in range(ref.shape[0] // size):
        base = copy * size
        ref[pl.ds(base + tile * MODES, HALF), :] = value[0]
        ref[pl.ds(base + tile * MODES + HALF, HALF), :] = value[1]
        ref[pl.ds(base + tiles * MODES + tile, 1), :] = decay


def clear_rest(ref, size, used):
    for copy in range(ref.shape[0] // size):
        ref[pl.ds(copy * size + used, size - used), :] = jnp.zeros((size - used, HD), F32)


def chip_kernel(pos_ref, own_ref, other_ref, cos_ref, sin_ref, out_ref):
    tiles = cos_ref.shape[2] // HD
    size = out_ref.shape[0] // NX
    core = pos_ref[3]
    first_core = core == 0
    half = pl.multiple_of(core * HALF, HALF)
    for tile in range(tiles):
        lanes = pl.ds(tile * HD, HD)
        rows = [pl.ds(pl.multiple_of(tile * 2 * MODES + i * MODES + half, HALF), HALF) for i in (0, 1)]
        own = [own_ref[at, :] for at in rows]
        other = [other_ref[at, :] for at in rows]
        at = pl.ds(tiles * 2 * MODES + tile, 1)
        own_decay, other_decay = own_ref[at, :], other_ref[at, :]
        fade = jnp.exp(-jnp.where(first_core, other_decay, own_decay))
        turn = [fade * ref[2, pl.ds(half, HALF), lanes] for ref in (cos_ref, sin_ref)]
        first = [jnp.where(first_core, own[i], other[i]) for i in (0, 1)]
        second = [jnp.where(first_core, other[i], own[i]) for i in (0, 1)]
        moved = cmul(first, turn)
        write_copies(
            out_ref, size, tiles, tile, [moved[i] + second[i] for i in (0, 1)], own_decay + other_decay
        )
    clear_rest(out_ref, size, tiles * (MODES + 1))


def chip_sum(pos, own, other, cos, sin):
    tiles = cos.shape[2] // HD
    return pl.pallas_call(
        chip_kernel,
        in_specs=[pl.BlockSpec(memory_space=pltpu.SMEM)] + [pl.BlockSpec()] * 4,
        out_shape=jax.ShapeDtypeStruct((NX * padded(tiles * (MODES + 1)), HD), F32),
        compiler_params=pltpu.CompilerParams(vmem_limit_bytes=4 * 2**20),
        cost_estimate=pl.CostEstimate(flops=100_000, bytes_accessed=300_000, transcendentals=640),
        name="chip_sum",
    )(pos, own, other, cos, sin)


def running(ref, size, tiles, tile, count, mine, step, state, turn):
    at = tiles * MODES + tile
    into = turned = None
    decay = jnp.zeros((1, HD), F32)
    zero = jnp.zeros((HALF, HD), F32)
    for k in range(count):
        if k:
            here = mine == k
            into = [jnp.where(here, state[i], into[i]) for i in (0, 1)]
            turned = [jnp.where(here, turn[i], turned[i]) for i in (0, 1)]
        else:
            into, turned = [zero, zero], list(turn)
        step_decay = ref[pl.ds(k * size + at, 1), :]
        fade = jnp.exp(-step_decay)
        moving = [fade * part for part in step]
        value = half_of(ref, tile, k * size)
        if k:
            moved = cmul(state, moving)
            state = [moved[i] + value[i] for i in (0, 1)]
        else:
            state = list(value)
        turn = cmul(turn, moving)
        decay = decay + step_decay
    return into, turned, state, decay


def row_kernel(pos_ref, chips_ref, cos_ref, sin_ref, row_ref, in_ref, turn_ref):
    tiles = in_ref.shape[0] // MODES
    size = chips_ref.shape[0] // NX
    half = pl.ds(pl.multiple_of(pos_ref[3] * HALF, HALF), HALF)
    one = (jnp.ones((HALF, HD), F32), jnp.zeros((HALF, HD), F32))
    for tile in range(tiles):
        lanes = pl.ds(tile * HD, HD)
        step = (cos_ref[3, half, lanes], sin_ref[3, half, lanes])
        into, turned, state, decay = running(chips_ref, size, tiles, tile, NX, pos_ref[4], step, None, one)
        write_copies(row_ref, size, tiles, tile, state, decay)
        for ref, value in ((in_ref, into), (turn_ref, turned)):
            ref[pl.ds(tile * MODES, HALF), :] = value[0]
            ref[pl.ds(tile * MODES + HALF, HALF), :] = value[1]
    clear_rest(row_ref, size, tiles * (MODES + 1))


def row_sum(pos, chips, cos, sin):
    tiles = cos.shape[2] // HD
    return pl.pallas_call(
        row_kernel,
        in_specs=[pl.BlockSpec(memory_space=pltpu.SMEM)] + [pl.BlockSpec()] * 3,
        out_shape=[
            jax.ShapeDtypeStruct((NY * padded(tiles * (MODES + 1)), HD), F32),
            jax.ShapeDtypeStruct((tiles * MODES, HD), F32),
            jax.ShapeDtypeStruct((tiles * MODES, HD), F32),
        ],
        compiler_params=pltpu.CompilerParams(vmem_limit_bytes=4 * 2**20),
        cost_estimate=pl.CostEstimate(flops=300_000, bytes_accessed=400_000, transcendentals=5000),
        name="row_sum",
    )(pos, chips, cos, sin)


def entry_kernel(pos_ref, rows_ref, in_ref, turn_ref, cos_ref, sin_ref, out_ref):
    tiles = in_ref.shape[0] // MODES
    size = rows_ref.shape[0] // NY
    half = pl.ds(pl.multiple_of(pos_ref[3] * HALF, HALF), HALF)
    one = (jnp.ones((HALF, HD), F32), jnp.zeros((HALF, HD), F32))
    for tile in range(tiles):
        lanes = pl.ds(tile * HD, HD)
        step = (cos_ref[4, half, lanes], sin_ref[4, half, lanes])
        row, _, _, _ = running(rows_ref, size, tiles, tile, NY, pos_ref[5], step, None, one)
        moved = cmul(row, half_of(turn_ref, tile))
        into = half_of(in_ref, tile)
        out_ref[pl.ds(tile * MODES, HALF), :] = moved[0] + into[0]
        out_ref[pl.ds(tile * MODES + HALF, HALF), :] = moved[1] + into[1]


def chip_entry(pos, rows, into, turn, cos, sin):
    return pl.pallas_call(
        entry_kernel,
        in_specs=[pl.BlockSpec(memory_space=pltpu.SMEM)] + [pl.BlockSpec()] * 5,
        out_shape=jax.ShapeDtypeStruct(into.shape, F32),
        compiler_params=pltpu.CompilerParams(vmem_limit_bytes=4 * 2**20),
        cost_estimate=pl.CostEstimate(flops=300_000, bytes_accessed=400_000, transcendentals=5000),
        name="chip_entry",
    )(pos, rows, into, turn, cos, sin)


def gathered(copies, count, groups):
    parts = copies.reshape(count, copies.shape[0] // count, copies.shape[1])
    return lax.all_to_all(parts, "seq", 0, 0, axis_index_groups=groups).reshape(copies.shape)


def finish_kernel(
    pos_ref, mine_ref, theirs_ref, other_ref, st_re, st_im, pass_re, pass_im, local_ref, fall_ref, cos_ref, sin_ref,
    cb_ref, rec_ref, start, acc, out
):
    heads = rec_ref.shape[1] // HD
    first_core = pos_ref[3] == 0
    for tile in range(heads):
        lanes = pl.ds(tile * HD, HD)
        mine, theirs = half_of(mine_ref, tile), half_of(theirs_ref, tile)
        at_chip = [
            jnp.concatenate(
                [jnp.where(first_core, mine[i], theirs[i]), jnp.where(first_core, theirs[i], mine[i])], axis=0
            )
            for i in (0, 1)
        ]
        fade = jnp.exp(-other_ref[pl.ds(heads * 2 * MODES + tile, 1), :])
        moved = cmul(at_chip, [fade * ref[2, :, lanes] for ref in (cos_ref, sin_ref)])
        other = [other_ref[pl.ds(tile * 2 * MODES + i * MODES, MODES), :] for i in (0, 1)]
        state = [jnp.where(first_core, at_chip[i], moved[i] + other[i]) for i in (0, 1)]
        start[tile, 0], start[tile, 1] = cmul(state, (cb_ref[0, :, lanes], cb_ref[1, :, lanes]))
    group = 8
    for tile in range(heads):
        lanes = pl.ds(tile * HD, HD)
        for base in range(0, MODES, group):
            older, newer, twice = [], [], []
            for m in range(base, base + group):
                at = pl.ds(m * NBLK, NBLK)
                own = pl.ds(m, 1)
                moved = cmul((pass_re[tile, at, :], pass_im[tile, at, :]), (start[tile, 0, own, :], start[tile, 1, own, :]))
                z = (st_re[tile, at, :] + moved[0], st_im[tile, at, :] + moved[1])
                cos = cos_ref[0, own, lanes]
                older.append(z[0])
                newer.append(cos * z[0] - sin_ref[0, own, lanes] * z[1])
                twice.append(jnp.broadcast_to(2.0 * cos, (NBLK, HD)))
            for r in range(BLK):
                if r > 0:
                    for i in range(group):
                        older[i], newer[i] = newer[i], twice[i] * newer[i] - older[i]
                total = functools.reduce(jnp.add, newer)
                if base == 0:
                    acc[r] = local_ref[r, :, lanes] + total
                else:
                    out[tile, pl.ds(r, NBLK, stride=BLK), :] = (acc[r] + total) * fall_ref[r, :, lanes]
        rec_ref[:, lanes] = out[tile]


def finish(pos, mine, theirs, other, states, passing, local, fall, cos, sin, cb):
    width = fall.shape[2]
    tiles = width // HD
    return pl.pallas_call(
        finish_kernel,
        in_specs=[pl.BlockSpec(memory_space=pltpu.SMEM)] + [pl.BlockSpec()] * 12,
        out_shape=jax.ShapeDtypeStruct((ROWS, width), F32),
        scratch_shapes=[
            pltpu.VMEM((tiles, 2, MODES, HD), F32),
            pltpu.VMEM((BLK, NBLK, HD), F32),
            pltpu.VMEM((tiles, ROWS, HD), F32),
        ],
        compiler_params=pltpu.CompilerParams(vmem_limit_bytes=12 * 2**20),
        cost_estimate=pl.CostEstimate(flops=8_000_000, bytes_accessed=5_000_000, transcendentals=0),
        name="finish",
    )(pos, mine, theirs, other, *states, *passing, local, fall, cos, sin, cb)


def shards(queries, keys, values, decay, gain, theta, mode_coeffs):
    width = queries.shape[1]
    me = lax.axis_index("seq")
    core = me % 2
    chip = me // 2

    own = jnp.stack([keys, values])
    two1 = lax.ppermute(own, "seq", chip_pairs(0, 1, (1,)))
    hop = lax.ppermute(own, "seq", two_back(0))
    up = lax.ppermute(own, "seq", CORE_UP)
    angles = jnp.asarray(TURNS, F32)[:, None, None] * theta[None]
    cos, sin = jnp.cos(angles), jnp.sin(angles)
    own_later, cos = lax.optimization_barrier((own, cos))
    two0 = lax.ppermute(own_later, "seq", chip_pairs(0, 1, (0,)))

    pos = jnp.stack(
        [
            (me >= 2).astype(jnp.int32),
            (me >= 4).astype(jnp.int32),
            ((me >= 3) | (core == 1)).astype(jnp.int32),
            core.astype(jnp.int32),
            (chip % NX).astype(jnp.int32),
            (chip // NX).astype(jnp.int32),
        ]
    )
    flat = jax.ShapeDtypeStruct(queries.shape, F32)
    far1 = lax.ppermute(two1, "seq", chip_pairs(0, 1, (1,)))
    high = lax.ppermute(two1, "seq", CORE_DOWN)
    made = tables(decay, gain[None, :], mode_coeffs, cos, sin, own)
    w, fall, fade, kern, total, cb, *passing = made
    two0 = gate(two0, high, hop, up, total)
    far0 = lax.ppermute(hop, "seq", two_back(1))
    low = lax.ppermute(two0, "seq", CORE_UP)
    run = attention_call(
        near_kernel, "attention_near", 2, [pos, queries, own, total, two0, two1, low, high], [flat] * 3, placed=5
    )
    far1 = gate(far1, far0)
    down = lax.ppermute(far1, "seq", CORE_DOWN)
    attn, wide, ssq = attention_call(
        far_kernel,
        "attention_far",
        2,
        [pos, queries, *run, far0, far1, up, down],
        [
            jax.ShapeDtypeStruct(queries.shape, jnp.bfloat16),
            jax.ShapeDtypeStruct((queries.shape[1] // HD, ROWS, HD), F32),
            jax.ShapeDtypeStruct((1, ROWS), F32),
        ],
        placed=4,
    )

    ssq_all = lax.all_to_all(jnp.broadcast_to(ssq, (NZ, ROWS)), "mp", 0, 0)

    g, *states, dev_sum = block_ends(wide, w, ssq_all, cos, sin, fade, total, cb)
    local = local_part(g, kern)

    other = lax.ppermute(dev_sum, "seq", CORE_SWAP)
    chips = gathered(chip_sum(pos, dev_sum, other, cos, sin), NX, X_GROUPS)
    row, into, turn = row_sum(pos, chips, cos, sin)
    rows = gathered(row, NY, Y_GROUPS)
    mine = chip_entry(pos, rows, into, turn, cos, sin)
    theirs = lax.ppermute(mine, "seq", CORE_SWAP)

    rec = finish(pos, mine, theirs, other, states, passing, local, fall, cos, sin, cb)
    return (attn, rec)


def solution(mesh):
    placed = (
        P("seq", "mp"),
        P("seq", "mp"),
        P("seq", "mp"),
        P("seq", "mp"),
        P("mp"),
        P(None, "mp"),
        P(None, None, "mp"),
    )
    return jax.shard_map(
        shards,
        mesh=mesh,
        in_specs=placed,
        out_specs=(P("seq", "mp"), P("seq", "mp")),
        check_vma=False,
    )
```
